32 devices in a mesh: parts: 1, dp: 2 (over core), expert: 16 (over z, y, x).
Axes of the slice: x: 2, y: 2, z: 4, core: 2. Of those that a mesh axis runs over, the one named last changes fastest.
Arguments:
- tokens: bfloat16 [2048, 2048], P(('parts', 'dp', 'expert')), may hold values from -6 to 6
- routes: int32 [2048, 8], P(('parts', 'dp', 'expert')), may hold values from 0 to 15, all different within a row; in each aligned block of 64 rows (0 to 63, 64 to 127, ...) at most 36 rows name the same one
- combine: bfloat16 [2048, 8], P(('parts', 'dp', 'expert')), may hold values from 0.099609375 to 1
- upstream: bfloat16 [2048, 2048], P(('parts', 'dp', 'expert')), may hold values from -6 to 6
- w_gate: bfloat16 [16, 2048, 768], P('expert', None, 'dp'), may hold values from -0.125 to 0.125
- w_up: bfloat16 [16, 2048, 768], P('expert', None, 'dp'), may hold values from -0.125 to 0.125
- w_down: bfloat16 [16, 768, 2048], P('expert', 'dp'), may hold values from -0.21875 to 0.21875
Outputs:
- grad_tokens: bfloat16 [2048, 2048], P(('parts', 'dp', 'expert'))
- grad_combine: bfloat16 [2048, 8], P(('parts', 'dp', 'expert'))
- grad_gate: bfloat16 [16, 2048, 768], P(('parts', 'expert'), None, 'dp')
- grad_up: bfloat16 [16, 2048, 768], P(('parts', 'expert'), None, 'dp')
- grad_down: bfloat16 [16, 768, 2048], P(('parts', 'expert'), 'dp')
The draws below stay inside these ranges and needn't reach their ends.
Inputs may be any that keep to these rules, and one draw needn't show every extreme that they name: `routes`: each row names 8 different experts. Among the rows of one device no expert is named by more than 36 rows, a bound that some block reaches.
All inputs are finite; a program needn't handle non-finite values.
Results may differ from the reference program's by a relative error of at most 0.008.
Values may be sent and summed in bfloat16 or wider, within the bound.
No kernel may reach another device: no remote copies, remote signals or barrier semaphores. Data moves between devices by JAX's collectives and lax.ppermute only.
A program may use at most 128 MiB of HBM per device.

```python
import math
import jax
import jax.numpy as jnp
import numpy as np
from jax import lax

D = 2048
FF = 768
TOP = 8
TOK_DEV = 64
EXPERTS = 16
CAP = 36
SOURCES = 32
TOKENS = 2048


def levels(stream_key, dims, pieces, low, largest):
    level, own = 1.0, jax.random.fold_in(stream_key, 6)
    for dim, shards_of in pieces:
        heights = jnp.exp(jax.random.uniform(jax.random.fold_in(own, dim), (shards_of,), jnp.float32, low / len(pieces), largest / len(pieces)))
        level = level * jnp.repeat(heights, dims[dim] // shards_of).reshape([-1 if axis == dim else 1 for axis in range(len(dims))])
    return level


def shared_out(stream_key, own, number, rows, number_of, top, reach, lean):
    order = jax.random.permutation(stream_key, number_of)
    crowded, common = portions_of(number_of, rows * top, reach, lean, True), portions_of(number_of, rows * top, reach, lean, False)
    places = jnp.arange(number_of)

    def named(sizes, offset_by):
        used = int((sizes > 0).sum())
        fixed = max(1, used // 4)
        passed = fixed + (places - fixed + offset_by * (used - fixed)) % max(1, number_of - fixed)
        return jnp.zeros((number_of,), jnp.int32).at[order[jnp.where(places < fixed, places, passed)]].set(jnp.asarray(sizes, jnp.int32))

    sizes = jnp.where(number % 4 == 0, named(crowded, number // 4), named(common, number - number // 4 - 1))
    mixed = jax.random.permutation(jax.random.fold_in(own, 3), number_of)
    donor, sink = mixed[0:number_of // 2 * 2:2], mixed[1:number_of // 2 * 2:2]
    room = jnp.minimum(sizes[donor] - 1, reach - sizes[sink]) // 2
    room = jnp.where((donor == order[0]) | (sink == order[0]) | (sizes[sink] == 0), 0, jnp.maximum(room, 0))
    passed = jax.random.randint(jax.random.fold_in(own, 4), (number_of // 2,), 0, 1 << 20) % (room + 1)
    sizes = sizes.at[donor].add(-passed).at[sink].add(passed)
    labels = jnp.searchsorted(jnp.cumsum(sizes), jnp.arange(rows * top), side="right").astype(jnp.int32)
    grid = labels.reshape(top, rows).T
    grid = grid[jax.random.permutation(jax.random.fold_in(own, 1), rows)]
    offset_by = jax.random.randint(jax.random.fold_in(own, 2), (rows, 1), 0, top)
    return jnp.take_along_axis(grid, (jnp.arange(top)[None, :] + offset_by) % top, axis=1)


def portions_of(count, total, reach, skew, full):
    portions = [(1 << 20) // math.isqrt(rank ** skew) + 1 for rank in range(1, count + 1)]
    largest = reach if full else min(reach, max(-(-total // count), total * portions[0] // sum(portions)))
    least = 1 if total - largest >= count - 1 else 0
    given, rest = [largest] + [least] * (count - 1), total - largest - least * (count - 1)
    while rest > 0:
        free = [i for i in range(1, count) if given[i] < largest] or [i for i in range(1, count) if given[i] < reach]
        whole, left = sum([portions[i] for i in free]), rest
        for i in free:
            more = min(reach - given[i], max(1, left * portions[i] // whole), rest)
            given[i] = given[i] + more
            rest = rest - more
    return np.array(given)


def normal_values(stream_key, shape, spread, limit, split=(), held_as=jnp.bfloat16):
    factor_of = levels(stream_key, shape, split, -0.22, 0.18) if split else 1.0
    entries = jax.random.normal(stream_key, shape, jnp.float32) * spread * factor_of
    return jnp.minimum(jnp.maximum(entries, -limit), limit).astype(held_as)


def setup_inputs(seed: int = 0, part: int = 0) -> dict:
    arg_keys = jax.random.split(jax.random.key(seed), 8)
    own_keys = jax.random.split(jax.random.fold_in(arg_keys[7], part), 8)
    tokens = normal_values(own_keys[0], (TOKENS, D), 1.0, 6.0, ((0, 32),))
    routes_keys = jax.random.split(jax.random.fold_in(own_keys[1], 1), TOKENS // TOK_DEV)
    routes_turns = jax.random.permutation(jax.random.fold_in(own_keys[1], 3), TOKENS // TOK_DEV)
    routes = jax.vmap(lambda own, number: shared_out(jax.random.fold_in(own_keys[1], 2), own, number, TOK_DEV, EXPERTS, TOP, CAP, 2))(routes_keys, routes_turns).reshape((TOKENS, TOP))
    combine = jnp.clip(jnp.exp(math.log(1.0) - 2.306499 * jax.random.uniform(own_keys[2], (TOKENS, TOP), jnp.float32) ** levels(own_keys[2], (TOKENS, TOP), ((0, 32),), -0.2, 0.2)), 0.099609375, 1.0).astype(jnp.bfloat16)
    upstream = normal_values(own_keys[3], (TOKENS, D), 1.0, 6.0, ((0, 32),))
    w_gate = normal_values(arg_keys[4], (EXPERTS, D, FF), D ** -0.5, 0.125, ((0, 16), (2, 2)))
    w_up = normal_values(arg_keys[5], (EXPERTS, D, FF), D ** -0.5, 0.125, ((0, 16), (2, 2)))
    w_down = normal_values(arg_keys[6], (EXPERTS, FF, D), FF ** -0.5, 0.21875, ((0, 16), (1, 2)))
    return {"tokens": tokens, "routes": routes, "combine": combine, "upstream": upstream, "w_gate": w_gate, "w_up": w_up, "w_down": w_down}


def expert_math(x_rows, d_rows, c_rows, gate_mat, up_mat, down_mat):
    gate_pre = jnp.dot(x_rows, gate_mat, preferred_element_type=jnp.float32)
    up_pre = jnp.dot(x_rows, up_mat, preferred_element_type=jnp.float32)
    logistic = jax.nn.sigmoid(gate_pre)
    hidden = (gate_pre * logistic * up_pre).astype(jnp.bfloat16)
    grad_hidden = jnp.dot(d_rows, down_mat.T, preferred_element_type=jnp.float32)
    comb_part = jnp.sum(hidden.astype(jnp.float32) * grad_hidden, axis=1)
    scale_col = c_rows.astype(jnp.float32)[:, None]
    scaled = (scale_col * d_rows.astype(jnp.float32)).astype(jnp.bfloat16)
    grad_mixed = scale_col * grad_hidden
    grad_gpre = (grad_mixed * up_pre * logistic * (1.0 + gate_pre * (1.0 - logistic))).astype(jnp.bfloat16)
    grad_upre = (grad_mixed * gate_pre * logistic).astype(jnp.bfloat16)
    grad_downw = jnp.dot(hidden.T, scaled, preferred_element_type=jnp.float32)
    grad_gatew = jnp.dot(x_rows.T, grad_gpre, preferred_element_type=jnp.float32)
    grad_upw = jnp.dot(x_rows.T, grad_upre, preferred_element_type=jnp.float32)
    row_part = jnp.dot(grad_gpre, gate_mat.T, preferred_element_type=jnp.float32)
    row_part = row_part + jnp.dot(grad_upre, up_mat.T, preferred_element_type=jnp.float32)
    return grad_gatew, grad_upw, grad_downw, row_part, comb_part


def reference(tokens, routes, combine, upstream, w_gate, w_up, w_down):
    route_count = TOKENS * TOP
    flat_ids = routes.reshape(-1).astype(jnp.int32)
    blocks = flat_ids.reshape(SOURCES, TOK_DEV * TOP)
    onehot = (blocks[:, :, None] == jnp.arange(EXPERTS, dtype=jnp.int32)[None, None, :]).astype(jnp.int32)
    earlier = jnp.cumsum(onehot, axis=1) - onehot
    position = jnp.sum(earlier * onehot, axis=2).reshape(-1)
    source_ids = jnp.arange(route_count, dtype=jnp.int32) // (TOK_DEV * TOP)
    place = flat_ids * (SOURCES * CAP) + source_ids * CAP + position
    owners = jnp.full((EXPERTS * SOURCES * CAP,), route_count, jnp.int32)
    owners = owners.at[place].set(jnp.arange(route_count, dtype=jnp.int32))
    owners = owners.reshape(EXPERTS, SOURCES * CAP)
    comb_flat = combine.reshape(-1)
    zero_half = jnp.zeros((), jnp.bfloat16)

    def per_expert(packed):
        gate_mat, up_mat, down_mat, owned = packed
        filled = owned < route_count
        safe_ids = jnp.where(filled, owned, 0)
        token_ids = safe_ids // TOP
        x_rows = jnp.where(filled[:, None], tokens[token_ids], zero_half)
        d_rows = jnp.where(filled[:, None], upstream[token_ids], zero_half)
        c_rows = jnp.where(filled, comb_flat[safe_ids], zero_half)
        grad_gatew, grad_upw, grad_downw, row_part, comb_part = expert_math(x_rows, d_rows, c_rows, gate_mat, up_mat, down_mat)
        return (grad_gatew.astype(jnp.bfloat16), grad_upw.astype(jnp.bfloat16), grad_downw.astype(jnp.bfloat16),
                row_part.astype(jnp.bfloat16), comb_part.astype(jnp.bfloat16))

    grad_gate, grad_up, grad_down, route_rows, route_comb = lax.map(per_expert, (w_gate, w_up, w_down, owners))
    picked = route_rows.reshape(-1, D)[place]
    grad_tokens = jnp.sum(picked.reshape(TOKENS, TOP, D).astype(jnp.float32), axis=1).astype(jnp.bfloat16)
    grad_combine = route_comb.reshape(-1)[place].reshape(TOKENS, TOP)
    return grad_tokens, grad_combine, grad_gate, grad_up, grad_down
```

```python
import functools

import jax
import jax.numpy as jnp
import numpy as np
from jax import lax
from jax.experimental import pallas as pl
from jax.experimental.pallas import tpu as pltpu
from jax.sharding import PartitionSpec as P

BF = jnp.bfloat16
F32 = jnp.float32
LANES = 128
HALF = 64
STRIDE = 1024
NOWHERE = -(1 << 20)
ANY = pl.BlockSpec(memory_space=pl.ANY)
VMEM = pl.BlockSpec(memory_space=pltpu.VMEM)
SMEM = pl.BlockSpec(memory_space=pltpu.SMEM)
TN = (((0,), (0,)), ((), ()))
NT = (((1,), (1,)), ((), ()))


def params(megabytes):
    return pltpu.CompilerParams(vmem_limit_bytes=megabytes << 20)


def cost(flops, moved):
    return pl.CostEstimate(flops=int(flops), bytes_accessed=int(moved), transcendentals=0)


class Plan:
    def __init__(self, experts, tok, top, width, hidden):
        self.experts, self.tok, self.top = experts, tok, top
        self.width, self.hidden = width, hidden
        outer = 1
        while outer * outer < experts:
            outer *= 2
        self.outer, self.inner = outer, experts // outer
        mean = tok * top // experts
        self.cap = min(tok, max(2, mean + tok * top // (8 * experts)))
        total = -(-self.outer * self.cap // 16) * 16
        first = self.outer // 2 * self.cap // 16 * 16
        self.chunks = ((0, first), (first, total))
        self.rows = tuple(b - a for a, b in self.chunks)
        self.cands = 2 * self.outer - 1
        self.use = (self.used(self.outer // 2), list(range(self.cands)))
        self.keys = [
            np.array(
                [[d * STRIDE + q for d in range(self.inner) for q in range(a, b)]], np.int32
            )
            for a, b in self.chunks
        ]

    def order(self, z):
        return sorted(range(self.outer), key=lambda s: abs(s - z))

    def cand(self, z, source):
        if source == z:
            return 0
        return z - source if source < z else self.outer - 1 + source - z

    def used(self, slots):
        return sorted({self.cand(z, s) for z in range(self.outer) for s in self.order(z)[:slots]})

    def partner(self, p, d):
        return p ^ d if self.inner & (self.inner - 1) == 0 else (d - p) % self.inner

    def table(self):
        rows = []
        for e in range(self.experts):
            z, p = divmod(e, self.inner)
            offs = [NOWHERE] * self.cands
            for slot, source in enumerate(self.order(z)):
                offs[self.cand(z, source)] = slot * self.cap
            rows.append(offs + [z * self.inner + self.partner(p, d) for d in range(self.inner)])
        return np.array(rows, np.int32)

    def line(self, step):
        return [
            (z * self.inner + p, (z + step) * self.inner + p)
            for z in range(self.outer)
            for p in range(self.inner)
            if 0 <= z + step < self.outer
        ]

    def across(self, d):
        return [
            (z * self.inner + p, z * self.inner + self.partner(p, d))
            for z in range(self.outer)
            for p in range(self.inner)
        ]

    def shift(self, r):
        return [
            (z * self.inner + p, (z + r) % self.outer * self.inner + p)
            for z in range(self.outer)
            for p in range(self.inner)
        ]


def pack_kernel(plan, tok_ref, up_ref, routes_ref, comb_ref, out_ref):
    tok, width = plan.tok, plan.width
    out_ref[:, :width] = tok_ref[...]
    out_ref[:, width : 2 * width] = up_ref[...]
    lane = lax.broadcasted_iota(jnp.int32, (tok, LANES), 1)
    weight = jnp.zeros((tok, LANES), F32)
    named = jnp.zeros((tok, LANES), F32)
    comb = comb_ref[...].astype(F32)
    for k in range(plan.top):
        e = routes_ref[:, k : k + 1]
        weight = jnp.where(lane == e, comb[:, k : k + 1], weight)
        named = jnp.where(lane == e + HALF, 1.0, named)
    row = lax.broadcasted_iota(jnp.int32, (tok, tok), 0)
    col = lax.broadcasted_iota(jnp.int32, (tok, tok), 1)
    upto = jnp.where(col <= row, 1.0, 0.0).astype(BF)
    count = jnp.dot(upto, named.astype(BF), preferred_element_type=F32)
    out_ref[:, 2 * width :] = (weight + count * named).astype(BF)


def picks(plan, meta, off, experts, key, scaled):
    tok = meta.shape[0]
    lane = lax.broadcasted_iota(jnp.int32, (tok, LANES), 1)
    one = jnp.zeros((tok, key.shape[1]), F32)
    two = jnp.zeros((tok, key.shape[1]), F32)
    for d, e in enumerate(experts):
        place = jnp.sum(jnp.where(lane == e + HALF, meta, 0.0), axis=1, keepdims=True)
        place = place.astype(jnp.int32)
        spot = jnp.where(place > 0, place - 1 + off + d * STRIDE, -1)
        hit = spot == key
        one = jnp.where(hit, 1.0, one)
        if scaled:
            weight = jnp.sum(jnp.where(lane == e, meta, 0.0), axis=1, keepdims=True)
            two = jnp.where(hit, weight, two)
    return one, two


def compact_kernel(plan, chunk, *refs):
    use, rows = plan.use[chunk], plan.rows[chunk]
    n, width, tok, inner = len(use), plan.width, plan.tok, plan.inner
    info, key_ref = refs[:2]
    blocks, outs = refs[2 : 2 + n], refs[2 + n : 2 + n + inner]
    held, one_s, two_s, sems = refs[2 + n + inner :]
    copies = [
        pltpu.make_async_copy(b, held.at[pl.ds(i * tok, tok)], sems.at[i])
        for i, b in enumerate(blocks)
    ]
    for c in copies:
        c.start()
    experts = [info[plan.cands + d] for d in range(inner)]
    for i, c in enumerate(copies):
        c.wait()
        meta = held[i * tok : (i + 1) * tok, 2 * width :].astype(F32)
        one, two = picks(plan, meta, info[use[i]], experts, key_ref[...], True)
        one_s[i * tok : (i + 1) * tok, :] = one.astype(BF)
        two_s[i * tok : (i + 1) * tok, :] = two.astype(BF)
    tile = 512
    for part, source in ((0, one_s), (1, two_s)):

        @pl.loop(0, width // tile)
        def _(j):
            at = pl.multiple_of(j * tile, tile)
            got = lax.dot_general(
                source[...],
                held[:, pl.ds(pl.multiple_of(part * width + at, tile), tile)],
                TN,
                preferred_element_type=F32,
            ).astype(BF)
            for d in range(inner):
                outs[d][part * rows : (part + 1) * rows, pl.ds(at, tile)] = got[
                    d * rows : (d + 1) * rows
                ]


def expert_kernel(plan, chunk, *refs):
    inner, rows, width, hidden = plan.inner, plan.rows[chunk], plan.width, plan.hidden
    part, count = hidden // 2, plan.inner * plan.rows[chunk]
    info = refs[0]
    got, weights = refs[1 : 1 + inner], refs[1 + inner : 7 + inner]
    hid_o, gate_o, up_o = refs[7 + inner : 10 + inner]
    backs = refs[10 + inner : 10 + 2 * inner]
    x_s, d_s, wg_s, wu_s, wd_s, comb_s, sems = refs[10 + 2 * inner :]
    x_copies = [
        pltpu.make_async_copy(g.at[pl.ds(0, rows)], x_s.at[pl.ds(d * rows, rows)], sems.at[d])
        for d, g in enumerate(got)
    ]
    d_copies = [
        pltpu.make_async_copy(
            g.at[pl.ds(rows, rows)], d_s.at[pl.ds(d * rows, rows)], sems.at[inner + d]
        )
        for d, g in enumerate(got)
    ]
    w_copies = []
    for i in range(6):
        half, where = pl.ds(i % 2 * part, part), (wg_s, wu_s, wd_s)[i // 2]
        to = where.at[half] if i >= 4 else where.at[:, half]
        w_copies.append(pltpu.make_async_copy(weights[i].at[0], to, sems.at[2 * inner + i]))
    for c in x_copies + w_copies[:4] + d_copies + w_copies[4:]:
        c.start()
    for c in x_copies + w_copies[:4] + d_copies + w_copies[4:]:
        c.wait()
    tile = 256
    comb_s[...] = jnp.zeros_like(comb_s)

    @pl.loop(0, hidden // tile)
    def _(n):
        at = pl.ds(pl.multiple_of(n * tile, tile), tile)
        gate = jnp.dot(x_s[...], wg_s[:, at], preferred_element_type=F32)
        up = jnp.dot(x_s[...], wu_s[:, at], preferred_element_type=F32)
        mixed = lax.dot_general(d_s[...], wd_s[at, :], NT, preferred_element_type=F32)
        logistic = jax.nn.sigmoid(gate)
        silu = gate * logistic
        hid = (silu * up).astype(BF)
        hid_o[:, at] = hid
        comb_s[...] += jnp.sum(hid.astype(F32) * mixed, axis=1, keepdims=True)
        gate_o[:, at] = (mixed * up * logistic * (1.0 + gate * (1.0 - logistic))).astype(BF)
        up_o[:, at] = (mixed * silu).astype(BF)

    wide = 256

    @pl.loop(0, width // wide)
    def _(j):
        at = pl.ds(pl.multiple_of(j * wide, wide), wide)
        back = lax.dot_general(gate_o[...], wg_s[at, :], NT, preferred_element_type=F32)
        back += lax.dot_general(up_o[...], wu_s[at, :], NT, preferred_element_type=F32)
        back = back.astype(BF)
        for d in range(inner):
            backs[d][:, at] = back[d * rows : (d + 1) * rows]

    lane = lax.broadcasted_iota(jnp.int32, (count, LANES), 1)
    comb = jnp.where(lane == info[plan.cands], comb_s[...], 0.0).astype(BF)
    for d in range(inner):
        backs[d][:, width:] = comb[d * rows : (d + 1) * rows]


def weight_kernel(plan, own, *refs):
    inner, width, hidden = plan.inner, plan.width, plan.hidden
    part, counts = hidden // 2, [inner * r for r in plan.rows]
    got = refs[: 2 * inner]
    mids = refs[2 * inner : 2 * inner + 6]
    at = 2 * inner + 6
    theirs = refs[at : at + 3] if own else None
    at += 3 if own else 0
    g_o, u_o, d_o = refs[at : at + 3]
    x_s, d_s, h_s, gu_s, sems = refs[at + 3 :]
    x_copies, d_copies = [], []
    start = 0
    for c in range(2):
        rows = plan.rows[c]
        for d in range(inner):
            g, to = got[c * inner + d], pl.ds(start, rows)
            i = c * inner + d
            x_copies.append(pltpu.make_async_copy(g.at[pl.ds(0, rows)], x_s.at[to], sems.at[i]))
            d_copies.append(
                pltpu.make_async_copy(g.at[pl.ds(rows, rows)], d_s.at[to], sems.at[2 * inner + i])
            )
            start += rows
    m_copies = []
    half = pl.ds(0 if own else part, part)
    for c in range(2):
        to = pl.ds(0 if c == 0 else counts[0], counts[c])
        hid, gate, up = mids[3 * c : 3 * c + 3]
        spots = (h_s.at[to], gu_s.at[to, pl.ds(0, part)], gu_s.at[to, pl.ds(part, part)])
        for i, (m, s) in enumerate(zip((hid, gate, up), spots)):
            m_copies.append(
                pltpu.make_async_copy(m.at[:, half], s, sems.at[4 * inner + 3 * c + i])
            )
    everything = x_copies + m_copies + d_copies
    for c in everything:
        c.start()
    for c in everything:
        c.wait()
    tile = 256

    @pl.loop(0, width // tile)
    def _(j):
        to = pl.ds(pl.multiple_of(j * tile, tile), tile)
        both = lax.dot_general(x_s[:, to], gu_s[...], TN, preferred_element_type=F32)
        first, second = both[:, :part], both[:, part:]
        if own:
            first += theirs[0][0, to, :].astype(F32)
            second += theirs[1][0, to, :].astype(F32)
        g_o[0, to, :] = first.astype(BF)
        u_o[0, to, :] = second.astype(BF)

    @pl.loop(0, width // tile)
    def _(j):
        to = pl.ds(pl.multiple_of(j * tile, tile), tile)
        down = lax.dot_general(h_s[...], d_s[:, to], TN, preferred_element_type=F32)
        if own:
            down += theirs[2][0, :, to].astype(F32)
        d_o[0, :, to] = down.astype(BF)


def spread_kernel(plan, *refs):
    inner, outer, tok, width = plan.inner, plan.outer, plan.tok, plan.width
    info, key_ref = refs[:2]
    blocks = refs[2 : 2 + plan.cands]
    backs = refs[2 + plan.cands : 2 + plan.cands + 2 * inner]
    outs = refs[2 + plan.cands + 2 * inner :][:outer]
    held, metas, pick_s, sems, meta_sems = refs[2 + plan.cands + 2 * inner + outer :]
    copies, start = [], 0
    for i, b in enumerate(blocks):
        copies.append(
            pltpu.make_async_copy(b.at[:, pl.ds(2 * width, LANES)], metas.at[i], meta_sems.at[i])
        )
    later = []
    for i, b in enumerate(backs):
        rows = plan.rows[i // inner]
        later.append(pltpu.make_async_copy(b, held.at[pl.ds(start, rows)], sems.at[i]))
        start += rows
    for c in copies + later:
        c.start()
    for c in copies:
        c.wait()
    experts = [info[plan.cands + d] for d in range(inner)]
    for r in range(outer):
        total = None
        for i in [0] if r == 0 else [outer - 1 + r, outer - r]:
            one, _ = picks(
                plan, metas[i].astype(F32), info[i], experts, key_ref[...], False
            )
            total = one if total is None else total + one
        pick_s[r * tok : (r + 1) * tok, :] = total.astype(BF)
    for c in later:
        c.wait()
    tile = 256

    def piece(at, size):
        sums = jnp.dot(pick_s[...], held[:, pl.ds(at, size)], preferred_element_type=F32)
        sums = sums.astype(BF)
        for r in range(outer):
            outs[r][:, pl.ds(at, size)] = sums[r * tok : (r + 1) * tok]

    @pl.loop(0, width // tile)
    def _(j):
        piece(pl.multiple_of(j * tile, tile), tile)

    piece(width, LANES)


def home_kernel(plan, *refs):
    parts, (routes_ref, comb_ref, tok_o, comb_o) = refs[: plan.outer], refs[plan.outer :]
    width, tok = plan.width, plan.tok
    total = parts[0][...].astype(F32)
    for p in parts[1:]:
        total += p[...].astype(F32)
    tok_o[...] = total[:, :width].astype(BF)
    found = total[:, width:]
    lane = lax.broadcasted_iota(jnp.int32, (tok, LANES), 1)
    slot = lax.broadcasted_iota(jnp.int32, (tok, plan.top), 1)
    out = jnp.zeros((tok, plan.top), F32)
    for k in range(plan.top):
        mine = jnp.where(lane == routes_ref[:, k : k + 1], found, 0.0)
        out = jnp.where(slot == k, jnp.sum(mine, axis=1, keepdims=True), out)
    comb_o[...] = (out / comb_ref[...].astype(F32)).astype(BF)


def on_device(plan, tokens, routes, combine, upstream, w_gate, w_up, w_down):
    tok, width, hidden = plan.tok, plan.width, plan.hidden
    inner, outer, part = plan.inner, plan.outer, plan.hidden // 2
    full = 2 * width + LANES
    shape = jax.ShapeDtypeStruct
    info = jnp.asarray(plan.table())[lax.axis_index("expert")]
    keys = [jnp.asarray(k) for k in plan.keys]
    swap = [(0, 1), (1, 0)]

    block = pl.pallas_call(
        functools.partial(pack_kernel, plan),
        out_shape=shape((tok, full), BF),
        in_specs=[VMEM] * 4,
        out_specs=VMEM,
        compiler_params=params(16),
        cost_estimate=cost(1e6, 4 * tok * full),
        name="pack",
    )(tokens, upstream, routes, combine)

    below, above = [block], [block]
    for _ in range(outer - 1):
        below.append(lax.ppermute(below[-1], "expert", plan.line(1)))
        above.append(lax.ppermute(above[-1], "expert", plan.line(-1)))
    blocks = [block] + below[1:] + above[1:]

    weights = []
    for w in (w_gate, w_up, w_down):
        weights += [w, lax.ppermute(w, "dp", swap)]

    got, mids, backs = [], [], []
    for c in range(2):
        rows, use = plan.rows[c], plan.use[c]
        count, n = inner * rows, len(use)
        sent = pl.pallas_call(
            functools.partial(compact_kernel, plan, c),
            out_shape=[shape((2 * rows, width), BF)] * inner,
            in_specs=[SMEM, VMEM] + [ANY] * n,
            out_specs=[VMEM] * inner,
            scratch_shapes=[
                pltpu.VMEM((n * tok, full), BF),
                pltpu.VMEM((n * tok, count), BF),
                pltpu.VMEM((n * tok, count), BF),
                pltpu.SemaphoreType.DMA((n,)),
            ],
            compiler_params=params(40),
            cost_estimate=cost(4 * n * tok * count * width, 2 * n * tok * full),
            name="compact",
        )(info, keys[c], *[blocks[i] for i in use])
        arrived = [sent[0]] + [
            lax.ppermute(sent[d], "expert", plan.across(d)) for d in range(1, inner)
        ]
        outs = pl.pallas_call(
            functools.partial(expert_kernel, plan, c),
            out_shape=[shape((count, hidden), BF)] * 3
            + [shape((rows, width + LANES), BF)] * inner,
            in_specs=[SMEM] + [ANY] * (inner + 6),
            out_specs=[VMEM] * (3 + inner),
            scratch_shapes=[
                pltpu.VMEM((count, width), BF),
                pltpu.VMEM((count, width), BF),
                pltpu.VMEM((width, hidden), BF),
                pltpu.VMEM((width, hidden), BF),
                pltpu.VMEM((hidden, width), BF),
                pltpu.VMEM((count, 1), F32),
                pltpu.SemaphoreType.DMA((2 * inner + 6,)),
            ],
            compiler_params=params(44),
            cost_estimate=cost(10 * count * hidden * width, 6 * hidden * width),
            name="expert",
        )(info, *arrived, *weights)
        got += arrived
        mids += outs[:3]
        backs += [outs[3]] + [
            lax.ppermute(outs[3 + d], "expert", plan.across(d)) for d in range(1, inner)
        ]

    count = inner * sum(plan.rows)

    def weight_grads(own, extra):
        return pl.pallas_call(
            functools.partial(weight_kernel, plan, own),
            out_shape=[
                shape((1, width, part), BF),
                shape((1, width, part), BF),
                shape((1, part, width), BF),
            ],
            in_specs=[ANY] * (2 * inner + 6) + [VMEM] * len(extra),
            out_specs=[VMEM] * 3,
            scratch_shapes=[
                pltpu.VMEM((count, width), BF),
                pltpu.VMEM((count, width), BF),
                pltpu.VMEM((count, part), BF),
                pltpu.VMEM((count, 2 * part), BF),
                pltpu.SemaphoreType.DMA((4 * inner + 6,)),
            ],
            compiler_params=params(44),
            cost_estimate=cost(6 * count * part * width, 4 * count * (width + hidden)),
            name="weight_grads",
        )(*got, *mids, *extra)

    theirs = [lax.ppermute(w, "dp", swap) for w in weight_grads(False, [])]
    grads = weight_grads(True, theirs)

    sums = pl.pallas_call(
        functools.partial(spread_kernel, plan),
        out_shape=[shape((tok, width + LANES), BF)] * outer,
        in_specs=[SMEM, VMEM] + [ANY] * (plan.cands + 2 * inner),
        out_specs=[VMEM] * outer,
        scratch_shapes=[
            pltpu.VMEM((count, width + LANES), BF),
            pltpu.VMEM((plan.cands, tok, LANES), BF),
            pltpu.VMEM((outer * tok, count), BF),
            pltpu.SemaphoreType.DMA((2 * inner,)),
            pltpu.SemaphoreType.DMA((plan.cands,)),
        ],
        compiler_params=params(32),
        cost_estimate=cost(2 * outer * tok * count * width, 2 * count * width),
        name="spread",
    )(info, jnp.concatenate(keys, axis=1), *blocks, *backs)
    home = [sums[0]] + [lax.ppermute(sums[r], "expert", plan.shift(r)) for r in range(1, outer)]
    grad_tokens, grad_combine = pl.pallas_call(
        functools.partial(home_kernel, plan),
        out_shape=[shape((tok, width), BF), shape((tok, plan.top), BF)],
        in_specs=[VMEM] * (outer + 2),
        out_specs=[VMEM] * 2,
        compiler_params=params(16),
        cost_estimate=cost(1e6, 2 * tok * width * (outer + 1)),
        name="home",
    )(*home, routes, combine)
    return (grad_tokens, grad_combine, *grads)


def solution(mesh):
    rows = P(("parts", "dp", "expert"), None)
    in_specs = (rows,) * 4 + (P("expert", None, "dp"),) * 2 + (P("expert", "dp", None),)
    out_specs = (rows,) * 2 + (P(("parts", "expert"), None, "dp"),) * 2
    out_specs += (P(("parts", "expert"), "dp", None),)
    shape = dict(mesh.shape)

    def whole(tokens, routes, combine, upstream, w_gate, w_up, w_down):
        devices = shape["parts"] * shape["dp"] * shape["expert"]
        plan = Plan(
            shape["expert"],
            tokens.shape[0] // devices,
            routes.shape[1],
            tokens.shape[1],
            w_gate.shape[2],
        )
        body = functools.partial(on_device, plan)
        return jax.shard_map(
            body, mesh=mesh, in_specs=in_specs, out_specs=out_specs, check_vma=False
        )(tokens, routes, combine, upstream, w_gate, w_up, w_down)

    return whole
```

```python
import functools

import jax
import jax.numpy as jnp
import numpy as np
from jax import lax
from jax.experimental import pallas as pl
from jax.experimental.pallas import tpu as pltpu
from jax.sharding import PartitionSpec as P

BF = jnp.bfloat16
F32 = jnp.float32
LANES = 128
HALF = 64
STRIDE = 1024
NOWHERE = -(1 << 20)
ANY = pl.BlockSpec(memory_space=pltpu.HBM)
VMEM = pl.BlockSpec(memory_space=pltpu.VMEM)
SMEM = pl.BlockSpec(memory_space=pltpu.SMEM)
TN = (((0,), (0,)), ((), ()))
NT = (((1,), (1,)), ((), ()))


def params(megabytes=60):
    return pltpu.CompilerParams(vmem_limit_bytes=megabytes << 20)


def cost(flops, moved):
    return pl.CostEstimate(flops=int(flops), bytes_accessed=int(moved), transcendentals=0)


class Plan:
    def __init__(self, experts, tok, top, width, hidden):
        self.experts, self.tok, self.top = experts, tok, top
        self.width, self.hidden = width, hidden
        outer = 1
        while outer * outer < experts:
            outer *= 2
        self.outer, self.inner = outer, experts // outer
        mean = tok * top // experts
        self.cap = min(tok, max(2, mean + tok * top // (8 * experts)))
        total = -(-self.outer * self.cap // 16) * 16
        first = self.outer // 2 * self.cap // 16 * 16
        self.chunks = ((0, first), (first, total))
        self.rows = tuple(b - a for a, b in self.chunks)
        self.cands = 2 * self.outer - 1
        self.use = (self.used(self.outer // 2), list(range(self.cands)))
        self.keys = [
            np.array(
                [[d * STRIDE + q for d in range(self.inner) for q in range(a, b)]], np.int32
            )
            for a, b in self.chunks
        ]

    def order(self, z):
        rest = [s for s in range(self.outer) if s not in (z, z ^ 1)]
        return [z ^ 1, z] + sorted(rest, key=lambda s: abs(s - z))

    def cand(self, z, source):
        if source == z:
            return 0
        return z - source if source < z else self.outer - 1 + source - z

    def used(self, slots):
        return sorted({self.cand(z, s) for z in range(self.outer) for s in self.order(z)[:slots]})

    def partner(self, p, d):
        return p ^ d if self.inner & (self.inner - 1) == 0 else (d - p) % self.inner

    def table(self):
        rows = []
        for e in range(self.experts):
            z, p = divmod(e, self.inner)
            offs = [NOWHERE] * self.cands
            for slot, source in enumerate(self.order(z)):
                offs[self.cand(z, source)] = slot * self.cap
            experts = [z * self.inner + self.partner(p, d) for d in range(self.inner)]
            homes = [self.cand(z, z ^ r) for r in range(self.outer)]
            rows.append(offs + experts + homes)
        return np.array(rows, np.int32)

    def line(self, step):
        return [
            (z * self.inner + p, (z + step) * self.inner + p)
            for z in range(self.outer)
            for p in range(self.inner)
            if 0 <= z + step < self.outer
        ]

    def across(self, d):
        return [
            (z * self.inner + p, z * self.inner + self.partner(p, d))
            for z in range(self.outer)
            for p in range(self.inner)
        ]

    def flip(self, r):
        return [
            (z * self.inner + p, (z ^ r) * self.inner + p)
            for z in range(self.outer)
            for p in range(self.inner)
        ]


def pack_kernel(plan, tok_ref, up_ref, routes_ref, comb_ref, out_ref):
    tok, width = plan.tok, plan.width
    out_ref[:, :width] = tok_ref[...]
    out_ref[:, width : 2 * width] = up_ref[...]
    kind = lax.broadcasted_iota(jnp.int32, (LANES, tok), 0)
    weight = jnp.zeros((LANES, tok), F32)
    named = jnp.zeros((LANES, tok), F32)
    comb = comb_ref[...].astype(F32)
    for k in range(plan.top):
        e = routes_ref[k : k + 1, :]
        weight = jnp.where(kind == e, comb[k : k + 1, :], weight)
        named = jnp.where(kind == e + HALF, 1.0, named)
    row = lax.broadcasted_iota(jnp.int32, (tok, tok), 0)
    col = lax.broadcasted_iota(jnp.int32, (tok, tok), 1)
    upto = jnp.where(row <= col, 1.0, 0.0).astype(BF)
    count = jnp.dot(named.astype(BF), upto, preferred_element_type=F32)
    table = (weight + count * named).astype(BF)
    same = jnp.where(row == col, 1.0, 0.0).astype(BF)
    turned = lax.dot_general(same, table, NT, preferred_element_type=F32)
    out_ref[:, 2 * width :] = turned.astype(BF)


def picks(plan, meta, off, experts, key, scaled):
    tok = meta.shape[0]
    lane = lax.broadcasted_iota(jnp.int32, (tok, LANES), 1)
    one = jnp.zeros((tok, key.shape[1]), F32)
    two = jnp.zeros((tok, key.shape[1]), F32)
    for d, e in enumerate(experts):
        place = jnp.sum(jnp.where(lane == e + HALF, meta, 0.0), axis=1, keepdims=True)
        place = place.astype(jnp.int32)
        spot = jnp.where(place > 0, place - 1 + off + d * STRIDE, -1)
        hit = spot == key
        one = jnp.where(hit, 1.0, one)
        if scaled:
            weight = jnp.sum(jnp.where(lane == e, meta, 0.0), axis=1, keepdims=True)
            two = jnp.where(hit, weight, two)
    return one, two


def compact_kernel(plan, chunk, *refs):
    use, rows = plan.use[chunk], plan.rows[chunk]
    n, width, tok, inner = len(use), plan.width, plan.tok, plan.inner
    info, key_ref = refs[:2]
    blocks, outs = refs[2 : 2 + n], refs[2 + n : 2 + n + inner]
    held, one_s, two_s, sems = refs[2 + n + inner :]
    copies = [
        pltpu.make_async_copy(b, held.at[pl.ds(i * tok, tok)], sems.at[i])
        for i, b in enumerate(blocks)
    ]
    for c in copies:
        c.start()
    experts = [info[plan.cands + d] for d in range(inner)]
    for i, c in enumerate(copies):
        c.wait()
        meta = held[i * tok : (i + 1) * tok, 2 * width :].astype(F32)
        one, two = picks(plan, meta, info[use[i]], experts, key_ref[...], True)
        one_s[i * tok : (i + 1) * tok, :] = one.astype(BF)
        two_s[i * tok : (i + 1) * tok, :] = two.astype(BF)
    for part, source in ((0, one_s), (1, two_s)):
        have = held[:, part * width : (part + 1) * width]
        found = lax.dot_general(source[...], have, TN, preferred_element_type=F32).astype(BF)
        for d in range(inner):
            outs[d][part * rows : (part + 1) * rows, :] = found[d * rows : (d + 1) * rows]


def expert_kernel(plan, chunk, *refs):
    inner, rows, width, hidden = plan.inner, plan.rows[chunk], plan.width, plan.hidden
    part, count = hidden // 2, plan.inner * plan.rows[chunk]
    info = refs[0]
    got, weights = refs[1 : 1 + inner], refs[1 + inner : 7 + inner]
    hid_o, gate_o, up_o = refs[7 + inner : 10 + inner]
    backs = refs[10 + inner : 10 + 2 * inner]
    x_s, d_s, wg_s, wu_s, wd_s, comb_s, sems = refs[10 + 2 * inner :]
    x_copies = [
        pltpu.make_async_copy(g.at[pl.ds(0, rows)], x_s.at[pl.ds(d * rows, rows)], sems.at[d])
        for d, g in enumerate(got)
    ]
    d_copies = [
        pltpu.make_async_copy(
            g.at[pl.ds(rows, rows)], d_s.at[pl.ds(d * rows, rows)], sems.at[inner + d]
        )
        for d, g in enumerate(got)
    ]
    tile, tiles = 256, []
    for n in range(hidden // tile):
        for kind, where in ((0, wg_s), (1, wu_s), (2, wd_s)):
            at, here = n * tile, []
            while at < (n + 1) * tile:
                half, start = divmod(at, part)
                size = min((n + 1) * tile, (half + 1) * part) - at
                source, to = pl.ds(start, size), pl.ds(at, size)
                w = weights[2 * kind + half].at[0]
                here.append((w.at[source], where.at[to]) if kind == 2 else (w.at[:, source], where.at[:, to]))
                at += size
            tiles.append(here)
    w_copies, used = [], 2 * inner
    for here in tiles:
        w_copies.append([])
        for source, to in here:
            w_copies[-1].append(pltpu.make_async_copy(source, to, sems.at[used]))
            used += 1
    for c in x_copies + w_copies[0] + w_copies[1] + d_copies:
        c.start()
    for here in w_copies[2:]:
        for c in here:
            c.start()
    for n in range(hidden // tile):
        at = slice(n * tile, (n + 1) * tile)
        gate_w, up_w, down_w = w_copies[3 * n : 3 * n + 3]
        for c in (x_copies if n == 0 else []) + gate_w:
            c.wait()
        gate = jnp.dot(x_s[...], wg_s[:, at], preferred_element_type=F32)
        for c in up_w:
            c.wait()
        up = jnp.dot(x_s[...], wu_s[:, at], preferred_element_type=F32)
        for c in (d_copies if n == 0 else []) + down_w:
            c.wait()
        mixed = lax.dot_general(d_s[...], wd_s[at, :], NT, preferred_element_type=F32)
        logistic = jax.nn.sigmoid(gate)
        silu = gate * logistic
        hid = (silu * up).astype(BF)
        hid_o[:, at] = hid
        comb = jnp.sum(hid.astype(F32) * mixed, axis=1, keepdims=True)
        comb_s[...] = comb if n == 0 else comb_s[...] + comb
        gate_o[:, at] = (mixed * up * logistic * (1.0 + gate * (1.0 - logistic))).astype(BF)
        up_o[:, at] = (mixed * silu).astype(BF)

    wide = 256

    @pl.loop(0, width // wide)
    def _(j):
        at = pl.ds(pl.multiple_of(j * wide, wide), wide)
        back = lax.dot_general(gate_o[...], wg_s[at, :], NT, preferred_element_type=F32)
        back += lax.dot_general(up_o[...], wu_s[at, :], NT, preferred_element_type=F32)
        back = back.astype(BF)
        for d in range(inner):
            backs[d][:, at] = back[d * rows : (d + 1) * rows]

    lane = lax.broadcasted_iota(jnp.int32, (count, LANES), 1)
    comb = jnp.where(lane == info[plan.cands], comb_s[...], 0.0).astype(BF)
    for d in range(inner):
        backs[d][:, width:] = comb[d * rows : (d + 1) * rows]


def weight_kernel(plan, own, *refs):
    inner, width, hidden = plan.inner, plan.width, plan.hidden
    part, counts = hidden // 2, [inner * r for r in plan.rows]
    got = refs[: 2 * inner]
    mids = refs[2 * inner : 2 * inner + 6]
    at = 2 * inner + 6
    theirs = refs[at : at + 3] if own else None
    at += 3 if own else 0
    g_o, u_o, d_o = refs[at : at + 3]
    x_s, d_s, h_s, gu_s, sems = refs[at + 3 :]
    x_copies, d_copies = [], []
    start = 0
    for c in range(2):
        rows = plan.rows[c]
        for d in range(inner):
            g, to = got[c * inner + d], pl.ds(start, rows)
            i = c * inner + d
            x_copies.append(pltpu.make_async_copy(g.at[pl.ds(0, rows)], x_s.at[to], sems.at[i]))
            d_copies.append(
                pltpu.make_async_copy(g.at[pl.ds(rows, rows)], d_s.at[to], sems.at[2 * inner + i])
            )
            start += rows
    m_copies = []
    half = pl.ds(0 if own else part, part)
    for c in range(2):
        to = pl.ds(0 if c == 0 else counts[0], counts[c])
        hid, gate, up = mids[3 * c : 3 * c + 3]
        spots = (h_s.at[to], gu_s.at[to, pl.ds(0, part)], gu_s.at[to, pl.ds(part, part)])
        for i, (m, s) in enumerate(zip((hid, gate, up), spots)):
            m_copies.append(
                pltpu.make_async_copy(m.at[:, half], s, sems.at[4 * inner + 3 * c + i])
            )
    everything = x_copies + m_copies + d_copies
    for c in everything:
        c.start()
    for c in everything:
        c.wait()
    tile = 256

    @pl.loop(0, width // tile)
    def _(j):
        to = pl.ds(pl.multiple_of(j * tile, tile), tile)
        both = lax.dot_general(x_s[:, to], gu_s[...], TN, preferred_element_type=F32)
        first, second = both[:, :part], both[:, part:]
        if own:
            first += theirs[0][0, to, :].astype(F32)
            second += theirs[1][0, to, :].astype(F32)
        g_o[0, to, :] = first.astype(BF)
        u_o[0, to, :] = second.astype(BF)

    down = lax.dot_general(h_s[...], d_s[...], TN, preferred_element_type=F32)
    if own:
        down += theirs[2][0].astype(F32)
    d_o[0] = down.astype(BF)


def spread_kernel(plan, homes, chunks, *refs):
    inner, tok, width = plan.inner, plan.tok, plan.width
    info, key_ref = refs[:2]
    blocks = refs[2 : 2 + plan.cands]
    at = 2 + plan.cands
    backs = refs[at : at + chunks * inner]
    outs = refs[-5 - len(homes) : -5]
    held, metas, pick_s, sems, meta_sems = refs[-5:]
    copies, later, start = [], [], 0
    for i, b in enumerate(blocks):
        copies.append(
            pltpu.make_async_copy(b.at[:, pl.ds(2 * width, LANES)], metas.at[i], meta_sems.at[i])
        )
    for i, b in enumerate(backs):
        rows = plan.rows[i // inner]
        later.append(pltpu.make_async_copy(b, held.at[pl.ds(start, rows)], sems.at[i]))
        start += rows
    for c in copies + later:
        c.start()
    for c in copies:
        c.wait()
    experts = [info[plan.cands + d] for d in range(inner)]
    for i, r in enumerate(homes):
        which = info[plan.cands + inner + r]
        meta = metas[which].astype(F32)
        one, _ = picks(plan, meta, info[which], experts, key_ref[...], False)
        pick_s[i * tok : (i + 1) * tok, :] = one.astype(BF)
    for c in later:
        c.wait()
    tile = 256

    def piece(at, size):
        sums = jnp.dot(pick_s[...], held[:, pl.ds(at, size)], preferred_element_type=F32)
        sums = sums.astype(BF)
        for i in range(len(homes)):
            outs[i][:, pl.ds(at, size)] = sums[i * tok : (i + 1) * tok]

    @pl.loop(0, width // tile)
    def _(j):
        piece(pl.multiple_of(j * tile, tile), tile)

    piece(width, LANES)


def add_kernel(a_ref, b_ref, o_ref):
    o_ref[...] = (a_ref[...].astype(F32) + b_ref[...].astype(F32)).astype(BF)


def home_kernel(plan, count, *refs):
    parts = refs[:count]
    routes_ref, comb_ref, _, tok_o, comb_o = refs[count:]
    width, tok = plan.width, plan.tok
    total = parts[0][...].astype(F32)
    for p in parts[1:]:
        total += p[...].astype(F32)
    tok_o[...] = total[:, :width].astype(BF)
    row = lax.broadcasted_iota(jnp.int32, (LANES, LANES), 0)
    col = lax.broadcasted_iota(jnp.int32, (LANES, LANES), 1)
    same = jnp.where(row == col, 1.0, 0.0).astype(BF)
    found = total[:, width:].astype(BF)
    found = lax.dot_general(same, found, NT, preferred_element_type=F32)
    kind = lax.broadcasted_iota(jnp.int32, (LANES, tok), 0)
    out = []
    for k in range(plan.top):
        mine = jnp.where(kind == routes_ref[k : k + 1, :], found, 0.0)
        out.append(jnp.sum(mine, axis=0, keepdims=True))
    out = jnp.concatenate(out, axis=0)
    comb_o[...] = (out / comb_ref[...].astype(F32)).astype(BF)


def on_device(plan, tokens, routes, combine, upstream, w_gate, w_up, w_down):
    tok, width, hidden = plan.tok, plan.width, plan.hidden
    inner, outer, part = plan.inner, plan.outer, plan.hidden // 2
    full = 2 * width + LANES
    shape = jax.ShapeDtypeStruct
    info = jnp.asarray(plan.table())[lax.axis_index("expert")]
    keys = [jnp.asarray(k) for k in plan.keys]
    swap = [(0, 1), (1, 0)]

    block = pl.pallas_call(
        functools.partial(pack_kernel, plan),
        out_shape=shape((tok, full), BF),
        in_specs=[VMEM] * 4,
        out_specs=VMEM,
        compiler_params=params(),
        cost_estimate=cost(1e6, 4 * tok * full),
        name="pack",
    )(tokens, upstream, routes.T, combine.T)

    others = [lax.ppermute(w, "dp", swap) for w in (w_gate, w_up, w_down)]
    blocks = [block] * plan.cands
    blocks[1] = lax.ppermute(block, "expert", plan.line(1))
    blocks[outer] = lax.ppermute(block, "expert", plan.line(-1))
    *others, blocks[1], blocks[outer] = lax.optimization_barrier(
        (*others, blocks[1], blocks[outer])
    )
    weights = []
    for w, other in zip((w_gate, w_up, w_down), others):
        weights += [w, other]

    def compact(c):
        rows, use = plan.rows[c], plan.use[c]
        count, n = inner * rows, len(use)
        return pl.pallas_call(
            functools.partial(compact_kernel, plan, c),
            out_shape=[shape((2 * rows, width), BF)] * inner,
            in_specs=[SMEM, VMEM] + [ANY] * n,
            out_specs=[VMEM] * inner,
            scratch_shapes=[
                pltpu.VMEM((n * tok, full), BF),
                pltpu.VMEM((n * tok, count), BF),
                pltpu.VMEM((n * tok, count), BF),
                pltpu.SemaphoreType.DMA((n,)),
            ],
            compiler_params=params(),
            cost_estimate=cost(4 * n * tok * count * width, 2 * n * tok * full),
            name="compact",
        )(info, keys[c], *[blocks[i] for i in use])

    def expert(c, arrived):
        rows = plan.rows[c]
        count = inner * rows
        return pl.pallas_call(
            functools.partial(expert_kernel, plan, c),
            out_shape=[shape((count, hidden), BF)] * 3
            + [shape((rows, width + LANES), BF)] * inner,
            in_specs=[SMEM] + [ANY] * (inner + 6),
            out_specs=[VMEM] * (3 + inner),
            scratch_shapes=[
                pltpu.VMEM((count, width), BF),
                pltpu.VMEM((count, width), BF),
                pltpu.VMEM((width, hidden), BF),
                pltpu.VMEM((width, hidden), BF),
                pltpu.VMEM((hidden, width), BF),
                pltpu.VMEM((count, 1), F32),
                pltpu.SemaphoreType.DMA((2 * inner + 6 * (hidden // 128),)),
            ],
            compiler_params=params(),
            cost_estimate=cost(10 * count * hidden * width, 6 * hidden * width),
            name="expert",
        )(info, *arrived, *weights)

    def cross(arrays):
        return [arrays[0]] + [
            lax.ppermute(arrays[d], "expert", plan.across(d)) for d in range(1, inner)
        ]

    near = max((i if i < outer else i - outer + 1) for i in plan.use[0])
    for r in range(2, near + 1):
        blocks[r] = lax.ppermute(blocks[r - 1], "expert", plan.line(1))
        blocks[outer - 1 + r] = lax.ppermute(blocks[outer - 2 + r], "expert", plan.line(-1))
    sent = compact(0)
    for r in range(near + 1, outer):
        blocks[r] = lax.ppermute(blocks[r - 1], "expert", plan.line(1))
        blocks[outer - 1 + r] = lax.ppermute(blocks[outer - 2 + r], "expert", plan.line(-1))
        if r == near + 1:
            blocks[r], blocks[outer - 1 + r], sent = lax.optimization_barrier(
                (blocks[r], blocks[outer - 1 + r], sent)
            )
    got = cross(sent)
    late = cross(compact(1))
    outs = expert(0, got)
    outs, late = lax.optimization_barrier((outs, late))
    backs = cross(outs[3:])
    more = expert(1, late)
    backs, more = lax.optimization_barrier((backs, more))
    got = got + late
    mids = outs[:3] + more[:3]
    backs = backs + cross(more[3:])

    count = inner * sum(plan.rows)

    def weight_grads(own, extra):
        return pl.pallas_call(
            functools.partial(weight_kernel, plan, own),
            out_shape=[
                shape((1, width, part), BF),
                shape((1, width, part), BF),
                shape((1, part, width), BF),
            ],
            in_specs=[ANY] * (2 * inner + 6) + [VMEM] * len(extra),
            out_specs=[VMEM] * 3,
            scratch_shapes=[
                pltpu.VMEM((count, width), BF),
                pltpu.VMEM((count, width), BF),
                pltpu.VMEM((count, part), BF),
                pltpu.VMEM((count, 2 * part), BF),
                pltpu.SemaphoreType.DMA((4 * inner + 6,)),
            ],
            compiler_params=params(),
            cost_estimate=cost(6 * count * part * width, 4 * count * (width + hidden)),
            name="weight_grads",
        )(*got, *mids, *extra)

    def spread(homes, chunks, extra):
        slots = inner * sum(plan.rows[:chunks])
        return pl.pallas_call(
            functools.partial(spread_kernel, plan, homes, chunks),
            out_shape=[shape((tok, width + LANES), BF)] * len(homes),
            in_specs=[SMEM, VMEM] + [ANY] * (plan.cands + chunks * inner + len(extra)),
            out_specs=[VMEM] * len(homes),
            scratch_shapes=[
                pltpu.VMEM((slots, width + LANES), BF),
                pltpu.VMEM((plan.cands, tok, LANES), BF),
                pltpu.VMEM((len(homes) * tok, slots), BF),
                pltpu.SemaphoreType.DMA((chunks * inner,)),
                pltpu.SemaphoreType.DMA((plan.cands,)),
            ],
            compiler_params=params(),
            cost_estimate=cost(2 * len(homes) * tok * slots * width, 2 * slots * width),
            name="spread",
        )(
            info,
            jnp.concatenate(keys[:chunks], axis=1),
            *blocks,
            *backs[: chunks * inner],
            *extra,
        )

    (first,) = spread([1], 1, [mids[3]])
    sums = {1: first}
    came = [lax.ppermute(first, "expert", plan.flip(1))]
    mine = weight_grads(False, [])
    mine, backs = lax.optimization_barrier((mine, backs))
    theirs = [lax.ppermute(w, "dp", swap) for w in mine]
    rest = [r for r in range(outer) if r != 1]
    sums.update(zip(rest, spread(rest, 2, [mine[0]])))
    bit = 1
    while bit < outer:
        for r in range(bit, outer, 2 * bit):
            if r == 1:
                continue
            sent = lax.ppermute(sums[r], "expert", plan.flip(bit))
            if r == bit:
                came.append(sent)
            else:
                sums[r - bit] = pl.pallas_call(
                    add_kernel,
                    out_shape=shape((tok, width + LANES), BF),
                    in_specs=[VMEM] * 2,
                    out_specs=VMEM,
                    name="add",
                )(sums[r - bit], sent)
        bit *= 2
    grads = weight_grads(True, theirs)
    home = [sums[0]] + came
    grad_tokens, grad_combine = pl.pallas_call(
        functools.partial(home_kernel, plan, len(home)),
        out_shape=[shape((tok, width), BF), shape((plan.top, tok), BF)],
        in_specs=[VMEM] * (len(home) + 2) + [ANY],
        out_specs=[VMEM] * 2,
        compiler_params=params(),
        cost_estimate=cost(1e6, 2 * tok * width * (outer + 1)),
        name="home",
    )(*home, routes.T, combine.T, grads[0])
    return (grad_tokens, grad_combine.T, *grads)


def solution(mesh):
    rows = P(("parts", "dp", "expert"), None)
    in_specs = (rows,) * 4 + (P("expert", None, "dp"),) * 2 + (P("expert", "dp", None),)
    out_specs = (rows,) * 2 + (P(("parts", "expert"), None, "dp"),) * 2
    out_specs += (P(("parts", "expert"), "dp", None),)
    shape = dict(mesh.shape)

    def whole(tokens, routes, combine, upstream, w_gate, w_up, w_down):
        devices = shape["parts"] * shape["dp"] * shape["expert"]
        plan = Plan(
            shape["expert"],
            tokens.shape[0] // devices,
            routes.shape[1],
            tokens.shape[1],
            w_gate.shape[2],
        )
        body = functools.partial(on_device, plan)
        return jax.shard_map(
            body, mesh=mesh, in_specs=in_specs, out_specs=out_specs, check_vma=False
        )(tokens, routes, combine, upstream, w_gate, w_up, w_down)

    return whole
```

```python
import functools

import jax
import jax.numpy as jnp
import numpy as np
from jax import lax
from jax.experimental import pallas as pl
from jax.experimental.pallas import tpu as pltpu
from jax.sharding import PartitionSpec as P

BF = jnp.bfloat16
F32 = jnp.float32
LANES = 128
HALF = 64
STRIDE = 1024
PARTS = 4
NOWHERE = -(1 << 20)
ANY = pl.BlockSpec(memory_space=pltpu.HBM)
VMEM = pl.BlockSpec(memory_space=pltpu.VMEM)
SMEM = pl.BlockSpec(memory_space=pltpu.SMEM)
TN = (((0,), (0,)), ((), ()))
NT = (((1,), (1,)), ((), ()))


def params(megabytes=60):
    return pltpu.CompilerParams(vmem_limit_bytes=megabytes << 20)


def cost(flops, moved):
    return pl.CostEstimate(flops=int(flops), bytes_accessed=int(moved), transcendentals=0)


class Plan:
    def __init__(self, experts, tok, top, width, hidden):
        self.experts, self.tok, self.top = experts, tok, top
        self.width, self.hidden = width, hidden
        outer = 1
        while outer * outer < experts:
            outer *= 2
        self.outer, self.inner = outer, experts // outer
        mean = tok * top // experts
        self.cap = min(tok, max(2, mean + tok * top // (8 * experts)))
        total = -(-self.outer * self.cap // 16) * 16
        step = self.outer // PARTS
        marks = [k * step * self.cap // 16 * 16 for k in range(PARTS)] + [total]
        self.chunks = [(marks[k], marks[k + 1]) for k in range(PARTS)]
        self.rows = [b - a for a, b in self.chunks]
        self.steps = [(k + 1) * step - 1 for k in range(PARTS)]
        self.groups = [range(PARTS - 1), range(PARTS - 1, PARTS)]
        self.spans = [(marks[g[0]], marks[g[-1] + 1]) for g in self.groups]
        self.sizes = [b - a for a, b in self.spans]
        self.cands = 2 * self.outer - 1
        self.use = [self.used(*c) for c in self.chunks]

    def keys(self, spans):
        return np.array(
            [[d * STRIDE + q for a, b in spans for d in range(self.inner) for q in range(a, b)]],
            np.int32,
        )

    def order(self, z):
        rest = [s for s in range(self.outer) if s not in (z, z ^ 1)]
        return [z, z ^ 1] + sorted(rest, key=lambda s: abs(s - z))

    def cand(self, z, source):
        if source == z:
            return 0
        return z - source if source < z else self.outer - 1 + source - z

    def used(self, a, b):
        slots = [k for k in range(self.outer) if k * self.cap < b and (k + 1) * self.cap > a]
        return sorted(
            {self.cand(z, self.order(z)[k]) for z in range(self.outer) for k in slots}
        )

    def partner(self, p, d):
        return p ^ d if self.inner & (self.inner - 1) == 0 else (d - p) % self.inner

    def table(self):
        rows = []
        for e in range(self.experts):
            z, p = divmod(e, self.inner)
            offs = [NOWHERE] * self.cands
            for slot, source in enumerate(self.order(z)):
                offs[self.cand(z, source)] = slot * self.cap
            experts = [z * self.inner + self.partner(p, d) for d in range(self.inner)]
            homes = [self.cand(z, z ^ r) for r in range(self.outer)]
            rows.append(offs + experts + homes)
        return np.array(rows, np.int32)

    def line(self, step):
        return [
            (z * self.inner + p, (z + step) * self.inner + p)
            for z in range(self.outer)
            for p in range(self.inner)
            if 0 <= z + step < self.outer
        ]

    def across(self, d):
        return [
            (z * self.inner + p, z * self.inner + self.partner(p, d))
            for z in range(self.outer)
            for p in range(self.inner)
        ]

    def flip(self, r):
        return [
            (z * self.inner + p, (z ^ r) * self.inner + p)
            for z in range(self.outer)
            for p in range(self.inner)
        ]


def pack_kernel(plan, tok_ref, up_ref, routes_ref, comb_ref, out_ref):
    tok, width = plan.tok, plan.width
    out_ref[:, :width] = tok_ref[...]
    out_ref[:, width : 2 * width] = up_ref[...]
    kind = lax.broadcasted_iota(jnp.int32, (LANES, tok), 0)
    weight = jnp.zeros((LANES, tok), F32)
    named = jnp.zeros((LANES, tok), F32)
    comb = comb_ref[...].astype(F32)
    for k in range(plan.top):
        e = routes_ref[k : k + 1, :]
        weight = jnp.where(kind == e, comb[k : k + 1, :], weight)
        named = jnp.where(kind == e + HALF, 1.0, named)
    row = lax.broadcasted_iota(jnp.int32, (tok, tok), 0)
    col = lax.broadcasted_iota(jnp.int32, (tok, tok), 1)
    upto = jnp.where(row <= col, 1.0, 0.0).astype(BF)
    count = jnp.dot(named.astype(BF), upto, preferred_element_type=F32)
    table = (weight + count * named).astype(BF)
    same = jnp.where(row == col, 1.0, 0.0).astype(BF)
    turned = lax.dot_general(same, table, NT, preferred_element_type=F32)
    out_ref[:, 2 * width :] = turned.astype(BF)


def picks(plan, meta, off, experts, key, scaled):
    tok = meta.shape[0]
    lane = lax.broadcasted_iota(jnp.int32, (tok, LANES), 1)
    one = jnp.zeros((tok, key.shape[1]), F32)
    two = jnp.zeros((tok, key.shape[1]), F32)
    for d, e in enumerate(experts):
        place = jnp.sum(jnp.where(lane == e + HALF, meta, 0.0), axis=1, keepdims=True)
        place = place.astype(jnp.int32)
        spot = jnp.where(place > 0, place - 1 + off + d * STRIDE, -1)
        hit = spot == key
        one = jnp.where(hit, 1.0, one)
        if scaled:
            weight = jnp.sum(jnp.where(lane == e, meta, 0.0), axis=1, keepdims=True)
            two = jnp.where(hit, weight, two)
    return one, two


def compact_kernel(plan, chunk, *refs):
    use, rows = plan.use[chunk], plan.rows[chunk]
    n, width, tok, inner = len(use), plan.width, plan.tok, plan.inner
    info, key_ref = refs[:2]
    blocks, outs = refs[2 : 2 + n], refs[2 + n : 2 + n + inner]
    held, one_s, two_s, sems = refs[2 + n + inner :]
    copies = [
        pltpu.make_async_copy(b, held.at[pl.ds(i * tok, tok)], sems.at[i])
        for i, b in enumerate(blocks)
    ]
    for c in copies:
        c.start()
    experts = [info[plan.cands + d] for d in range(inner)]
    for i, c in enumerate(copies):
        c.wait()
        meta = held[i * tok : (i + 1) * tok, 2 * width :].astype(F32)
        one, two = picks(plan, meta, info[use[i]], experts, key_ref[...], True)
        one_s[i * tok : (i + 1) * tok, :] = one.astype(BF)
        two_s[i * tok : (i + 1) * tok, :] = two.astype(BF)
    for part, source in ((0, one_s), (1, two_s)):
        have = held[:, part * width : (part + 1) * width]
        found = lax.dot_general(source[...], have, TN, preferred_element_type=F32).astype(BF)
        for d in range(inner):
            outs[d][part * rows : (part + 1) * rows, :] = found[d * rows : (d + 1) * rows]


def pieces(plan, group, got, x_s, d_s, sems, base=0):
    inner, size, first = plan.inner, plan.sizes[group], plan.spans[group][0]
    x_copies, d_copies = [], []
    for i, g in enumerate(got):
        c, d = plan.groups[group][i // inner], i % inner
        rows = plan.rows[c]
        to = pl.ds(base + d * size + plan.chunks[c][0] - first, rows)
        x_copies.append(pltpu.make_async_copy(g.at[pl.ds(0, rows)], x_s.at[to], sems.at[2 * i]))
        d_copies.append(
            pltpu.make_async_copy(g.at[pl.ds(rows, rows)], d_s.at[to], sems.at[2 * i + 1])
        )
    return x_copies, d_copies


def expert_kernel(plan, group, *refs):
    inner, rows, width, hidden = plan.inner, plan.sizes[group], plan.width, plan.hidden
    part, count, n = hidden // 2, inner * rows, inner * len(plan.groups[group])
    info = refs[0]
    got, weights = refs[1 : 1 + n], refs[1 + n : 7 + n]
    hid_o, gate_o, up_o = refs[7 + n : 10 + n]
    backs = refs[10 + n : 10 + n + inner]
    x_s, d_s, wg_s, wu_s, wd_s, comb_s, sems = refs[10 + n + inner :]
    x_copies, d_copies = pieces(plan, group, got, x_s, d_s, sems)
    tile, tiles = 256, []
    for t in range(hidden // tile):
        for kind, where in ((0, wg_s), (1, wu_s), (2, wd_s)):
            at, here = t * tile, []
            while at < (t + 1) * tile:
                half, start = divmod(at, part)
                size = min((t + 1) * tile, (half + 1) * part) - at
                source, to = pl.ds(start, size), pl.ds(at, size)
                w = weights[2 * kind + half].at[0]
                here.append((w.at[source], where.at[to]) if kind == 2 else (w.at[:, source], where.at[:, to]))
                at += size
            tiles.append(here)
    w_copies, used = [], 2 * n
    for here in tiles:
        w_copies.append([])
        for source, to in here:
            w_copies[-1].append(pltpu.make_async_copy(source, to, sems.at[used]))
            used += 1
    for c in x_copies + w_copies[0] + w_copies[1] + d_copies:
        c.start()
    for here in w_copies[2:]:
        for c in here:
            c.start()
    for t in range(hidden // tile):
        at = slice(t * tile, (t + 1) * tile)
        gate_w, up_w, down_w = w_copies[3 * t : 3 * t + 3]
        for c in (x_copies if t == 0 else []) + gate_w:
            c.wait()
        gate = jnp.dot(x_s[...], wg_s[:, at], preferred_element_type=F32)
        for c in up_w:
            c.wait()
        up = jnp.dot(x_s[...], wu_s[:, at], preferred_element_type=F32)
        for c in (d_copies if t == 0 else []) + down_w:
            c.wait()
        mixed = lax.dot_general(d_s[...], wd_s[at, :], NT, preferred_element_type=F32)
        logistic = jax.nn.sigmoid(gate)
        silu = gate * logistic
        hid = (silu * up).astype(BF)
        hid_o[:, at] = hid
        comb = jnp.sum(hid.astype(F32) * mixed, axis=1, keepdims=True)
        comb_s[...] = comb if t == 0 else comb_s[...] + comb
        gate_o[:, at] = (mixed * up * logistic * (1.0 + gate * (1.0 - logistic))).astype(BF)
        up_o[:, at] = (mixed * silu).astype(BF)

    wide = 256

    @pl.loop(0, width // wide)
    def _(j):
        at = pl.ds(pl.multiple_of(j * wide, wide), wide)
        back = lax.dot_general(gate_o[...], wg_s[at, :], NT, preferred_element_type=F32)
        back += lax.dot_general(up_o[...], wu_s[at, :], NT, preferred_element_type=F32)
        back = back.astype(BF)
        for d in range(inner):
            backs[d][:, at] = back[d * rows : (d + 1) * rows]

    lane = lax.broadcasted_iota(jnp.int32, (count, LANES), 1)
    comb = jnp.where(lane == info[plan.cands], comb_s[...], 0.0).astype(BF)
    for d in range(inner):
        backs[d][:, width:] = comb[d * rows : (d + 1) * rows]


def weight_kernel(plan, own, *refs):
    inner, width, hidden = plan.inner, plan.width, plan.hidden
    part, n = hidden // 2, plan.inner * PARTS
    got, mids = refs[:n], refs[n : n + 6]
    at = n + 6
    theirs = refs[at : at + 3] if own else None
    at += 3 if own else 0
    g_o, u_o, d_o = refs[at : at + 3]
    x_s, d_s, h_s, gu_s, sems, mid_sems = refs[at + 3 :]
    everything, base, taken = [], 0, 0
    half = pl.ds(0 if own else part, part)
    for g in range(2):
        many = inner * len(plan.groups[g])
        mine = got[taken : taken + many]
        at_sems = sems.at[pl.ds(2 * taken, 2 * many)]
        x_copies, d_copies = pieces(plan, g, mine, x_s, d_s, at_sems, base)
        everything += x_copies + d_copies
        to = pl.ds(base, inner * plan.sizes[g])
        spots = (h_s.at[to], gu_s.at[to, pl.ds(0, part)], gu_s.at[to, pl.ds(part, part)])
        for i, (m, s) in enumerate(zip(mids[3 * g : 3 * g + 3], spots)):
            everything.append(
                pltpu.make_async_copy(m.at[:, half], s, mid_sems.at[3 * g + i])
            )
        taken += many
        base += inner * plan.sizes[g]
    for c in everything:
        c.start()
    for c in everything:
        c.wait()
    tile = 256

    @pl.loop(0, width // tile)
    def _(j):
        to = pl.ds(pl.multiple_of(j * tile, tile), tile)
        both = lax.dot_general(x_s[:, to], gu_s[...], TN, preferred_element_type=F32)
        first, second = both[:, :part], both[:, part:]
        if own:
            first += theirs[0][0, to, :].astype(F32)
            second += theirs[1][0, to, :].astype(F32)
        g_o[0, to, :] = first.astype(BF)
        u_o[0, to, :] = second.astype(BF)

    down = lax.dot_general(h_s[...], d_s[...], TN, preferred_element_type=F32)
    if own:
        down += theirs[2][0].astype(F32)
    d_o[0] = down.astype(BF)


def spread_kernel(plan, homes, groups, *refs):
    inner, tok, width = plan.inner, plan.tok, plan.width
    info, key_ref = refs[:2]
    blocks = refs[2 : 2 + plan.cands]
    at = 2 + plan.cands
    backs = refs[at : at + groups * inner]
    outs = refs[-5 - len(homes) : -5]
    held, metas, pick_s, sems, meta_sems = refs[-5:]
    copies, later, start = [], [], 0
    for i, b in enumerate(blocks):
        copies.append(
            pltpu.make_async_copy(b.at[:, pl.ds(2 * width, LANES)], metas.at[i], meta_sems.at[i])
        )
    for i, b in enumerate(backs):
        rows = plan.sizes[i // inner]
        later.append(pltpu.make_async_copy(b, held.at[pl.ds(start, rows)], sems.at[i]))
        start += rows
    for c in copies + later:
        c.start()
    for c in copies:
        c.wait()
    experts = [info[plan.cands + d] for d in range(inner)]
    for i, r in enumerate(homes):
        which = info[plan.cands + inner + r]
        meta = metas[which].astype(F32)
        one, _ = picks(plan, meta, info[which], experts, key_ref[...], False)
        pick_s[i * tok : (i + 1) * tok, :] = one.astype(BF)
    for c in later:
        c.wait()
    tile = 256

    def piece(at, size):
        sums = jnp.dot(pick_s[...], held[:, pl.ds(at, size)], preferred_element_type=F32)
        sums = sums.astype(BF)
        for i in range(len(homes)):
            outs[i][:, pl.ds(at, size)] = sums[i * tok : (i + 1) * tok]

    @pl.loop(0, width // tile)
    def _(j):
        piece(pl.multiple_of(j * tile, tile), tile)

    piece(width, LANES)


def add_kernel(a_ref, b_ref, o_ref):
    o_ref[...] = (a_ref[...].astype(F32) + b_ref[...].astype(F32)).astype(BF)


def home_kernel(plan, count, *refs):
    parts = refs[:count]
    routes_ref, comb_ref, _, tok_o, comb_o = refs[count:]
    width, tok = plan.width, plan.tok
    total = parts[0][...].astype(F32)
    for p in parts[1:]:
        total += p[...].astype(F32)
    tok_o[...] = total[:, :width].astype(BF)
    row = lax.broadcasted_iota(jnp.int32, (LANES, LANES), 0)
    col = lax.broadcasted_iota(jnp.int32, (LANES, LANES), 1)
    same = jnp.where(row == col, 1.0, 0.0).astype(BF)
    found = total[:, width:].astype(BF)
    found = lax.dot_general(same, found, NT, preferred_element_type=F32)
    kind = lax.broadcasted_iota(jnp.int32, (LANES, tok), 0)
    out = []
    for k in range(plan.top):
        mine = jnp.where(kind == routes_ref[k : k + 1, :], found, 0.0)
        out.append(jnp.sum(mine, axis=0, keepdims=True))
    out = jnp.concatenate(out, axis=0)
    comb_o[...] = (out / comb_ref[...].astype(F32)).astype(BF)


def on_device(plan, tokens, routes, combine, upstream, w_gate, w_up, w_down):
    tok, width, hidden = plan.tok, plan.width, plan.hidden
    inner, outer, part = plan.inner, plan.outer, plan.hidden // 2
    full = 2 * width + LANES
    shape = jax.ShapeDtypeStruct
    info = jnp.asarray(plan.table())[lax.axis_index("expert")]
    swap = [(0, 1), (1, 0)]

    block = pl.pallas_call(
        functools.partial(pack_kernel, plan),
        out_shape=shape((tok, full), BF),
        in_specs=[VMEM] * 4,
        out_specs=VMEM,
        compiler_params=params(),
        cost_estimate=cost(1e6, 4 * tok * full),
        name="pack",
    )(tokens, upstream, routes.T, combine.T)

    others = [lax.ppermute(w, "dp", swap) for w in (w_gate, w_up, w_down)]
    blocks = [block] * plan.cands
    blocks[1] = lax.ppermute(block, "expert", plan.line(1))
    blocks[outer] = lax.ppermute(block, "expert", plan.line(-1))
    *others, blocks[1], blocks[outer] = lax.optimization_barrier(
        (*others, blocks[1], blocks[outer])
    )
    weights = []
    for w, other in zip((w_gate, w_up, w_down), others):
        weights += [w, other]

    def compact(c):
        rows, use = plan.rows[c], plan.use[c]
        count, n = inner * rows, len(use)
        return pl.pallas_call(
            functools.partial(compact_kernel, plan, c),
            out_shape=[shape((2 * rows, width), BF)] * inner,
            in_specs=[SMEM, VMEM] + [ANY] * n,
            out_specs=[VMEM] * inner,
            scratch_shapes=[
                pltpu.VMEM((n * tok, full), BF),
                pltpu.VMEM((n * tok, count), BF),
                pltpu.VMEM((n * tok, count), BF),
                pltpu.SemaphoreType.DMA((n,)),
            ],
            compiler_params=params(),
            cost_estimate=cost(4 * n * tok * count * width, 2 * n * tok * full),
            name="compact",
        )(info, jnp.asarray(plan.keys([plan.chunks[c]])), *[blocks[i] for i in use])

    def expert(g, arrived):
        rows, n = plan.sizes[g], inner * len(plan.groups[g])
        count = inner * rows
        return pl.pallas_call(
            functools.partial(expert_kernel, plan, g),
            out_shape=[shape((count, hidden), BF)] * 3
            + [shape((rows, width + LANES), BF)] * inner,
            in_specs=[SMEM] + [ANY] * (n + 6),
            out_specs=[VMEM] * (3 + inner),
            scratch_shapes=[
                pltpu.VMEM((count, width), BF),
                pltpu.VMEM((count, width), BF),
                pltpu.VMEM((width, hidden), BF),
                pltpu.VMEM((width, hidden), BF),
                pltpu.VMEM((hidden, width), BF),
                pltpu.VMEM((count, 1), F32),
                pltpu.SemaphoreType.DMA((2 * n + 6 * (hidden // 128),)),
            ],
            compiler_params=params(),
            cost_estimate=cost(10 * count * hidden * width, 6 * hidden * width),
            name="expert",
        )(info, *arrived, *weights)

    def cross(arrays):
        return [arrays[0]] + [
            lax.ppermute(arrays[d], "expert", plan.across(d)) for d in range(1, inner)
        ]

    got, done = [], 1
    for c in range(PARTS):
        for r in range(done + 1, plan.steps[c] + 1):
            blocks[r] = lax.ppermute(blocks[r - 1], "expert", plan.line(1))
            blocks[outer - 1 + r] = lax.ppermute(blocks[outer - 2 + r], "expert", plan.line(-1))
        done = max(done, plan.steps[c])
        if c >= 2:
            got[c - 2], low, high = lax.optimization_barrier(
                (got[c - 2], blocks[done], blocks[outer - 1 + done])
            )
            blocks[done], blocks[outer - 1 + done] = low, high
        sent = compact(c)
        got.append(cross(sent))
    outs = expert(0, sum(got[:-1], []))
    late = got[-1]
    outs, late = lax.optimization_barrier((outs, late))
    got[-1] = late
    backs = cross(outs[3:])
    more = expert(1, late)
    backs, more = lax.optimization_barrier((backs, more))
    got = sum(got, [])
    mids = outs[:3] + more[:3]
    backs = backs + cross(more[3:])

    count = inner * sum(plan.rows)

    def weight_grads(own, extra):
        return pl.pallas_call(
            functools.partial(weight_kernel, plan, own),
            out_shape=[
                shape((1, width, part), BF),
                shape((1, width, part), BF),
                shape((1, part, width), BF),
            ],
            in_specs=[ANY] * (inner * PARTS + 6) + [VMEM] * len(extra),
            out_specs=[VMEM] * 3,
            scratch_shapes=[
                pltpu.VMEM((count, width), BF),
                pltpu.VMEM((count, width), BF),
                pltpu.VMEM((count, part), BF),
                pltpu.VMEM((count, 2 * part), BF),
                pltpu.SemaphoreType.DMA((2 * inner * PARTS,)),
                pltpu.SemaphoreType.DMA((6,)),
            ],
            compiler_params=params(),
            cost_estimate=cost(6 * count * part * width, 4 * count * (width + hidden)),
            name="weight_grads",
        )(*got, *mids, *extra)

    def spread(homes, groups, extra):
        slots = inner * sum(plan.sizes[:groups])
        return pl.pallas_call(
            functools.partial(spread_kernel, plan, homes, groups),
            out_shape=[shape((tok, width + LANES), BF)] * len(homes),
            in_specs=[SMEM, VMEM] + [ANY] * (plan.cands + groups * inner + len(extra)),
            out_specs=[VMEM] * len(homes),
            scratch_shapes=[
                pltpu.VMEM((slots, width + LANES), BF),
                pltpu.VMEM((plan.cands, tok, LANES), BF),
                pltpu.VMEM((len(homes) * tok, slots), BF),
                pltpu.SemaphoreType.DMA((groups * inner,)),
                pltpu.SemaphoreType.DMA((plan.cands,)),
            ],
            compiler_params=params(),
            cost_estimate=cost(2 * len(homes) * tok * slots * width, 2 * slots * width),
            name="spread",
        )(
            info,
            jnp.asarray(plan.keys(plan.spans[:groups])),
            *blocks,
            *backs[: groups * inner],
            *extra,
        )

    (first,) = spread([1], 1, [mids[3]])
    sums = {}
    mine = weight_grads(False, [])
    mine, backs, first = lax.optimization_barrier((mine, backs, first))
    came = [lax.ppermute(first, "expert", plan.flip(1))]
    theirs = [lax.ppermute(w, "dp", swap) for w in mine]
    rest = [r for r in range(outer) if r != 1]
    sums.update(zip(rest, spread(rest, 2, [mine[0], first])))
    bit = 1
    while bit < outer:
        for r in range(bit, outer, 2 * bit):
            if r == 1:
                continue
            sent = lax.ppermute(sums[r], "expert", plan.flip(bit))
            if r == bit:
                came.append(sent)
            else:
                sums[r - bit] = pl.pallas_call(
                    add_kernel,
                    out_shape=shape((tok, width + LANES), BF),
                    in_specs=[VMEM] * 2,
                    out_specs=VMEM,
                    name="add",
                )(sums[r - bit], sent)
        bit *= 2
    grads = weight_grads(True, theirs)
    home = [sums[0]] + came
    grad_tokens, grad_combine = pl.pallas_call(
        functools.partial(home_kernel, plan, len(home)),
        out_shape=[shape((tok, width), BF), shape((plan.top, tok), BF)],
        in_specs=[VMEM] * (len(home) + 2) + [ANY],
        out_specs=[VMEM] * 2,
        compiler_params=params(),
        cost_estimate=cost(1e6, 2 * tok * width * (outer + 1)),
        name="home",
    )(*home, routes.T, combine.T, grads[0])
    return (grad_tokens, grad_combine.T, *grads)


def solution(mesh):
    rows = P(("parts", "dp", "expert"), None)
    in_specs = (rows,) * 4 + (P("expert", None, "dp"),) * 2 + (P("expert", "dp", None),)
    out_specs = (rows,) * 2 + (P(("parts", "expert"), None, "dp"),) * 2
    out_specs += (P(("parts", "expert"), "dp", None),)
    shape = dict(mesh.shape)

    def whole(tokens, routes, combine, upstream, w_gate, w_up, w_down):
        devices = shape["parts"] * shape["dp"] * shape["expert"]
        plan = Plan(
            shape["expert"],
            tokens.shape[0] // devices,
            routes.shape[1],
            tokens.shape[1],
            w_gate.shape[2],
        )
        body = functools.partial(on_device, plan)
        return jax.shard_map(
            body, mesh=mesh, in_specs=in_specs, out_specs=out_specs, check_vma=False
        )(tokens, routes, combine, upstream, w_gate, w_up, w_down)

    return whole
```

```python
import functools

import jax
import jax.numpy as jnp
import numpy as np
from jax import lax
from jax.experimental import pallas as pl
from jax.experimental.pallas import tpu as pltpu
from jax.sharding import PartitionSpec as P

BF = jnp.bfloat16
F32 = jnp.float32
LANES = 128
HALF = 64
STRIDE = 1024
PARTS = 4
NOWHERE = -(1 << 20)
ANY = pl.BlockSpec(memory_space=pltpu.HBM)
VMEM = pl.BlockSpec(memory_space=pltpu.VMEM)
SMEM = pl.BlockSpec(memory_space=pltpu.SMEM)
TN = (((0,), (0,)), ((), ()))
NT = (((1,), (1,)), ((), ()))


def params(megabytes=60):
    return pltpu.CompilerParams(vmem_limit_bytes=megabytes << 20)


def cost(flops, moved):
    return pl.CostEstimate(flops=int(flops), bytes_accessed=int(moved), transcendentals=0)


class Plan:
    def __init__(self, experts, tok, top, width, hidden):
        self.experts, self.tok, self.top = experts, tok, top
        self.width, self.hidden = width, hidden
        outer = 1
        while outer * outer < experts:
            outer *= 2
        self.outer, self.inner = outer, experts // outer
        mean = tok * top // experts
        self.cap = min(tok, max(2, mean + tok * top // (8 * experts)))
        total = -(-self.outer * self.cap // 16) * 16
        step = self.outer // PARTS
        marks = [k * step * self.cap // 16 * 16 for k in range(PARTS)] + [total]
        self.chunks = [(marks[k], marks[k + 1]) for k in range(PARTS)]
        self.rows = [b - a for a, b in self.chunks]
        self.steps = [(k + 1) * step - 1 for k in range(PARTS)]
        self.groups = [range(PARTS - 1), range(PARTS - 1, PARTS)]
        self.spans = [(marks[g[0]], marks[g[-1] + 1]) for g in self.groups]
        self.sizes = [b - a for a, b in self.spans]
        self.cands = 2 * self.outer - 1
        self.use = [self.used(*c) for c in self.chunks]

    def keys(self, spans):
        return np.array(
            [[d * STRIDE + q for a, b in spans for d in range(self.inner) for q in range(a, b)]],
            np.int32,
        )

    def order(self, z):
        rest = [s for s in range(self.outer) if s not in (z, z ^ 1)]
        return [z, z ^ 1] + sorted(rest, key=lambda s: abs(s - z))

    def cand(self, z, source):
        if source == z:
            return 0
        return z - source if source < z else self.outer - 1 + source - z

    def used(self, a, b):
        slots = [k for k in range(self.outer) if k * self.cap < b and (k + 1) * self.cap > a]
        return sorted(
            {self.cand(z, self.order(z)[k]) for z in range(self.outer) for k in slots}
        )

    def partner(self, p, d):
        return p ^ d if self.inner & (self.inner - 1) == 0 else (d - p) % self.inner

    def table(self):
        rows = []
        for e in range(self.experts):
            z, p = divmod(e, self.inner)
            offs = [NOWHERE] * self.cands
            for slot, source in enumerate(self.order(z)):
                offs[self.cand(z, source)] = slot * self.cap
            experts = [z * self.inner + self.partner(p, d) for d in range(self.inner)]
            homes = [self.cand(z, z ^ r) for r in range(self.outer)]
            rows.append(offs + experts + homes)
        return np.array(rows, np.int32)

    def line(self, step):
        return [
            (z * self.inner + p, (z + step) * self.inner + p)
            for z in range(self.outer)
            for p in range(self.inner)
            if 0 <= z + step < self.outer
        ]

    def across(self, d):
        return [
            (z * self.inner + p, z * self.inner + self.partner(p, d))
            for z in range(self.outer)
            for p in range(self.inner)
        ]

    def flip(self, r):
        return [
            (z * self.inner + p, (z ^ r) * self.inner + p)
            for z in range(self.outer)
            for p in range(self.inner)
        ]


def pack_kernel(plan, tok_ref, up_ref, routes_ref, comb_ref, out_ref):
    tok, width = plan.tok, plan.width
    out_ref[:, :width] = tok_ref[...]
    out_ref[:, width : 2 * width] = up_ref[...]
    kind = lax.broadcasted_iota(jnp.int32, (LANES, tok), 0)
    weight = jnp.zeros((LANES, tok), F32)
    named = jnp.zeros((LANES, tok), F32)
    comb = comb_ref[...].astype(F32)
    for k in range(plan.top):
        e = routes_ref[k : k + 1, :]
        weight = jnp.where(kind == e, comb[k : k + 1, :], weight)
        named = jnp.where(kind == e + HALF, 1.0, named)
    row = lax.broadcasted_iota(jnp.int32, (tok, tok), 0)
    col = lax.broadcasted_iota(jnp.int32, (tok, tok), 1)
    upto = jnp.where(row <= col, 1.0, 0.0).astype(BF)
    count = jnp.dot(named.astype(BF), upto, preferred_element_type=F32)
    table = (weight + count * named).astype(BF)
    same = jnp.where(row == col, 1.0, 0.0).astype(BF)
    turned = lax.dot_general(same, table, NT, preferred_element_type=F32)
    out_ref[:, 2 * width :] = turned.astype(BF)


def picks(plan, meta, off, experts, key, scaled):
    tok = meta.shape[0]
    lane = lax.broadcasted_iota(jnp.int32, (tok, LANES), 1)
    one = jnp.zeros((tok, key.shape[1]), F32)
    two = jnp.zeros((tok, key.shape[1]), F32)
    for d, e in enumerate(experts):
        place = jnp.sum(jnp.where(lane == e + HALF, meta, 0.0), axis=1, keepdims=True)
        place = place.astype(jnp.int32)
        spot = jnp.where(place > 0, place - 1 + off + d * STRIDE, -1)
        hit = spot == key
        one = jnp.where(hit, 1.0, one)
        if scaled:
            weight = jnp.sum(jnp.where(lane == e, meta, 0.0), axis=1, keepdims=True)
            two = jnp.where(hit, weight, two)
    return one, two


def compact_kernel(plan, chunk, *refs):
    use, rows = plan.use[chunk], plan.rows[chunk]
    n, width, tok, inner = len(use), plan.width, plan.tok, plan.inner
    info, key_ref = refs[:2]
    blocks, outs = refs[2 : 2 + n], refs[2 + n : 2 + n + inner]
    held, one_s, two_s, sems = refs[2 + n + inner :]
    copies = [
        pltpu.make_async_copy(b, held.at[pl.ds(i * tok, tok)], sems.at[i])
        for i, b in enumerate(blocks)
    ]
    for c in copies:
        c.start()
    experts = [info[plan.cands + d] for d in range(inner)]
    for i, c in enumerate(copies):
        c.wait()
        meta = held[i * tok : (i + 1) * tok, 2 * width :].astype(F32)
        one, two = picks(plan, meta, info[use[i]], experts, key_ref[...], True)
        one_s[i * tok : (i + 1) * tok, :] = one.astype(BF)
        two_s[i * tok : (i + 1) * tok, :] = two.astype(BF)
    for part, source in ((0, one_s), (1, two_s)):
        have = held[:, part * width : (part + 1) * width]
        found = lax.dot_general(source[...], have, TN, preferred_element_type=F32).astype(BF)
        for d in range(inner):
            outs[d][part * rows : (part + 1) * rows, :] = found[d * rows : (d + 1) * rows]


def pieces(plan, group, got, x_s, d_s, sems, base=0):
    inner, size, first = plan.inner, plan.sizes[group], plan.spans[group][0]
    x_copies, d_copies = [], []
    for i, g in enumerate(got):
        c, d = plan.groups[group][i // inner], i % inner
        rows = plan.rows[c]
        to = pl.ds(base + d * size + plan.chunks[c][0] - first, rows)
        x_copies.append(pltpu.make_async_copy(g.at[pl.ds(0, rows)], x_s.at[to], sems.at[2 * i]))
        d_copies.append(
            pltpu.make_async_copy(g.at[pl.ds(rows, rows)], d_s.at[to], sems.at[2 * i + 1])
        )
    return x_copies, d_copies


def expert_kernel(plan, group, *refs):
    inner, rows, width, hidden = plan.inner, plan.sizes[group], plan.width, plan.hidden
    part, count, n = hidden // 2, inner * rows, inner * len(plan.groups[group])
    info = refs[0]
    got, weights = refs[1 : 1 + n], refs[1 + n : 7 + n]
    hid_o, gate_o, up_o = refs[7 + n : 10 + n]
    backs = refs[10 + n : 10 + n + inner]
    x_s, d_s, wg_s, wu_s, wd_s, comb_s, sems = refs[10 + n + inner :]
    x_copies, d_copies = pieces(plan, group, got, x_s, d_s, sems)
    tile, tiles = hidden, []
    for t in range(hidden // tile):
        for kind, where in ((0, wg_s), (1, wu_s), (2, wd_s)):
            at, here = t * tile, []
            while at < (t + 1) * tile:
                half, start = divmod(at, part)
                size = min((t + 1) * tile, (half + 1) * part) - at
                source, to = pl.ds(start, size), pl.ds(at, size)
                w = weights[2 * kind + half].at[0]
                here.append((w.at[source], where.at[to]) if kind == 2 else (w.at[:, source], where.at[:, to]))
                at += size
            tiles.append(here)
    w_copies, used = [], 2 * n
    for here in tiles:
        w_copies.append([])
        for source, to in here:
            w_copies[-1].append(pltpu.make_async_copy(source, to, sems.at[used]))
            used += 1
    for c in x_copies + w_copies[0] + w_copies[1] + d_copies:
        c.start()
    for here in w_copies[2:]:
        for c in here:
            c.start()
    for t in range(hidden // tile):
        at = slice(t * tile, (t + 1) * tile)
        gate_w, up_w, down_w = w_copies[3 * t : 3 * t + 3]
        for c in (x_copies if t == 0 else []) + gate_w:
            c.wait()
        gate = jnp.dot(x_s[...], wg_s[:, at], preferred_element_type=F32)
        for c in up_w:
            c.wait()
        up = jnp.dot(x_s[...], wu_s[:, at], preferred_element_type=F32)
        for c in (d_copies if t == 0 else []) + down_w:
            c.wait()
        mixed = lax.dot_general(d_s[...], wd_s[at, :], NT, preferred_element_type=F32)
        logistic = jax.nn.sigmoid(gate)
        silu = gate * logistic
        hid = (silu * up).astype(BF)
        hid_o[:, at] = hid
        comb = jnp.sum(hid.astype(F32) * mixed, axis=1, keepdims=True)
        comb_s[...] = comb if t == 0 else comb_s[...] + comb
        gate_o[:, at] = (mixed * up * logistic * (1.0 + gate * (1.0 - logistic))).astype(BF)
        up_o[:, at] = (mixed * silu).astype(BF)

    wide = width // 2

    @pl.loop(0, width // wide)
    def _(j):
        at = pl.ds(pl.multiple_of(j * wide, wide), wide)
        back = lax.dot_general(gate_o[...], wg_s[at, :], NT, preferred_element_type=F32)
        back += lax.dot_general(up_o[...], wu_s[at, :], NT, preferred_element_type=F32)
        back = back.astype(BF)
        for d in range(inner):
            backs[d][:, at] = back[d * rows : (d + 1) * rows]

    lane = lax.broadcasted_iota(jnp.int32, (count, LANES), 1)
    comb = jnp.where(lane == info[plan.cands], comb_s[...], 0.0).astype(BF)
    for d in range(inner):
        backs[d][:, width:] = comb[d * rows : (d + 1) * rows]


def weight_kernel(plan, own, *refs):
    inner, width, hidden = plan.inner, plan.width, plan.hidden
    part, n = hidden // 2, plan.inner * PARTS
    got, mids = refs[:n], refs[n : n + 6]
    at = n + 6
    theirs = refs[at : at + 3] if own else None
    at += 3 if own else 0
    g_o, u_o, d_o = refs[at : at + 3]
    x_s, d_s, h_s, gu_s, sems, mid_sems = refs[at + 3 :]
    everything, base, taken = [], 0, 0
    half = pl.ds(0 if own else part, part)
    for g in range(2):
        many = inner * len(plan.groups[g])
        mine = got[taken : taken + many]
        at_sems = sems.at[pl.ds(2 * taken, 2 * many)]
        x_copies, d_copies = pieces(plan, g, mine, x_s, d_s, at_sems, base)
        everything += x_copies + d_copies
        to = pl.ds(base, inner * plan.sizes[g])
        spots = (h_s.at[to], gu_s.at[to, pl.ds(0, part)], gu_s.at[to, pl.ds(part, part)])
        for i, (m, s) in enumerate(zip(mids[3 * g : 3 * g + 3], spots)):
            everything.append(
                pltpu.make_async_copy(m.at[:, half], s, mid_sems.at[3 * g + i])
            )
        taken += many
        base += inner * plan.sizes[g]
    for c in everything:
        c.start()
    for c in everything:
        c.wait()
    tile = width // 2

    @pl.loop(0, width // tile)
    def _(j):
        to = pl.ds(pl.multiple_of(j * tile, tile), tile)
        both = lax.dot_general(x_s[:, to], gu_s[...], TN, preferred_element_type=F32)
        first, second = both[:, :part], both[:, part:]
        if own:
            first += theirs[0][0, to, :].astype(F32)
            second += theirs[1][0, to, :].astype(F32)
        g_o[0, to, :] = first.astype(BF)
        u_o[0, to, :] = second.astype(BF)

    down = lax.dot_general(h_s[...], d_s[...], TN, preferred_element_type=F32)
    if own:
        down += theirs[2][0].astype(F32)
    d_o[0] = down.astype(BF)


def spread_kernel(plan, homes, groups, *refs):
    inner, tok, width = plan.inner, plan.tok, plan.width
    info, key_ref = refs[:2]
    blocks = refs[2 : 2 + plan.cands]
    at = 2 + plan.cands
    backs = refs[at : at + groups * inner]
    outs = refs[-5 - len(homes) : -5]
    held, metas, pick_s, sems, meta_sems = refs[-5:]
    copies, later, start = [], [], 0
    for i, b in enumerate(blocks):
        copies.append(
            pltpu.make_async_copy(b.at[:, pl.ds(2 * width, LANES)], metas.at[i], meta_sems.at[i])
        )
    for i, b in enumerate(backs):
        rows = plan.sizes[i // inner]
        later.append(pltpu.make_async_copy(b, held.at[pl.ds(start, rows)], sems.at[i]))
        start += rows
    for c in copies + later:
        c.start()
    for c in copies:
        c.wait()
    experts = [info[plan.cands + d] for d in range(inner)]
    for i, r in enumerate(homes):
        which = info[plan.cands + inner + r]
        meta = metas[which].astype(F32)
        one, _ = picks(plan, meta, info[which], experts, key_ref[...], False)
        pick_s[i * tok : (i + 1) * tok, :] = one.astype(BF)
    for c in later:
        c.wait()
    sums = jnp.dot(pick_s[...], held[...], preferred_element_type=F32).astype(BF)
    for i in range(len(homes)):
        outs[i][...] = sums[i * tok : (i + 1) * tok]


def add_kernel(a_ref, b_ref, o_ref):
    o_ref[...] = (a_ref[...].astype(F32) + b_ref[...].astype(F32)).astype(BF)


def home_kernel(plan, count, *refs):
    parts = refs[:count]
    routes_ref, comb_ref, _, tok_o, comb_o = refs[count:]
    width, tok = plan.width, plan.tok
    total = parts[0][...].astype(F32)
    for p in parts[1:]:
        total += p[...].astype(F32)
    tok_o[...] = total[:, :width].astype(BF)
    row = lax.broadcasted_iota(jnp.int32, (LANES, LANES), 0)
    col = lax.broadcasted_iota(jnp.int32, (LANES, LANES), 1)
    same = jnp.where(row == col, 1.0, 0.0).astype(BF)
    found = total[:, width:].astype(BF)
    found = lax.dot_general(same, found, NT, preferred_element_type=F32)
    kind = lax.broadcasted_iota(jnp.int32, (LANES, tok), 0)
    out = []
    for k in range(plan.top):
        mine = jnp.where(kind == routes_ref[k : k + 1, :], found, 0.0)
        out.append(jnp.sum(mine, axis=0, keepdims=True))
    out = jnp.concatenate(out, axis=0)
    comb_o[...] = (out / comb_ref[...].astype(F32)).astype(BF)


def on_device(plan, tokens, routes, combine, upstream, w_gate, w_up, w_down):
    tok, width, hidden = plan.tok, plan.width, plan.hidden
    inner, outer, part = plan.inner, plan.outer, plan.hidden // 2
    full = 2 * width + LANES
    shape = jax.ShapeDtypeStruct
    info = jnp.asarray(plan.table())[lax.axis_index("expert")]
    swap = [(0, 1), (1, 0)]

    block = pl.pallas_call(
        functools.partial(pack_kernel, plan),
        out_shape=shape((tok, full), BF),
        in_specs=[VMEM] * 4,
        out_specs=VMEM,
        compiler_params=params(),
        cost_estimate=cost(1e6, 4 * tok * full),
        name="pack",
    )(tokens, upstream, routes.T, combine.T)

    others = [lax.ppermute(w, "dp", swap) for w in (w_gate, w_up, w_down)]
    blocks = [block] * plan.cands
    blocks[1] = lax.ppermute(block, "expert", plan.line(1))
    blocks[outer] = lax.ppermute(block, "expert", plan.line(-1))
    def compact(c):
        rows, use = plan.rows[c], plan.use[c]
        count, n = inner * rows, len(use)
        return pl.pallas_call(
            functools.partial(compact_kernel, plan, c),
            out_shape=[shape((2 * rows, width), BF)] * inner,
            in_specs=[SMEM, VMEM] + [ANY] * n,
            out_specs=[VMEM] * inner,
            scratch_shapes=[
                pltpu.VMEM((n * tok, full), BF),
                pltpu.VMEM((n * tok, count), BF),
                pltpu.VMEM((n * tok, count), BF),
                pltpu.SemaphoreType.DMA((n,)),
            ],
            compiler_params=params(),
            cost_estimate=cost(4 * n * tok * count * width, 2 * n * tok * full),
            name="compact",
        )(info, jnp.asarray(plan.keys([plan.chunks[c]])), *[blocks[i] for i in use])

    def expert(g, arrived):
        rows, n = plan.sizes[g], inner * len(plan.groups[g])
        count = inner * rows
        return pl.pallas_call(
            functools.partial(expert_kernel, plan, g),
            out_shape=[shape((count, hidden), BF)] * 3
            + [shape((rows, width + LANES), BF)] * inner,
            in_specs=[SMEM] + [ANY] * (n + 6),
            out_specs=[VMEM] * (3 + inner),
            scratch_shapes=[
                pltpu.VMEM((count, width), BF),
                pltpu.VMEM((count, width), BF),
                pltpu.VMEM((width, hidden), BF),
                pltpu.VMEM((width, hidden), BF),
                pltpu.VMEM((hidden, width), BF),
                pltpu.VMEM((count, 1), F32),
                pltpu.SemaphoreType.DMA((2 * n + 6 * (hidden // 128),)),
            ],
            compiler_params=params(),
            cost_estimate=cost(10 * count * hidden * width, 6 * hidden * width),
            name="expert",
        )(info, *arrived, *weights)

    def cross(arrays):
        return [arrays[0]] + [
            lax.ppermute(arrays[d], "expert", plan.across(d)) for d in range(1, inner)
        ]

    got, done = [], 1
    for c in range(PARTS):
        for r in range(done + 1, plan.steps[c] + 1):
            blocks[r] = lax.ppermute(blocks[r - 1], "expert", plan.line(1))
            blocks[outer - 1 + r] = lax.ppermute(blocks[outer - 2 + r], "expert", plan.line(-1))
        done = max(done, plan.steps[c])
        sent = compact(c)
        if c == 0:
            others, sent = lax.optimization_barrier((others, sent))
        else:
            got[-1], sent = lax.optimization_barrier((got[-1], sent))
        got.append(cross(sent))
    weights = []
    for w, other in zip((w_gate, w_up, w_down), others):
        weights += [w, other]
    outs = expert(0, sum(got[:-1], []))
    late = got[-1]
    outs, late = lax.optimization_barrier((outs, late))
    got[-1] = late
    backs = cross(outs[3:])
    more = expert(1, late)
    got = sum(got, [])
    mids = outs[:3] + more[:3]

    count = inner * sum(plan.rows)

    def weight_grads(own, extra):
        return pl.pallas_call(
            functools.partial(weight_kernel, plan, own),
            out_shape=[
                shape((1, width, part), BF),
                shape((1, width, part), BF),
                shape((1, part, width), BF),
            ],
            in_specs=[ANY] * (inner * PARTS + 6) + [VMEM] * len(extra),
            out_specs=[VMEM] * 3,
            scratch_shapes=[
                pltpu.VMEM((count, width), BF),
                pltpu.VMEM((count, width), BF),
                pltpu.VMEM((count, part), BF),
                pltpu.VMEM((count, 2 * part), BF),
                pltpu.SemaphoreType.DMA((2 * inner * PARTS,)),
                pltpu.SemaphoreType.DMA((6,)),
            ],
            compiler_params=params(),
            cost_estimate=cost(6 * count * part * width, 4 * count * (width + hidden)),
            name="weight_grads",
        )(*got, *mids, *extra)

    def spread(homes, groups, extra):
        slots = inner * sum(plan.sizes[:groups])
        return pl.pallas_call(
            functools.partial(spread_kernel, plan, homes, groups),
            out_shape=[shape((tok, width + LANES), BF)] * len(homes),
            in_specs=[SMEM, VMEM] + [ANY] * (plan.cands + groups * inner + len(extra)),
            out_specs=[VMEM] * len(homes),
            scratch_shapes=[
                pltpu.VMEM((slots, width + LANES), BF),
                pltpu.VMEM((plan.cands, tok, LANES), BF),
                pltpu.VMEM((len(homes) * tok, slots), BF),
                pltpu.SemaphoreType.DMA((groups * inner,)),
                pltpu.SemaphoreType.DMA((plan.cands,)),
            ],
            compiler_params=params(),
            cost_estimate=cost(2 * len(homes) * tok * slots * width, 2 * slots * width),
            name="spread",
        )(
            info,
            jnp.asarray(plan.keys(plan.spans[:groups])),
            *blocks,
            *backs[: groups * inner],
            *extra,
        )

    mine = weight_grads(False, [])
    backs, more, mine = lax.optimization_barrier((backs, more, mine))
    backs = backs + cross(more[3:])
    (first,) = spread([1], 1, [])
    sums = {}
    mine, backs, first = lax.optimization_barrier((mine, backs, first))
    came = [lax.ppermute(first, "expert", plan.flip(1))]
    theirs = [lax.ppermute(w, "dp", swap) for w in mine]
    rest = [r for r in range(outer) if r != 1]
    sums.update(zip(rest, spread(rest, 2, [mine[0], first])))
    bit = 1
    while bit < outer:
        for r in range(bit, outer, 2 * bit):
            if r == 1:
                continue
            sent = lax.ppermute(sums[r], "expert", plan.flip(bit))
            if r == bit:
                came.append(sent)
            else:
                sums[r - bit] = pl.pallas_call(
                    add_kernel,
                    out_shape=shape((tok, width + LANES), BF),
                    in_specs=[VMEM] * 2,
                    out_specs=VMEM,
                    name="add",
                )(sums[r - bit], sent)
        bit *= 2
    grads = weight_grads(True, theirs)
    home = [sums[0]] + came
    grad_tokens, grad_combine = pl.pallas_call(
        functools.partial(home_kernel, plan, len(home)),
        out_shape=[shape((tok, width), BF), shape((plan.top, tok), BF)],
        in_specs=[VMEM] * (len(home) + 2) + [ANY],
        out_specs=[VMEM] * 2,
        compiler_params=params(),
        cost_estimate=cost(1e6, 2 * tok * width * (outer + 1)),
        name="home",
    )(*home, routes.T, combine.T, grads[0])
    return (grad_tokens, grad_combine.T, *grads)


def solution(mesh):
    rows = P(("parts", "dp", "expert"), None)
    in_specs = (rows,) * 4 + (P("expert", None, "dp"),) * 2 + (P("expert", "dp", None),)
    out_specs = (rows,) * 2 + (P(("parts", "expert"), None, "dp"),) * 2
    out_specs += (P(("parts", "expert"), "dp", None),)
    shape = dict(mesh.shape)

    def whole(tokens, routes, combine, upstream, w_gate, w_up, w_down):
        devices = shape["parts"] * shape["dp"] * shape["expert"]
        plan = Plan(
            shape["expert"],
            tokens.shape[0] // devices,
            routes.shape[1],
            tokens.shape[1],
            w_gate.shape[2],
        )
        body = functools.partial(on_device, plan)
        return jax.shard_map(
            body, mesh=mesh, in_specs=in_specs, out_specs=out_specs, check_vma=False
        )(tokens, routes, combine, upstream, w_gate, w_up, w_down)

    return whole
```

```python
import functools

import jax
import jax.numpy as jnp
import numpy as np
from jax import lax
from jax.experimental import pallas as pl
from jax.experimental.pallas import tpu as pltpu
from jax.sharding import PartitionSpec as P

BF = jnp.bfloat16
F32 = jnp.float32
LANES = 128
HALF = 64
STRIDE = 1024
PARTS = 4
NOWHERE = -(1 << 20)
ANY = pl.BlockSpec(memory_space=pltpu.HBM)
VMEM = pl.BlockSpec(memory_space=pltpu.VMEM)
SMEM = pl.BlockSpec(memory_space=pltpu.SMEM)
TN = (((0,), (0,)), ((), ()))
NT = (((1,), (1,)), ((), ()))


def params(megabytes=60):
    return pltpu.CompilerParams(vmem_limit_bytes=megabytes << 20)


def cost(flops, moved):
    return pl.CostEstimate(flops=int(flops), bytes_accessed=int(moved), transcendentals=0)


class Plan:
    def __init__(self, experts, tok, top, width, hidden):
        self.experts, self.tok, self.top = experts, tok, top
        self.width, self.hidden = width, hidden
        outer = 1
        while outer * outer < experts:
            outer *= 2
        self.outer, self.inner = outer, experts // outer
        mean = tok * top // experts
        self.cap = min(tok, max(2, mean + tok * top // (8 * experts)))
        total = -(-self.outer * self.cap // 16) * 16
        step = self.outer // PARTS
        marks = [k * step * self.cap // 16 * 16 for k in range(PARTS)] + [total]
        self.chunks = [(marks[k], marks[k + 1]) for k in range(PARTS)]
        self.rows = [b - a for a, b in self.chunks]
        self.steps = [(k + 1) * step - 1 for k in range(PARTS)]
        self.groups = [range(PARTS - 1), range(PARTS - 1, PARTS)]
        self.spans = [(marks[g[0]], marks[g[-1] + 1]) for g in self.groups]
        self.sizes = [b - a for a, b in self.spans]
        self.cands = 2 * self.outer - 1
        self.use = [self.used(*c) for c in self.chunks]
        needed = set().union(*self.use)
        self.last = [
            max(i for i in needed if 0 < i < outer),
            max(i for i in needed if i >= outer) - outer + 1,
        ]

    def keys(self, spans):
        return np.array(
            [[d * STRIDE + q for a, b in spans for d in range(self.inner) for q in range(a, b)]],
            np.int32,
        )

    def order(self, z):
        rest = [s for s in range(self.outer) if s not in (z, z ^ 1)]
        return [z, z ^ 1] + sorted(rest, key=lambda s: abs(s - z))

    def swap(self, z, odd):
        to = z - 1 if (z % 2 == 0) == odd else z + 1
        return to if 0 <= to < self.outer else z

    def trace(self):
        held = {0: list(range(self.outer))}
        for chain in (0, 1):
            last = held[0]
            for r in range(1, self.outer):
                odd = (r % 2 == 0) == (chain == 0)
                last = [last[self.swap(z, odd)] for z in range(self.outer)]
                held[chain * (self.outer - 1) + r] = last
        return held

    def cand(self, z, source):
        step = lambda i: i if i < self.outer else i - self.outer + 1
        found = [i for i, held in self.trace().items() if held[z] == source]
        return min(found, key=lambda i: (step(i), i))

    def exchange(self, r, chain):
        odd = (r % 2 == 0) == (chain == 0)
        return [
            (z * self.inner + p, self.swap(z, odd) * self.inner + p)
            for z in range(self.outer)
            for p in range(self.inner)
        ]

    def used(self, a, b):
        slots = [k for k in range(self.outer) if k * self.cap < b and (k + 1) * self.cap > a]
        return sorted(
            {self.cand(z, self.order(z)[k]) for z in range(self.outer) for k in slots}
        )

    def partner(self, p, d):
        return p ^ d if self.inner & (self.inner - 1) == 0 else (d - p) % self.inner

    def table(self):
        rows = []
        for e in range(self.experts):
            z, p = divmod(e, self.inner)
            offs = [NOWHERE] * self.cands
            for slot, source in enumerate(self.order(z)):
                offs[self.cand(z, source)] = slot * self.cap
            experts = [z * self.inner + self.partner(p, d) for d in range(self.inner)]
            homes = [self.cand(z, z ^ r) for r in range(self.outer)]
            rows.append(offs + experts + homes)
        return np.array(rows, np.int32)

    def across(self, d):
        return [
            (z * self.inner + p, z * self.inner + self.partner(p, d))
            for z in range(self.outer)
            for p in range(self.inner)
        ]

    def flip(self, r):
        return [
            (z * self.inner + p, (z ^ r) * self.inner + p)
            for z in range(self.outer)
            for p in range(self.inner)
        ]


def pack_kernel(plan, tok_ref, up_ref, routes_ref, comb_ref, out_ref):
    tok, width = plan.tok, plan.width
    out_ref[:, :width] = tok_ref[...]
    out_ref[:, width : 2 * width] = up_ref[...]
    kind = lax.broadcasted_iota(jnp.int32, (LANES, tok), 0)
    weight = jnp.zeros((LANES, tok), F32)
    named = jnp.zeros((LANES, tok), F32)
    comb = comb_ref[...].astype(F32)
    for k in range(plan.top):
        e = routes_ref[k : k + 1, :]
        weight = jnp.where(kind == e, comb[k : k + 1, :], weight)
        named = jnp.where(kind == e + HALF, 1.0, named)
    row = lax.broadcasted_iota(jnp.int32, (tok, tok), 0)
    col = lax.broadcasted_iota(jnp.int32, (tok, tok), 1)
    upto = jnp.where(row <= col, 1.0, 0.0).astype(BF)
    count = jnp.dot(named.astype(BF), upto, preferred_element_type=F32)
    table = (weight + count * named).astype(BF)
    same = jnp.where(row == col, 1.0, 0.0).astype(BF)
    turned = lax.dot_general(same, table, NT, preferred_element_type=F32)
    out_ref[:, 2 * width :] = turned.astype(BF)


def picks(plan, meta, off, experts, key, scaled):
    tok = meta.shape[0]
    lane = lax.broadcasted_iota(jnp.int32, (tok, LANES), 1)
    one = jnp.zeros((tok, key.shape[1]), F32)
    two = jnp.zeros((tok, key.shape[1]), F32)
    for d, e in enumerate(experts):
        place = jnp.sum(jnp.where(lane == e + HALF, meta, 0.0), axis=1, keepdims=True)
        place = place.astype(jnp.int32)
        spot = jnp.where(place > 0, place - 1 + off + d * STRIDE, -1)
        hit = spot == key
        one = jnp.where(hit, 1.0, one)
        if scaled:
            weight = jnp.sum(jnp.where(lane == e, meta, 0.0), axis=1, keepdims=True)
            two = jnp.where(hit, weight, two)
    return one, two


def compact_kernel(plan, chunk, *refs):
    use, rows = plan.use[chunk], plan.rows[chunk]
    n, width, tok, inner = len(use), plan.width, plan.tok, plan.inner
    info, key_ref = refs[:2]
    blocks, outs = refs[2 : 2 + n], refs[2 + n : 2 + n + inner]
    held, one_s, two_s, sems = refs[2 + n + inner :]
    copies = [
        pltpu.make_async_copy(b, held.at[pl.ds(i * tok, tok)], sems.at[i])
        for i, b in enumerate(blocks)
    ]
    for c in copies:
        c.start()
    experts = [info[plan.cands + d] for d in range(inner)]
    for i, c in enumerate(copies):
        c.wait()
        meta = held[i * tok : (i + 1) * tok, 2 * width :].astype(F32)
        one, two = picks(plan, meta, info[use[i]], experts, key_ref[...], True)
        one_s[i * tok : (i + 1) * tok, :] = one.astype(BF)
        two_s[i * tok : (i + 1) * tok, :] = two.astype(BF)
    for part, source in ((0, one_s), (1, two_s)):
        have = held[:, part * width : (part + 1) * width]
        found = lax.dot_general(source[...], have, TN, preferred_element_type=F32).astype(BF)
        for d in range(inner):
            outs[d][part * rows : (part + 1) * rows, :] = found[d * rows : (d + 1) * rows]


def pieces(plan, group, got, x_s, d_s, sems, base=0):
    inner, size, first = plan.inner, plan.sizes[group], plan.spans[group][0]
    x_copies, d_copies = [], []
    for i, g in enumerate(got):
        c, d = plan.groups[group][i // inner], i % inner
        rows = plan.rows[c]
        to = pl.ds(base + d * size + plan.chunks[c][0] - first, rows)
        x_copies.append(pltpu.make_async_copy(g.at[pl.ds(0, rows)], x_s.at[to], sems.at[2 * i]))
        d_copies.append(
            pltpu.make_async_copy(g.at[pl.ds(rows, rows)], d_s.at[to], sems.at[2 * i + 1])
        )
    return x_copies, d_copies


def expert_kernel(plan, group, *refs):
    inner, rows, width, hidden = plan.inner, plan.sizes[group], plan.width, plan.hidden
    part, count, n = hidden // 2, inner * rows, inner * len(plan.groups[group])
    info = refs[0]
    got, weights = refs[1 : 1 + n], refs[1 + n : 7 + n]
    hid_o, gate_o, up_o = refs[7 + n : 10 + n]
    backs = refs[10 + n : 10 + n + inner]
    x_s, d_s, wg_s, wu_s, wd_s, comb_s, sems = refs[10 + n + inner :]
    x_copies, d_copies = pieces(plan, group, got, x_s, d_s, sems)
    tile, tiles = hidden, []
    for t in range(hidden // tile):
        for kind, where in ((0, wg_s), (1, wu_s), (2, wd_s)):
            at, here = t * tile, []
            while at < (t + 1) * tile:
                half, start = divmod(at, part)
                size = min((t + 1) * tile, (half + 1) * part) - at
                source, to = pl.ds(start, size), pl.ds(at, size)
                w = weights[2 * kind + half].at[0]
                here.append((w.at[source], where.at[to]) if kind == 2 else (w.at[:, source], where.at[:, to]))
                at += size
            tiles.append(here)
    w_copies, used = [], 2 * n
    for here in tiles:
        w_copies.append([])
        for source, to in here:
            w_copies[-1].append(pltpu.make_async_copy(source, to, sems.at[used]))
            used += 1
    for c in x_copies + w_copies[0] + w_copies[1] + d_copies:
        c.start()
    for here in w_copies[2:]:
        for c in here:
            c.start()
    for t in range(hidden // tile):
        at = slice(t * tile, (t + 1) * tile)
        gate_w, up_w, down_w = w_copies[3 * t : 3 * t + 3]
        for c in (x_copies if t == 0 else []) + gate_w:
            c.wait()
        gate = jnp.dot(x_s[...], wg_s[:, at], preferred_element_type=F32)
        for c in up_w:
            c.wait()
        up = jnp.dot(x_s[...], wu_s[:, at], preferred_element_type=F32)
        for c in (d_copies if t == 0 else []) + down_w:
            c.wait()
        mixed = lax.dot_general(d_s[...], wd_s[at, :], NT, preferred_element_type=F32)
        logistic = jax.nn.sigmoid(gate)
        silu = gate * logistic
        hid = (silu * up).astype(BF)
        hid_o[:, at] = hid
        comb = jnp.sum(hid.astype(F32) * mixed, axis=1, keepdims=True)
        comb_s[...] = comb if t == 0 else comb_s[...] + comb
        gate_o[:, at] = (mixed * up * logistic * (1.0 + gate * (1.0 - logistic))).astype(BF)
        up_o[:, at] = (mixed * silu).astype(BF)

    wide = width // 2

    @pl.loop(0, width // wide)
    def _(j):
        at = pl.ds(pl.multiple_of(j * wide, wide), wide)
        back = lax.dot_general(gate_o[...], wg_s[at, :], NT, preferred_element_type=F32)
        back += lax.dot_general(up_o[...], wu_s[at, :], NT, preferred_element_type=F32)
        back = back.astype(BF)
        for d in range(inner):
            backs[d][:, at] = back[d * rows : (d + 1) * rows]

    lane = lax.broadcasted_iota(jnp.int32, (count, LANES), 1)
    comb = jnp.where(lane == info[plan.cands], comb_s[...], 0.0).astype(BF)
    for d in range(inner):
        backs[d][:, width:] = comb[d * rows : (d + 1) * rows]


def weight_kernel(plan, own, *refs):
    inner, width, hidden = plan.inner, plan.width, plan.hidden
    part, n = hidden // 2, plan.inner * PARTS
    got, mids = refs[:n], refs[n : n + 6]
    at = n + 6
    theirs = refs[at : at + 3] if own else None
    at += 3 if own else 0
    g_o, u_o, d_o = refs[at : at + 3]
    x_s, d_s, h_s, gu_s, sems, mid_sems = refs[at + 3 :]
    everything, base, taken = [], 0, 0
    half = pl.ds(0 if own else part, part)
    for g in range(2):
        many = inner * len(plan.groups[g])
        mine = got[taken : taken + many]
        at_sems = sems.at[pl.ds(2 * taken, 2 * many)]
        x_copies, d_copies = pieces(plan, g, mine, x_s, d_s, at_sems, base)
        everything += x_copies + d_copies
        to = pl.ds(base, inner * plan.sizes[g])
        spots = (h_s.at[to], gu_s.at[to, pl.ds(0, part)], gu_s.at[to, pl.ds(part, part)])
        for i, (m, s) in enumerate(zip(mids[3 * g : 3 * g + 3], spots)):
            everything.append(
                pltpu.make_async_copy(m.at[:, half], s, mid_sems.at[3 * g + i])
            )
        taken += many
        base += inner * plan.sizes[g]
    for c in everything:
        c.start()
    for c in everything:
        c.wait()
    tile = width // 2

    @pl.loop(0, width // tile)
    def _(j):
        to = pl.ds(pl.multiple_of(j * tile, tile), tile)
        both = lax.dot_general(x_s[:, to], gu_s[...], TN, preferred_element_type=F32)
        first, second = both[:, :part], both[:, part:]
        if own:
            first += theirs[0][0, to, :].astype(F32)
            second += theirs[1][0, to, :].astype(F32)
        g_o[0, to, :] = first.astype(BF)
        u_o[0, to, :] = second.astype(BF)

    down = lax.dot_general(h_s[...], d_s[...], TN, preferred_element_type=F32)
    if own:
        down += theirs[2][0].astype(F32)
    d_o[0] = down.astype(BF)


def spread_kernel(plan, homes, groups, *refs):
    inner, tok, width = plan.inner, plan.tok, plan.width
    info, key_ref = refs[:2]
    blocks = refs[2 : 2 + plan.cands]
    at = 2 + plan.cands
    backs = refs[at : at + groups * inner]
    outs = refs[-5 - len(homes) : -5]
    held, metas, pick_s, sems, meta_sems = refs[-5:]
    copies, later, start = [], [], 0
    for i, b in enumerate(blocks):
        copies.append(
            pltpu.make_async_copy(b.at[:, pl.ds(2 * width, LANES)], metas.at[i], meta_sems.at[i])
        )
    for i, b in enumerate(backs):
        rows = plan.sizes[i // inner]
        later.append(pltpu.make_async_copy(b, held.at[pl.ds(start, rows)], sems.at[i]))
        start += rows
    for c in copies + later:
        c.start()
    for c in copies:
        c.wait()
    experts = [info[plan.cands + d] for d in range(inner)]
    for i, r in enumerate(homes):
        which = info[plan.cands + inner + r]
        meta = metas[which].astype(F32)
        one, _ = picks(plan, meta, info[which], experts, key_ref[...], False)
        pick_s[i * tok : (i + 1) * tok, :] = one.astype(BF)
    for c in later:
        c.wait()
    sums = jnp.dot(pick_s[...], held[...], preferred_element_type=F32).astype(BF)
    for i in range(len(homes)):
        outs[i][...] = sums[i * tok : (i + 1) * tok]


def add_kernel(a_ref, b_ref, o_ref):
    o_ref[...] = (a_ref[...].astype(F32) + b_ref[...].astype(F32)).astype(BF)


def home_kernel(plan, count, *refs):
    parts = refs[:count]
    routes_ref, comb_ref, _, tok_o, comb_o = refs[count:]
    width, tok = plan.width, plan.tok
    total = parts[0][...].astype(F32)
    for p in parts[1:]:
        total += p[...].astype(F32)
    tok_o[...] = total[:, :width].astype(BF)
    row = lax.broadcasted_iota(jnp.int32, (LANES, LANES), 0)
    col = lax.broadcasted_iota(jnp.int32, (LANES, LANES), 1)
    same = jnp.where(row == col, 1.0, 0.0).astype(BF)
    found = total[:, width:].astype(BF)
    found = lax.dot_general(same, found, NT, preferred_element_type=F32)
    kind = lax.broadcasted_iota(jnp.int32, (LANES, tok), 0)
    out = []
    for k in range(plan.top):
        mine = jnp.where(kind == routes_ref[k : k + 1, :], found, 0.0)
        out.append(jnp.sum(mine, axis=0, keepdims=True))
    out = jnp.concatenate(out, axis=0)
    comb_o[...] = (out / comb_ref[...].astype(F32)).astype(BF)


def on_device(plan, tokens, routes, combine, upstream, w_gate, w_up, w_down):
    tok, width, hidden = plan.tok, plan.width, plan.hidden
    inner, outer, part = plan.inner, plan.outer, plan.hidden // 2
    full = 2 * width + LANES
    shape = jax.ShapeDtypeStruct
    info = jnp.asarray(plan.table())[lax.axis_index("expert")]
    swap = [(0, 1), (1, 0)]

    block = pl.pallas_call(
        functools.partial(pack_kernel, plan),
        out_shape=shape((tok, full), BF),
        in_specs=[VMEM] * 4,
        out_specs=VMEM,
        compiler_params=params(),
        cost_estimate=cost(1e6, 4 * tok * full),
        name="pack",
    )(tokens, upstream, routes.T, combine.T)

    others = [lax.ppermute(w, "dp", swap) for w in (w_gate, w_up, w_down)]
    blocks = [block] * plan.cands

    def hop(r):
        for chain in (0, 1):
            if r <= plan.last[chain]:
                i = chain * (outer - 1) + r
                before = block if r == 1 else blocks[i - 1]
                blocks[i] = lax.ppermute(before, "expert", plan.exchange(r, chain))

    hop(1)
    def compact(c):
        rows, use = plan.rows[c], plan.use[c]
        count, n = inner * rows, len(use)
        return pl.pallas_call(
            functools.partial(compact_kernel, plan, c),
            out_shape=[shape((2 * rows, width), BF)] * inner,
            in_specs=[SMEM, VMEM] + [ANY] * n,
            out_specs=[VMEM] * inner,
            scratch_shapes=[
                pltpu.VMEM((n * tok, full), BF),
                pltpu.VMEM((n * tok, count), BF),
                pltpu.VMEM((n * tok, count), BF),
                pltpu.SemaphoreType.DMA((n,)),
            ],
            compiler_params=params(),
            cost_estimate=cost(4 * n * tok * count * width, 2 * n * tok * full),
            name="compact",
        )(info, jnp.asarray(plan.keys([plan.chunks[c]])), *[blocks[i] for i in use])

    def expert(g, arrived):
        rows, n = plan.sizes[g], inner * len(plan.groups[g])
        count = inner * rows
        return pl.pallas_call(
            functools.partial(expert_kernel, plan, g),
            out_shape=[shape((count, hidden), BF)] * 3
            + [shape((rows, width + LANES), BF)] * inner,
            in_specs=[SMEM] + [ANY] * (n + 6),
            out_specs=[VMEM] * (3 + inner),
            scratch_shapes=[
                pltpu.VMEM((count, width), BF),
                pltpu.VMEM((count, width), BF),
                pltpu.VMEM((width, hidden), BF),
                pltpu.VMEM((width, hidden), BF),
                pltpu.VMEM((hidden, width), BF),
                pltpu.VMEM((count, 1), F32),
                pltpu.SemaphoreType.DMA((2 * n + 6 * (hidden // 128),)),
            ],
            compiler_params=params(),
            cost_estimate=cost(10 * count * hidden * width, 6 * hidden * width),
            name="expert",
        )(info, *arrived, *weights)

    def cross(arrays):
        return [arrays[0]] + [
            lax.ppermute(arrays[d], "expert", plan.across(d)) for d in range(1, inner)
        ]

    got, done = [], 1
    for c in range(PARTS):
        for r in range(done + 1, plan.steps[c] + 1):
            hop(r)
        done = max(done, plan.steps[c])
        sent = compact(c)
        if c == 0:
            others, sent = lax.optimization_barrier((others, sent))
            blocks[done], blocks[outer - 1 + done], sent = lax.optimization_barrier(
                (blocks[done], blocks[outer - 1 + done], sent)
            )
        else:
            got[-1], sent = lax.optimization_barrier((got[-1], sent))
        got.append(cross(sent))
    weights = []
    for w, other in zip((w_gate, w_up, w_down), others):
        weights += [w, other]
    outs = expert(0, sum(got[:-1], []))
    late = got[-1]
    outs, late = lax.optimization_barrier((outs, late))
    got[-1] = late
    backs = cross(outs[3:])
    more = expert(1, late)
    got = sum(got, [])
    mids = outs[:3] + more[:3]

    count = inner * sum(plan.rows)

    def weight_grads(own, extra):
        return pl.pallas_call(
            functools.partial(weight_kernel, plan, own),
            out_shape=[
                shape((1, width, part), BF),
                shape((1, width, part), BF),
                shape((1, part, width), BF),
            ],
            in_specs=[ANY] * (inner * PARTS + 6) + [VMEM] * len(extra),
            out_specs=[VMEM] * 3,
            scratch_shapes=[
                pltpu.VMEM((count, width), BF),
                pltpu.VMEM((count, width), BF),
                pltpu.VMEM((count, part), BF),
                pltpu.VMEM((count, 2 * part), BF),
                pltpu.SemaphoreType.DMA((2 * inner * PARTS,)),
                pltpu.SemaphoreType.DMA((6,)),
            ],
            compiler_params=params(),
            cost_estimate=cost(6 * count * part * width, 4 * count * (width + hidden)),
            name="weight_grads",
        )(*got, *mids, *extra)

    def spread(homes, groups, extra):
        slots = inner * sum(plan.sizes[:groups])
        return pl.pallas_call(
            functools.partial(spread_kernel, plan, homes, groups),
            out_shape=[shape((tok, width + LANES), BF)] * len(homes),
            in_specs=[SMEM, VMEM] + [ANY] * (plan.cands + groups * inner + len(extra)),
            out_specs=[VMEM] * len(homes),
            scratch_shapes=[
                pltpu.VMEM((slots, width + LANES), BF),
                pltpu.VMEM((plan.cands, tok, LANES), BF),
                pltpu.VMEM((len(homes) * tok, slots), BF),
                pltpu.SemaphoreType.DMA((groups * inner,)),
                pltpu.SemaphoreType.DMA((plan.cands,)),
            ],
            compiler_params=params(),
            cost_estimate=cost(2 * len(homes) * tok * slots * width, 2 * slots * width),
            name="spread",
        )(
            info,
            jnp.asarray(plan.keys(plan.spans[:groups])),
            *blocks,
            *backs[: groups * inner],
            *extra,
        )

    mine = weight_grads(False, [])
    backs = backs + cross(more[3:])
    (first,) = spread([1], 1, [])
    sums = {}
    mine, backs, first = lax.optimization_barrier((mine, backs, first))
    came = [lax.ppermute(first, "expert", plan.flip(1))]
    theirs = [lax.ppermute(w, "dp", swap) for w in mine]
    rest = [r for r in range(outer) if r != 1]
    sums.update(zip(rest, spread(rest, 2, [mine[0], first])))
    bit = 1
    while bit < outer:
        for r in range(bit, outer, 2 * bit):
            if r == 1:
                continue
            sent = lax.ppermute(sums[r], "expert", plan.flip(bit))
            if r == bit:
                came.append(sent)
            else:
                sums[r - bit] = pl.pallas_call(
                    add_kernel,
                    out_shape=shape((tok, width + LANES), BF),
                    in_specs=[VMEM] * 2,
                    out_specs=VMEM,
                    name="add",
                )(sums[r - bit], sent)
        bit *= 2
    grads = weight_grads(True, theirs)
    home = [sums[0]] + came
    grad_tokens, grad_combine = pl.pallas_call(
        functools.partial(home_kernel, plan, len(home)),
        out_shape=[shape((tok, width), BF), shape((plan.top, tok), BF)],
        in_specs=[VMEM] * (len(home) + 2) + [ANY],
        out_specs=[VMEM] * 2,
        compiler_params=params(),
        cost_estimate=cost(1e6, 2 * tok * width * (outer + 1)),
        name="home",
    )(*home, routes.T, combine.T, grads[0])
    return (grad_tokens, grad_combine.T, *grads)


def solution(mesh):
    rows = P(("parts", "dp", "expert"), None)
    in_specs = (rows,) * 4 + (P("expert", None, "dp"),) * 2 + (P("expert", "dp", None),)
    out_specs = (rows,) * 2 + (P(("parts", "expert"), None, "dp"),) * 2
    out_specs += (P(("parts", "expert"), "dp", None),)
    shape = dict(mesh.shape)

    def whole(tokens, routes, combine, upstream, w_gate, w_up, w_down):
        devices = shape["parts"] * shape["dp"] * shape["expert"]
        plan = Plan(
            shape["expert"],
            tokens.shape[0] // devices,
            routes.shape[1],
            tokens.shape[1],
            w_gate.shape[2],
        )
        body = functools.partial(on_device, plan)
        return jax.shard_map(
            body, mesh=mesh, in_specs=in_specs, out_specs=out_specs, check_vma=False
        )(tokens, routes, combine, upstream, w_gate, w_up, w_down)

    return whole
```

```python
import functools

import jax
import jax.numpy as jnp
import numpy as np
from jax import lax
from jax.experimental import pallas as pl
from jax.experimental.pallas import tpu as pltpu
from jax.sharding import PartitionSpec as P

BF = jnp.bfloat16
F32 = jnp.float32
LANES = 128
HALF = 64
STRIDE = 1024
PARTS = 4
NOWHERE = -(1 << 20)
ANY = pl.BlockSpec(memory_space=pltpu.HBM)
VMEM = pl.BlockSpec(memory_space=pltpu.VMEM)
SMEM = pl.BlockSpec(memory_space=pltpu.SMEM)
TN = (((0,), (0,)), ((), ()))
NT = (((1,), (1,)), ((), ()))


def params(megabytes=60):
    return pltpu.CompilerParams(vmem_limit_bytes=megabytes << 20)


def cost(flops, moved):
    return pl.CostEstimate(flops=int(flops), bytes_accessed=int(moved), transcendentals=0)


class Plan:
    def __init__(self, experts, tok, top, width, hidden):
        self.experts, self.tok, self.top = experts, tok, top
        self.width, self.hidden = width, hidden
        outer = 1
        while outer * outer < experts:
            outer *= 2
        self.outer, self.inner = outer, experts // outer
        mean = tok * top // experts
        self.cap = min(tok, max(2, mean + tok * top // (8 * experts)))
        total = -(-self.outer * self.cap // 16) * 16
        step = self.outer // PARTS
        marks = [k * step * self.cap // 16 * 16 for k in range(PARTS)] + [total]
        if marks[1] >= 32:
            marks[1] = marks[1] // 32 * 16
        self.chunks = [(marks[k], marks[k + 1]) for k in range(PARTS)]
        self.rows = [b - a for a, b in self.chunks]
        self.steps = [(k + 1) * step - 1 for k in range(PARTS)]
        self.groups = [range(PARTS - 1), range(PARTS - 1, PARTS)]
        self.spans = [(marks[g[0]], marks[g[-1] + 1]) for g in self.groups]
        self.sizes = [b - a for a, b in self.spans]
        self.cands = 2 * self.outer - 1
        self.use = [self.used(*c) for c in self.chunks]
        needed = set().union(*self.use)
        self.last = [
            max(i for i in needed if 0 < i < outer),
            max(i for i in needed if i >= outer) - outer + 1,
        ]

    def keys(self, spans):
        return np.array(
            [[d * STRIDE + q for a, b in spans for d in range(self.inner) for q in range(a, b)]],
            np.int32,
        )

    def order(self, z):
        rest = [s for s in range(self.outer) if s not in (z, z ^ 1)]
        return [z, z ^ 1] + sorted(rest, key=lambda s: abs(s - z))

    def swap(self, z, odd):
        to = z - 1 if (z % 2 == 0) == odd else z + 1
        return to if 0 <= to < self.outer else z

    def trace(self):
        held = {0: list(range(self.outer))}
        for chain in (0, 1):
            last = held[0]
            for r in range(1, self.outer):
                odd = (r % 2 == 0) == (chain == 0)
                last = [last[self.swap(z, odd)] for z in range(self.outer)]
                held[chain * (self.outer - 1) + r] = last
        return held

    def cand(self, z, source):
        step = lambda i: i if i < self.outer else i - self.outer + 1
        found = [i for i, held in self.trace().items() if held[z] == source]
        return min(found, key=lambda i: (step(i), i))

    def exchange(self, r, chain):
        odd = (r % 2 == 0) == (chain == 0)
        return [
            (z * self.inner + p, self.swap(z, odd) * self.inner + p)
            for z in range(self.outer)
            for p in range(self.inner)
        ]

    def used(self, a, b):
        slots = [k for k in range(self.outer) if k * self.cap < b and (k + 1) * self.cap > a]
        return sorted(
            {self.cand(z, self.order(z)[k]) for z in range(self.outer) for k in slots}
        )

    def partner(self, p, d):
        return p ^ d if self.inner & (self.inner - 1) == 0 else (d - p) % self.inner

    def table(self):
        rows = []
        for e in range(self.experts):
            z, p = divmod(e, self.inner)
            offs = [NOWHERE] * self.cands
            for slot, source in enumerate(self.order(z)):
                offs[self.cand(z, source)] = slot * self.cap
            experts = [z * self.inner + self.partner(p, d) for d in range(self.inner)]
            homes = [self.cand(z, z ^ r) for r in range(self.outer)]
            rows.append(offs + experts + homes)
        return np.array(rows, np.int32)

    def across(self, d):
        return [
            (z * self.inner + p, z * self.inner + self.partner(p, d))
            for z in range(self.outer)
            for p in range(self.inner)
        ]

    def flip(self, r):
        return [
            (z * self.inner + p, (z ^ r) * self.inner + p)
            for z in range(self.outer)
            for p in range(self.inner)
        ]


def pack_kernel(plan, tok_ref, up_ref, routes_ref, comb_ref, out_ref):
    tok, width = plan.tok, plan.width
    out_ref[:, :width] = tok_ref[...]
    out_ref[:, width : 2 * width] = up_ref[...]
    kind = lax.broadcasted_iota(jnp.int32, (LANES, tok), 0)
    weight = jnp.zeros((LANES, tok), F32)
    named = jnp.zeros((LANES, tok), F32)
    comb = comb_ref[...].astype(F32)
    for k in range(plan.top):
        e = routes_ref[k : k + 1, :]
        weight = jnp.where(kind == e, comb[k : k + 1, :], weight)
        named = jnp.where(kind == e + HALF, 1.0, named)
    row = lax.broadcasted_iota(jnp.int32, (tok, tok), 0)
    col = lax.broadcasted_iota(jnp.int32, (tok, tok), 1)
    upto = jnp.where(row <= col, 1.0, 0.0).astype(BF)
    count = jnp.dot(named.astype(BF), upto, preferred_element_type=F32)
    table = (weight + count * named).astype(BF)
    same = jnp.where(row == col, 1.0, 0.0).astype(BF)
    turned = lax.dot_general(same, table, NT, preferred_element_type=F32)
    out_ref[:, 2 * width :] = turned.astype(BF)


def picks(plan, meta, off, experts, key, scaled):
    tok = meta.shape[0]
    lane = lax.broadcasted_iota(jnp.int32, (tok, LANES), 1)
    one = jnp.zeros((tok, key.shape[1]), F32)
    two = jnp.zeros((tok, key.shape[1]), F32)
    for d, e in enumerate(experts):
        place = jnp.sum(jnp.where(lane == e + HALF, meta, 0.0), axis=1, keepdims=True)
        place = place.astype(jnp.int32)
        spot = jnp.where(place > 0, place - 1 + off + d * STRIDE, -1)
        hit = spot == key
        one = jnp.where(hit, 1.0, one)
        if scaled:
            weight = jnp.sum(jnp.where(lane == e, meta, 0.0), axis=1, keepdims=True)
            two = jnp.where(hit, weight, two)
    return one, two


def compact_kernel(plan, chunk, *refs):
    use, rows = plan.use[chunk], plan.rows[chunk]
    n, width, tok, inner = len(use), plan.width, plan.tok, plan.inner
    info, key_ref = refs[:2]
    blocks, outs = refs[2 : 2 + n], refs[2 + n : 2 + n + inner]
    held, one_s, two_s, sems = refs[2 + n + inner :]
    copies = [
        pltpu.make_async_copy(b, held.at[pl.ds(i * tok, tok)], sems.at[i])
        for i, b in enumerate(blocks)
    ]
    for c in copies:
        c.start()
    experts = [info[plan.cands + d] for d in range(inner)]
    for i, c in enumerate(copies):
        c.wait()
        meta = held[i * tok : (i + 1) * tok, 2 * width :].astype(F32)
        one, two = picks(plan, meta, info[use[i]], experts, key_ref[...], True)
        one_s[i * tok : (i + 1) * tok, :] = one.astype(BF)
        two_s[i * tok : (i + 1) * tok, :] = two.astype(BF)
    for part, source in ((0, one_s), (1, two_s)):
        have = held[:, part * width : (part + 1) * width]
        found = lax.dot_general(source[...], have, TN, preferred_element_type=F32).astype(BF)
        for d in range(inner):
            outs[d][part * rows : (part + 1) * rows, :] = found[d * rows : (d + 1) * rows]


def pieces(plan, group, got, x_s, d_s, sems, base=0):
    inner, size, first = plan.inner, plan.sizes[group], plan.spans[group][0]
    x_copies, d_copies = [], []
    for i, g in enumerate(got):
        c, d = plan.groups[group][i // inner], i % inner
        rows = plan.rows[c]
        to = pl.ds(base + d * size + plan.chunks[c][0] - first, rows)
        x_copies.append(pltpu.make_async_copy(g.at[pl.ds(0, rows)], x_s.at[to], sems.at[2 * i]))
        d_copies.append(
            pltpu.make_async_copy(g.at[pl.ds(rows, rows)], d_s.at[to], sems.at[2 * i + 1])
        )
    return x_copies, d_copies


def expert_kernel(plan, group, *refs):
    inner, rows, width, hidden = plan.inner, plan.sizes[group], plan.width, plan.hidden
    part, count, n = hidden // 2, inner * rows, inner * len(plan.groups[group])
    info = refs[0]
    got, weights = refs[1 : 1 + n], refs[1 + n : 6 + n]
    hid_o, gate_o, up_o = refs[6 + n : 9 + n]
    backs = refs[9 + n : 9 + n + inner]
    x_s, d_s, wg_s, wu_s, wd_s, comb_s, sems = refs[9 + n + inner :]
    own_g, own_u, own_d, both, other_d = [w.at[0] for w in weights]
    views = [
        (own_g, both.at[:, pl.ds(0, part)]),
        (own_u, both.at[:, pl.ds(part, part)]),
        (own_d, other_d),
    ]
    x_copies, d_copies = pieces(plan, group, got, x_s, d_s, sems)
    tile, tiles = hidden, []
    for t in range(hidden // tile):
        for kind, where in ((0, wg_s), (1, wu_s), (2, wd_s)):
            at, here = t * tile, []
            while at < (t + 1) * tile:
                half, start = divmod(at, part)
                size = min((t + 1) * tile, (half + 1) * part) - at
                source, to = pl.ds(start, size), pl.ds(at, size)
                w = views[kind][half]
                here.append((w.at[source], where.at[to]) if kind == 2 else (w.at[:, source], where.at[:, to]))
                at += size
            tiles.append(here)
    w_copies, used = [], 2 * n
    for here in tiles:
        w_copies.append([])
        for source, to in here:
            w_copies[-1].append(pltpu.make_async_copy(source, to, sems.at[used]))
            used += 1
    for c in x_copies + w_copies[0] + w_copies[1] + d_copies:
        c.start()
    for here in w_copies[2:]:
        for c in here:
            c.start()
    for t in range(hidden // tile):
        at = slice(t * tile, (t + 1) * tile)
        gate_w, up_w, down_w = w_copies[3 * t : 3 * t + 3]
        for c in (x_copies if t == 0 else []) + gate_w:
            c.wait()
        gate = jnp.dot(x_s[...], wg_s[:, at], preferred_element_type=F32)
        for c in up_w:
            c.wait()
        up = jnp.dot(x_s[...], wu_s[:, at], preferred_element_type=F32)
        for c in (d_copies if t == 0 else []) + down_w:
            c.wait()
        mixed = lax.dot_general(d_s[...], wd_s[at, :], NT, preferred_element_type=F32)
        logistic = jax.nn.sigmoid(gate)
        silu = gate * logistic
        hid = (silu * up).astype(BF)
        hid_o[:, at] = hid
        comb = jnp.sum(hid.astype(F32) * mixed, axis=1, keepdims=True)
        comb_s[...] = comb if t == 0 else comb_s[...] + comb
        gate_o[:, at] = (mixed * up * logistic * (1.0 + gate * (1.0 - logistic))).astype(BF)
        up_o[:, at] = (mixed * silu).astype(BF)

    wide = width // 2

    @pl.loop(0, width // wide)
    def _(j):
        at = pl.ds(pl.multiple_of(j * wide, wide), wide)
        back = lax.dot_general(gate_o[...], wg_s[at, :], NT, preferred_element_type=F32)
        back += lax.dot_general(up_o[...], wu_s[at, :], NT, preferred_element_type=F32)
        back = back.astype(BF)
        for d in range(inner):
            backs[d][:, at] = back[d * rows : (d + 1) * rows]

    lane = lax.broadcasted_iota(jnp.int32, (count, LANES), 1)
    comb = jnp.where(lane == info[plan.cands], comb_s[...], 0.0).astype(BF)
    for d in range(inner):
        backs[d][:, width:] = comb[d * rows : (d + 1) * rows]


def weight_kernel(plan, own, *refs):
    inner, width, hidden = plan.inner, plan.width, plan.hidden
    part, n = hidden // 2, plan.inner * PARTS
    got, mids = refs[:n], refs[n : n + 6]
    at = n + 6
    theirs = refs[at : at + 3] if own else None
    at += 3 if own else 0
    g_o, u_o, d_o = refs[at : at + 3]
    x_s, d_s, h_s, gu_s, sems, mid_sems = refs[at + 3 :]
    everything, base, taken = [], 0, 0
    half = pl.ds(0 if own else part, part)
    for g in range(2):
        many = inner * len(plan.groups[g])
        mine = got[taken : taken + many]
        at_sems = sems.at[pl.ds(2 * taken, 2 * many)]
        x_copies, d_copies = pieces(plan, g, mine, x_s, d_s, at_sems, base)
        everything += x_copies + d_copies
        to = pl.ds(base, inner * plan.sizes[g])
        spots = (h_s.at[to], gu_s.at[to, pl.ds(0, part)], gu_s.at[to, pl.ds(part, part)])
        for i, (m, s) in enumerate(zip(mids[3 * g : 3 * g + 3], spots)):
            everything.append(
                pltpu.make_async_copy(m.at[:, half], s, mid_sems.at[3 * g + i])
            )
        taken += many
        base += inner * plan.sizes[g]
    for c in everything:
        c.start()
    for c in everything:
        c.wait()
    tile = width // 2

    @pl.loop(0, width // tile)
    def _(j):
        to = pl.ds(pl.multiple_of(j * tile, tile), tile)
        both = lax.dot_general(x_s[:, to], gu_s[...], TN, preferred_element_type=F32)
        first, second = both[:, :part], both[:, part:]
        if own:
            first += theirs[0][0, to, :].astype(F32)
            second += theirs[1][0, to, :].astype(F32)
        g_o[0, to, :] = first.astype(BF)
        u_o[0, to, :] = second.astype(BF)

    down = lax.dot_general(h_s[...], d_s[...], TN, preferred_element_type=F32)
    if own:
        down += theirs[2][0].astype(F32)
    d_o[0] = down.astype(BF)


def spread_kernel(plan, homes, groups, *refs):
    inner, tok, width = plan.inner, plan.tok, plan.width
    info, key_ref = refs[:2]
    blocks = refs[2 : 2 + plan.cands]
    at = 2 + plan.cands
    backs = refs[at : at + groups * inner]
    outs = refs[-5 - len(homes) : -5]
    held, metas, pick_s, sems, meta_sems = refs[-5:]
    copies, later, start = [], [], 0
    for i, b in enumerate(blocks):
        copies.append(
            pltpu.make_async_copy(b.at[:, pl.ds(2 * width, LANES)], metas.at[i], meta_sems.at[i])
        )
    for i, b in enumerate(backs):
        rows = plan.sizes[i // inner]
        later.append(pltpu.make_async_copy(b, held.at[pl.ds(start, rows)], sems.at[i]))
        start += rows
    for c in copies + later:
        c.start()
    for c in copies:
        c.wait()
    experts = [info[plan.cands + d] for d in range(inner)]
    for i, r in enumerate(homes):
        which = info[plan.cands + inner + r]
        meta = metas[which].astype(F32)
        one, _ = picks(plan, meta, info[which], experts, key_ref[...], False)
        pick_s[i * tok : (i + 1) * tok, :] = one.astype(BF)
    for c in later:
        c.wait()
    sums = jnp.dot(pick_s[...], held[...], preferred_element_type=F32).astype(BF)
    for i in range(len(homes)):
        outs[i][...] = sums[i * tok : (i + 1) * tok]


def add_kernel(a_ref, b_ref, o_ref):
    o_ref[...] = (a_ref[...].astype(F32) + b_ref[...].astype(F32)).astype(BF)


def home_kernel(plan, count, *refs):
    parts = refs[:count]
    routes_ref, comb_ref, _, tok_o, comb_o = refs[count:]
    width, tok = plan.width, plan.tok
    total = parts[0][...].astype(F32)
    for p in parts[1:]:
        total += p[...].astype(F32)
    tok_o[...] = total[:, :width].astype(BF)
    row = lax.broadcasted_iota(jnp.int32, (LANES, LANES), 0)
    col = lax.broadcasted_iota(jnp.int32, (LANES, LANES), 1)
    same = jnp.where(row == col, 1.0, 0.0).astype(BF)
    found = total[:, width:].astype(BF)
    found = lax.dot_general(same, found, NT, preferred_element_type=F32)
    kind = lax.broadcasted_iota(jnp.int32, (LANES, tok), 0)
    out = []
    for k in range(plan.top):
        mine = jnp.where(kind == routes_ref[k : k + 1, :], found, 0.0)
        out.append(jnp.sum(mine, axis=0, keepdims=True))
    out = jnp.concatenate(out, axis=0)
    comb_o[...] = (out / comb_ref[...].astype(F32)).astype(BF)


def on_device(plan, tokens, routes, combine, upstream, w_gate, w_up, w_down):
    tok, width, hidden = plan.tok, plan.width, plan.hidden
    inner, outer, part = plan.inner, plan.outer, plan.hidden // 2
    full = 2 * width + LANES
    shape = jax.ShapeDtypeStruct
    info = jnp.asarray(plan.table())[lax.axis_index("expert")]
    swap = [(0, 1), (1, 0)]

    block = pl.pallas_call(
        functools.partial(pack_kernel, plan),
        out_shape=shape((tok, full), BF),
        in_specs=[VMEM] * 4,
        out_specs=VMEM,
        compiler_params=params(),
        cost_estimate=cost(1e6, 4 * tok * full),
        name="pack",
    )(tokens, upstream, routes.T, combine.T)

    gate_up = jnp.concatenate([w_gate, w_up], axis=2)
    blocks = [block] * plan.cands

    def hop(r):
        for chain in (0, 1):
            if r <= plan.last[chain]:
                i = chain * (outer - 1) + r
                before = block if r == 1 else blocks[i - 1]
                blocks[i] = lax.ppermute(before, "expert", plan.exchange(r, chain))
        if 1 < r <= min(plan.last):
            i = outer - 1 + r
            blocks[r], blocks[i] = lax.optimization_barrier((blocks[r], blocks[i]))

    hop(1)
    def compact(c):
        rows, use = plan.rows[c], plan.use[c]
        count, n = inner * rows, len(use)
        return pl.pallas_call(
            functools.partial(compact_kernel, plan, c),
            out_shape=[shape((2 * rows, width), BF)] * inner,
            in_specs=[SMEM, VMEM] + [ANY] * n,
            out_specs=[VMEM] * inner,
            scratch_shapes=[
                pltpu.VMEM((n * tok, full), BF),
                pltpu.VMEM((n * tok, count), BF),
                pltpu.VMEM((n * tok, count), BF),
                pltpu.SemaphoreType.DMA((n,)),
            ],
            compiler_params=params(),
            cost_estimate=cost(4 * n * tok * count * width, 2 * n * tok * full),
            name="compact",
        )(info, jnp.asarray(plan.keys([plan.chunks[c]])), *[blocks[i] for i in use])

    def expert(g, arrived):
        rows, n = plan.sizes[g], inner * len(plan.groups[g])
        count = inner * rows
        return pl.pallas_call(
            functools.partial(expert_kernel, plan, g),
            out_shape=[shape((count, hidden), BF)] * 3
            + [shape((rows, width + LANES), BF)] * inner,
            in_specs=[SMEM] + [ANY] * (n + 5),
            out_specs=[VMEM] * (3 + inner),
            scratch_shapes=[
                pltpu.VMEM((count, width), BF),
                pltpu.VMEM((count, width), BF),
                pltpu.VMEM((width, hidden), BF),
                pltpu.VMEM((width, hidden), BF),
                pltpu.VMEM((hidden, width), BF),
                pltpu.VMEM((count, 1), F32),
                pltpu.SemaphoreType.DMA((2 * n + 6 * (hidden // 128),)),
            ],
            compiler_params=params(),
            cost_estimate=cost(10 * count * hidden * width, 6 * hidden * width),
            name="expert",
        )(info, *arrived, *weights)

    def cross(arrays):
        return [arrays[0]] + [
            lax.ppermute(arrays[d], "expert", plan.across(d)) for d in range(1, inner)
        ]

    got, done = [], 1
    for c in range(PARTS):
        for r in range(done + 1, plan.steps[c] + 1):
            hop(r)
        done = max(done, plan.steps[c])
        sent = compact(c)
        if c > 0:
            got[-1], sent = lax.optimization_barrier((got[-1], sent))
        if c == PARTS - 2:
            gate_up, sent = lax.optimization_barrier((gate_up, sent))
            gate_up = lax.ppermute(gate_up, "dp", swap)
        if c == PARTS - 1:
            gate_up, sent = lax.optimization_barrier((gate_up, sent))
            down = lax.ppermute(lax.optimization_barrier((w_down, sent))[0], "dp", swap)
        got.append(cross(sent))
        if c == 0:
            i = outer - 1 + done
            got[0], blocks[done], blocks[i] = lax.optimization_barrier(
                (got[0], blocks[done], blocks[i])
            )
    weights = [w_gate, w_up, w_down, gate_up, down]
    outs = expert(0, sum(got[:-1], []))
    late = got[-1]
    outs, late = lax.optimization_barrier((outs, late))
    got[-1] = late
    backs = cross(outs[3:])
    more = expert(1, late)
    got = sum(got, [])
    mids = outs[:3] + more[:3]

    count = inner * sum(plan.rows)

    def weight_grads(own, extra):
        return pl.pallas_call(
            functools.partial(weight_kernel, plan, own),
            out_shape=[
                shape((1, width, part), BF),
                shape((1, width, part), BF),
                shape((1, part, width), BF),
            ],
            in_specs=[ANY] * (inner * PARTS + 6) + [VMEM] * len(extra),
            out_specs=[VMEM] * 3,
            scratch_shapes=[
                pltpu.VMEM((count, width), BF),
                pltpu.VMEM((count, width), BF),
                pltpu.VMEM((count, part), BF),
                pltpu.VMEM((count, 2 * part), BF),
                pltpu.SemaphoreType.DMA((2 * inner * PARTS,)),
                pltpu.SemaphoreType.DMA((6,)),
            ],
            compiler_params=params(),
            cost_estimate=cost(6 * count * part * width, 4 * count * (width + hidden)),
            name="weight_grads",
        )(*got, *mids, *extra)

    def spread(homes, groups, extra):
        slots = inner * sum(plan.sizes[:groups])
        return pl.pallas_call(
            functools.partial(spread_kernel, plan, homes, groups),
            out_shape=[shape((tok, width + LANES), BF)] * len(homes),
            in_specs=[SMEM, VMEM] + [ANY] * (plan.cands + groups * inner + len(extra)),
            out_specs=[VMEM] * len(homes),
            scratch_shapes=[
                pltpu.VMEM((slots, width + LANES), BF),
                pltpu.VMEM((plan.cands, tok, LANES), BF),
                pltpu.VMEM((len(homes) * tok, slots), BF),
                pltpu.SemaphoreType.DMA((groups * inner,)),
                pltpu.SemaphoreType.DMA((plan.cands,)),
            ],
            compiler_params=params(),
            cost_estimate=cost(2 * len(homes) * tok * slots * width, 2 * slots * width),
            name="spread",
        )(
            info,
            jnp.asarray(plan.keys(plan.spans[:groups])),
            *blocks,
            *backs[: groups * inner],
            *extra,
        )

    mine = weight_grads(False, [])
    backs = backs + cross(more[3:])
    (first,) = spread([1], 1, [])
    sums = {}
    mine, backs, first = lax.optimization_barrier((mine, backs, first))
    came = [lax.ppermute(first, "expert", plan.flip(1))]
    theirs = [lax.ppermute(w, "dp", swap) for w in mine]
    rest = [r for r in range(outer) if r != 1]
    sums.update(zip(rest, spread(rest, 2, [mine[0], first])))
    bit = 1
    while bit < outer:
        for r in range(bit, outer, 2 * bit):
            if r == 1:
                continue
            sent = lax.ppermute(sums[r], "expert", plan.flip(bit))
            if r == bit:
                came.append(sent)
            else:
                sums[r - bit] = pl.pallas_call(
                    add_kernel,
                    out_shape=shape((tok, width + LANES), BF),
                    in_specs=[VMEM] * 2,
                    out_specs=VMEM,
                    name="add",
                )(sums[r - bit], sent)
        bit *= 2
    grads = weight_grads(True, theirs)
    home = [sums[0]] + came
    grad_tokens, grad_combine = pl.pallas_call(
        functools.partial(home_kernel, plan, len(home)),
        out_shape=[shape((tok, width), BF), shape((plan.top, tok), BF)],
        in_specs=[VMEM] * (len(home) + 2) + [ANY],
        out_specs=[VMEM] * 2,
        compiler_params=params(),
        cost_estimate=cost(1e6, 2 * tok * width * (outer + 1)),
        name="home",
    )(*home, routes.T, combine.T, grads[0])
    return (grad_tokens, grad_combine.T, *grads)


def solution(mesh):
    rows = P(("parts", "dp", "expert"), None)
    in_specs = (rows,) * 4 + (P("expert", None, "dp"),) * 2 + (P("expert", "dp", None),)
    out_specs = (rows,) * 2 + (P(("parts", "expert"), None, "dp"),) * 2
    out_specs += (P(("parts", "expert"), "dp", None),)
    shape = dict(mesh.shape)

    def whole(tokens, routes, combine, upstream, w_gate, w_up, w_down):
        devices = shape["parts"] * shape["dp"] * shape["expert"]
        plan = Plan(
            shape["expert"],
            tokens.shape[0] // devices,
            routes.shape[1],
            tokens.shape[1],
            w_gate.shape[2],
        )
        body = functools.partial(on_device, plan)
        return jax.shard_map(
            body, mesh=mesh, in_specs=in_specs, out_specs=out_specs, check_vma=False
        )(tokens, routes, combine, upstream, w_gate, w_up, w_down)

    return whole
```

```python
import functools

import jax
import jax.numpy as jnp
import numpy as np
from jax import lax
from jax.experimental import pallas as pl
from jax.experimental.pallas import tpu as pltpu
from jax.sharding import PartitionSpec as P

BF = jnp.bfloat16
F32 = jnp.float32
LANES = 128
HALF = 64
STRIDE = 1024
PARTS = 4
NOWHERE = -(1 << 20)
ANY = pl.BlockSpec(memory_space=pltpu.HBM)
VMEM = pl.BlockSpec(memory_space=pltpu.VMEM)
SMEM = pl.BlockSpec(memory_space=pltpu.SMEM)
TN = (((0,), (0,)), ((), ()))
NT = (((1,), (1,)), ((), ()))


def params(megabytes=60):
    return pltpu.CompilerParams(vmem_limit_bytes=megabytes << 20)


def cost(flops, moved):
    return pl.CostEstimate(flops=int(flops), bytes_accessed=int(moved), transcendentals=0)


class Plan:
    def __init__(self, experts, tok, top, width, hidden):
        self.experts, self.tok, self.top = experts, tok, top
        self.width, self.hidden = width, hidden
        outer = 1
        while outer * outer < experts:
            outer *= 2
        self.outer, self.inner = outer, experts // outer
        mean = tok * top // experts
        self.cap = min(tok, max(2, mean + tok * top // (8 * experts)))
        total = -(-self.outer * self.cap // 16) * 16
        step = self.outer // PARTS
        marks = [k * step * self.cap // 16 * 16 for k in range(PARTS)] + [total]
        if marks[1] >= 32:
            marks[1] = marks[1] // 32 * 16
            marks[2] = marks[1] + 32
        self.chunks = [(marks[k], marks[k + 1]) for k in range(PARTS)]
        self.rows = [b - a for a, b in self.chunks]
        self.steps = [(k + 1) * step - 1 for k in range(PARTS)]
        self.groups = [range(PARTS - 1), range(PARTS - 1, PARTS)]
        self.spans = [(marks[g[0]], marks[g[-1] + 1]) for g in self.groups]
        self.sizes = [b - a for a, b in self.spans]
        self.cands = 2 * self.outer - 1
        self.use = [self.used(*c) for c in self.chunks]
        needed = set().union(*self.use)
        self.last = [
            max(i for i in needed if 0 < i < outer),
            max(i for i in needed if i >= outer) - outer + 1,
        ]

    def keys(self, spans):
        return np.array(
            [[d * STRIDE + q for a, b in spans for d in range(self.inner) for q in range(a, b)]],
            np.int32,
        )

    def order(self, z):
        rest = [s for s in range(self.outer) if s not in (z, z ^ 1)]
        return [z, z ^ 1] + sorted(rest, key=lambda s: abs(s - z))

    def swap(self, z, odd):
        to = z - 1 if (z % 2 == 0) == odd else z + 1
        return to if 0 <= to < self.outer else z

    def trace(self):
        held = {0: list(range(self.outer))}
        for chain in (0, 1):
            last = held[0]
            for r in range(1, self.outer):
                odd = (r % 2 == 0) == (chain == 0)
                last = [last[self.swap(z, odd)] for z in range(self.outer)]
                held[chain * (self.outer - 1) + r] = last
        return held

    def cand(self, z, source):
        step = lambda i: i if i < self.outer else i - self.outer + 1
        found = [i for i, held in self.trace().items() if held[z] == source]
        return min(found, key=lambda i: (step(i), i))

    def exchange(self, r, chain):
        odd = (r % 2 == 0) == (chain == 0)
        return [
            (z * self.inner + p, self.swap(z, odd) * self.inner + p)
            for z in range(self.outer)
            for p in range(self.inner)
        ]

    def used(self, a, b):
        slots = [k for k in range(self.outer) if k * self.cap < b and (k + 1) * self.cap > a]
        return sorted(
            {self.cand(z, self.order(z)[k]) for z in range(self.outer) for k in slots}
        )

    def partner(self, p, d):
        return p ^ d if self.inner & (self.inner - 1) == 0 else (d - p) % self.inner

    def table(self):
        rows = []
        for e in range(self.experts):
            z, p = divmod(e, self.inner)
            offs = [NOWHERE] * self.cands
            for slot, source in enumerate(self.order(z)):
                offs[self.cand(z, source)] = slot * self.cap
            experts = [z * self.inner + self.partner(p, d) for d in range(self.inner)]
            homes = [self.cand(z, z ^ r) for r in range(self.outer)]
            rows.append(offs + experts + homes)
        return np.array(rows, np.int32)

    def across(self, d):
        return [
            (z * self.inner + p, z * self.inner + self.partner(p, d))
            for z in range(self.outer)
            for p in range(self.inner)
        ]

    def flip(self, r):
        return [
            (z * self.inner + p, (z ^ r) * self.inner + p)
            for z in range(self.outer)
            for p in range(self.inner)
        ]


def pack_kernel(plan, tok_ref, up_ref, routes_ref, comb_ref, out_ref):
    tok, width = plan.tok, plan.width
    out_ref[:, :width] = tok_ref[...]
    out_ref[:, width : 2 * width] = up_ref[...]
    kind = lax.broadcasted_iota(jnp.int32, (LANES, tok), 0)
    weight = jnp.zeros((LANES, tok), F32)
    named = jnp.zeros((LANES, tok), F32)
    comb = comb_ref[...].astype(F32)
    for k in range(plan.top):
        e = routes_ref[k : k + 1, :]
        weight = jnp.where(kind == e, comb[k : k + 1, :], weight)
        named = jnp.where(kind == e + HALF, 1.0, named)
    row = lax.broadcasted_iota(jnp.int32, (tok, tok), 0)
    col = lax.broadcasted_iota(jnp.int32, (tok, tok), 1)
    upto = jnp.where(row <= col, 1.0, 0.0).astype(BF)
    count = jnp.dot(named.astype(BF), upto, preferred_element_type=F32)
    table = (weight + count * named).astype(BF)
    same = jnp.where(row == col, 1.0, 0.0).astype(BF)
    turned = lax.dot_general(same, table, NT, preferred_element_type=F32)
    out_ref[:, 2 * width :] = turned.astype(BF)


def picks(plan, meta, off, experts, key, scaled):
    tok = meta.shape[0]
    lane = lax.broadcasted_iota(jnp.int32, (tok, LANES), 1)
    one = jnp.zeros((tok, key.shape[1]), F32)
    two = jnp.zeros((tok, key.shape[1]), F32)
    for d, e in enumerate(experts):
        place = jnp.sum(jnp.where(lane == e + HALF, meta, 0.0), axis=1, keepdims=True)
        place = place.astype(jnp.int32)
        spot = jnp.where(place > 0, place - 1 + off + d * STRIDE, -1)
        hit = spot == key
        one = jnp.where(hit, 1.0, one)
        if scaled:
            weight = jnp.sum(jnp.where(lane == e, meta, 0.0), axis=1, keepdims=True)
            two = jnp.where(hit, weight, two)
    return one, two


def compact_kernel(plan, chunk, *refs):
    use, rows = plan.use[chunk], plan.rows[chunk]
    n, width, tok, inner = len(use), plan.width, plan.tok, plan.inner
    info, key_ref = refs[:2]
    blocks, outs = refs[2 : 2 + n], refs[2 + n : 2 + n + inner]
    held, one_s, two_s, sems = refs[2 + n + inner :]
    copies = [
        pltpu.make_async_copy(b, held.at[pl.ds(i * tok, tok)], sems.at[i])
        for i, b in enumerate(blocks)
    ]
    for c in copies:
        c.start()
    experts = [info[plan.cands + d] for d in range(inner)]
    for i, c in enumerate(copies):
        c.wait()
        meta = held[i * tok : (i + 1) * tok, 2 * width :].astype(F32)
        one, two = picks(plan, meta, info[use[i]], experts, key_ref[...], True)
        one_s[i * tok : (i + 1) * tok, :] = one.astype(BF)
        two_s[i * tok : (i + 1) * tok, :] = two.astype(BF)
    for part, source in ((0, one_s), (1, two_s)):
        have = held[:, part * width : (part + 1) * width]
        found = lax.dot_general(source[...], have, TN, preferred_element_type=F32).astype(BF)
        for d in range(inner):
            outs[d][part * rows : (part + 1) * rows, :] = found[d * rows : (d + 1) * rows]


def pieces(plan, group, got, x_s, d_s, sems, base=0):
    inner, size, first = plan.inner, plan.sizes[group], plan.spans[group][0]
    x_copies, d_copies = [], []
    for i, g in enumerate(got):
        c, d = plan.groups[group][i // inner], i % inner
        rows = plan.rows[c]
        to = pl.ds(base + d * size + plan.chunks[c][0] - first, rows)
        x_copies.append(pltpu.make_async_copy(g.at[pl.ds(0, rows)], x_s.at[to], sems.at[2 * i]))
        d_copies.append(
            pltpu.make_async_copy(g.at[pl.ds(rows, rows)], d_s.at[to], sems.at[2 * i + 1])
        )
    return x_copies, d_copies


def expert_kernel(plan, group, *refs):
    inner, rows, width, hidden = plan.inner, plan.sizes[group], plan.width, plan.hidden
    part, count, n = hidden // 2, inner * rows, inner * len(plan.groups[group])
    info = refs[0]
    got, weights = refs[1 : 1 + n], refs[1 + n : 6 + n]
    hid_o, gate_o, up_o = refs[6 + n : 9 + n]
    backs = refs[9 + n : 9 + n + inner]
    x_s, d_s, wg_s, wu_s, wd_s, comb_s, sems = refs[9 + n + inner :]
    own_g, own_u, own_d, both, other_d = [w.at[0] for w in weights]
    views = [
        (own_g, both.at[:, pl.ds(0, part)]),
        (own_u, both.at[:, pl.ds(part, part)]),
        (own_d, other_d),
    ]
    x_copies, d_copies = pieces(plan, group, got, x_s, d_s, sems)
    tile, tiles = hidden, []
    for t in range(hidden // tile):
        for kind, where in ((0, wg_s), (1, wu_s), (2, wd_s)):
            at, here = t * tile, []
            while at < (t + 1) * tile:
                half, start = divmod(at, part)
                size = min((t + 1) * tile, (half + 1) * part) - at
                source, to = pl.ds(start, size), pl.ds(at, size)
                w = views[kind][half]
                here.append((w.at[source], where.at[to]) if kind == 2 else (w.at[:, source], where.at[:, to]))
                at += size
            tiles.append(here)
    w_copies, used = [], 2 * n
    for here in tiles:
        w_copies.append([])
        for source, to in here:
            w_copies[-1].append(pltpu.make_async_copy(source, to, sems.at[used]))
            used += 1
    for c in x_copies + w_copies[0] + w_copies[1] + d_copies:
        c.start()
    for here in w_copies[2:]:
        for c in here:
            c.start()
    for t in range(hidden // tile):
        at = slice(t * tile, (t + 1) * tile)
        gate_w, up_w, down_w = w_copies[3 * t : 3 * t + 3]
        for c in (x_copies if t == 0 else []) + gate_w:
            c.wait()
        gate = jnp.dot(x_s[...], wg_s[:, at], preferred_element_type=F32)
        for c in up_w:
            c.wait()
        up = jnp.dot(x_s[...], wu_s[:, at], preferred_element_type=F32)
        for c in (d_copies if t == 0 else []) + down_w:
            c.wait()
        mixed = lax.dot_general(d_s[...], wd_s[at, :], NT, preferred_element_type=F32)
        logistic = jax.nn.sigmoid(gate)
        silu = gate * logistic
        hid = (silu * up).astype(BF)
        hid_o[:, at] = hid
        comb = jnp.sum(hid.astype(F32) * mixed, axis=1, keepdims=True)
        comb_s[...] = comb if t == 0 else comb_s[...] + comb
        gate_o[:, at] = (mixed * up * logistic * (1.0 + gate * (1.0 - logistic))).astype(BF)
        up_o[:, at] = (mixed * silu).astype(BF)

    wide = width // 2

    @pl.loop(0, width // wide)
    def _(j):
        at = pl.ds(pl.multiple_of(j * wide, wide), wide)
        back = lax.dot_general(gate_o[...], wg_s[at, :], NT, preferred_element_type=F32)
        back += lax.dot_general(up_o[...], wu_s[at, :], NT, preferred_element_type=F32)
        back = back.astype(BF)
        for d in range(inner):
            backs[d][:, at] = back[d * rows : (d + 1) * rows]

    lane = lax.broadcasted_iota(jnp.int32, (count, LANES), 1)
    comb = jnp.where(lane == info[plan.cands], comb_s[...], 0.0).astype(BF)
    for d in range(inner):
        backs[d][:, width:] = comb[d * rows : (d + 1) * rows]


def weight_kernel(plan, own, *refs):
    inner, width, hidden = plan.inner, plan.width, plan.hidden
    part, n = hidden // 2, plan.inner * PARTS
    got, mids = refs[:n], refs[n : n + 6]
    at = n + 6
    theirs = refs[at : at + 3] if own else None
    at += 3 if own else 0
    outs = refs[at : at + 3]
    x_s, d_s, h_s, gu_s, g_s, u_s, w_s, sems, mid_sems, out_sems = refs[at + 3 : at + 13]
    kept = refs[at + 13 :]
    first, second, base, taken = [], [], 0, 0
    half = pl.ds(0 if own else part, part)
    for g in range(2):
        many = inner * len(plan.groups[g])
        mine = got[taken : taken + many]
        at_sems = sems.at[pl.ds(2 * taken, 2 * many)]
        x_copies, d_copies = pieces(plan, g, mine, x_s, d_s, at_sems, base)
        first += x_copies
        second += d_copies
        to = pl.ds(base, inner * plan.sizes[g])
        spots = (h_s.at[to], gu_s.at[to, pl.ds(0, part)], gu_s.at[to, pl.ds(part, part)])
        for i, (m, s) in enumerate(zip(mids[3 * g : 3 * g + 3], spots)):
            copy = pltpu.make_async_copy(m.at[:, half], s, mid_sems.at[3 * g + i])
            (second if i == 0 else first).append(copy)
        taken += many
        base += inner * plan.sizes[g]
    came = []
    if own:
        came = [
            pltpu.make_async_copy(t.at[0], k, out_sems.at[5 + i])
            for i, (t, k) in enumerate(zip(theirs, kept))
        ]
    for c in first + came[:2] + second + came[2:]:
        c.start()
    for c in first + came[:2]:
        c.wait()
    tile, left = width // 2, []
    for j in range(2):
        to = slice(j * tile, (j + 1) * tile)
        both = lax.dot_general(x_s[:, to], gu_s[...], TN, preferred_element_type=F32)
        for i, (o, s) in enumerate(zip(outs, (g_s, u_s))):
            value = both[:, i * part : (i + 1) * part]
            if own:
                value += kept[i][to, :].astype(F32)
            s[to, :] = value.astype(BF)
            rows = pl.ds(j * tile, tile)
            left.append(
                pltpu.make_async_copy(s.at[rows], o.at[0, rows], out_sems.at[2 * j + i])
            )
            left[-1].start()
    for c in second + came[2:]:
        c.wait()
    down = lax.dot_general(h_s[...], d_s[...], TN, preferred_element_type=F32)
    if own:
        down += kept[2][...].astype(F32)
    w_s[...] = down.astype(BF)
    left.append(pltpu.make_async_copy(w_s, outs[2].at[0], out_sems.at[4]))
    left[-1].start()
    for c in left:
        c.wait()


def spread_kernel(plan, homes, groups, *refs):
    inner, tok, width = plan.inner, plan.tok, plan.width
    info, key_ref = refs[:2]
    blocks = refs[2 : 2 + plan.cands]
    at = 2 + plan.cands
    backs = refs[at : at + groups * inner]
    outs = refs[-5 - len(homes) : -5]
    held, metas, pick_s, sems, meta_sems = refs[-5:]
    copies, later, start = [], [], 0
    for i, b in enumerate(blocks):
        copies.append(
            pltpu.make_async_copy(b.at[:, pl.ds(2 * width, LANES)], metas.at[i], meta_sems.at[i])
        )
    for i, b in enumerate(backs):
        rows = plan.sizes[i // inner]
        later.append(pltpu.make_async_copy(b, held.at[pl.ds(start, rows)], sems.at[i]))
        start += rows
    for c in copies + later:
        c.start()
    for c in copies:
        c.wait()
    experts = [info[plan.cands + d] for d in range(inner)]
    for i, r in enumerate(homes):
        which = info[plan.cands + inner + r]
        meta = metas[which].astype(F32)
        one, _ = picks(plan, meta, info[which], experts, key_ref[...], False)
        pick_s[i * tok : (i + 1) * tok, :] = one.astype(BF)
    for c in later:
        c.wait()
    sums = jnp.dot(pick_s[...], held[...], preferred_element_type=F32).astype(BF)
    for i in range(len(homes)):
        outs[i][...] = sums[i * tok : (i + 1) * tok]


def add_kernel(a_ref, b_ref, o_ref):
    o_ref[...] = (a_ref[...].astype(F32) + b_ref[...].astype(F32)).astype(BF)


def home_kernel(plan, count, *refs):
    parts = refs[:count]
    routes_ref, comb_ref, _, tok_o, comb_o = refs[count:]
    width, tok = plan.width, plan.tok
    total = parts[0][...].astype(F32)
    for p in parts[1:]:
        total += p[...].astype(F32)
    tok_o[...] = total[:, :width].astype(BF)
    row = lax.broadcasted_iota(jnp.int32, (LANES, LANES), 0)
    col = lax.broadcasted_iota(jnp.int32, (LANES, LANES), 1)
    same = jnp.where(row == col, 1.0, 0.0).astype(BF)
    found = total[:, width:].astype(BF)
    found = lax.dot_general(same, found, NT, preferred_element_type=F32)
    kind = lax.broadcasted_iota(jnp.int32, (LANES, tok), 0)
    out = []
    for k in range(plan.top):
        mine = jnp.where(kind == routes_ref[k : k + 1, :], found, 0.0)
        out.append(jnp.sum(mine, axis=0, keepdims=True))
    out = jnp.concatenate(out, axis=0)
    comb_o[...] = (out / comb_ref[...].astype(F32)).astype(BF)


def on_device(plan, tokens, routes, combine, upstream, w_gate, w_up, w_down):
    tok, width, hidden = plan.tok, plan.width, plan.hidden
    inner, outer, part = plan.inner, plan.outer, plan.hidden // 2
    full = 2 * width + LANES
    shape = jax.ShapeDtypeStruct
    info = jnp.asarray(plan.table())[lax.axis_index("expert")]
    swap = [(0, 1), (1, 0)]

    block = pl.pallas_call(
        functools.partial(pack_kernel, plan),
        out_shape=shape((tok, full), BF),
        in_specs=[VMEM] * 4,
        out_specs=VMEM,
        compiler_params=params(),
        cost_estimate=cost(1e6, 4 * tok * full),
        name="pack",
    )(tokens, upstream, routes.T, combine.T)

    gate_up = jnp.concatenate([w_gate, w_up], axis=2)
    blocks = [block] * plan.cands

    def hop(r):
        for chain in (0, 1):
            if r <= plan.last[chain]:
                i = chain * (outer - 1) + r
                before = block if r == 1 else blocks[i - 1]
                blocks[i] = lax.ppermute(before, "expert", plan.exchange(r, chain))
        if 1 < r <= min(plan.last):
            i = outer - 1 + r
            blocks[r], blocks[i] = lax.optimization_barrier((blocks[r], blocks[i]))

    hop(1)
    def compact(c):
        rows, use = plan.rows[c], plan.use[c]
        count, n = inner * rows, len(use)
        return pl.pallas_call(
            functools.partial(compact_kernel, plan, c),
            out_shape=[shape((2 * rows, width), BF)] * inner,
            in_specs=[SMEM, VMEM] + [ANY] * n,
            out_specs=[VMEM] * inner,
            scratch_shapes=[
                pltpu.VMEM((n * tok, full), BF),
                pltpu.VMEM((n * tok, count), BF),
                pltpu.VMEM((n * tok, count), BF),
                pltpu.SemaphoreType.DMA((n,)),
            ],
            compiler_params=params(),
            cost_estimate=cost(4 * n * tok * count * width, 2 * n * tok * full),
            name="compact",
        )(info, jnp.asarray(plan.keys([plan.chunks[c]])), *[blocks[i] for i in use])

    def expert(g, arrived):
        rows, n = plan.sizes[g], inner * len(plan.groups[g])
        count = inner * rows
        return pl.pallas_call(
            functools.partial(expert_kernel, plan, g),
            out_shape=[shape((count, hidden), BF)] * 3
            + [shape((rows, width + LANES), BF)] * inner,
            in_specs=[SMEM] + [ANY] * (n + 5),
            out_specs=[VMEM] * (3 + inner),
            scratch_shapes=[
                pltpu.VMEM((count, width), BF),
                pltpu.VMEM((count, width), BF),
                pltpu.VMEM((width, hidden), BF),
                pltpu.VMEM((width, hidden), BF),
                pltpu.VMEM((hidden, width), BF),
                pltpu.VMEM((count, 1), F32),
                pltpu.SemaphoreType.DMA((2 * n + 6 * (hidden // 128),)),
            ],
            compiler_params=params(),
            cost_estimate=cost(10 * count * hidden * width, 6 * hidden * width),
            name="expert",
        )(info, *arrived, *weights)

    def cross(arrays):
        return [arrays[0]] + [
            lax.ppermute(arrays[d], "expert", plan.across(d)) for d in range(1, inner)
        ]

    got, done = [], 1
    for c in range(PARTS):
        for r in range(done + 1, plan.steps[c] + 1):
            hop(r)
        done = max(done, plan.steps[c])
        sent = compact(c)
        if c > 0:
            got[-1], sent = lax.optimization_barrier((got[-1], sent))
        if c == PARTS - 2:
            gate_up, sent = lax.optimization_barrier((gate_up, sent))
            gate_up = lax.ppermute(gate_up, "dp", swap)
        if c == PARTS - 1:
            gate_up, sent = lax.optimization_barrier((gate_up, sent))
            down = lax.ppermute(lax.optimization_barrier((w_down, sent))[0], "dp", swap)
        got.append(cross(sent))
        if c == 0:
            i = outer - 1 + done
            got[0], blocks[done], blocks[i] = lax.optimization_barrier(
                (got[0], blocks[done], blocks[i])
            )
    weights = [w_gate, w_up, w_down, gate_up, down]
    outs = expert(0, sum(got[:-1], []))
    late = got[-1]
    outs, late = lax.optimization_barrier((outs, late))
    got[-1] = late
    backs = cross(outs[3:])
    more = expert(1, late)
    got = sum(got, [])
    mids = outs[:3] + more[:3]

    count = inner * sum(plan.rows)

    grad_scratch = [
        pltpu.VMEM((width, part), BF),
        pltpu.VMEM((width, part), BF),
        pltpu.VMEM((part, width), BF),
    ]

    def weight_grads(own, extra):
        return pl.pallas_call(
            functools.partial(weight_kernel, plan, own),
            out_shape=[
                shape((1, width, part), BF),
                shape((1, width, part), BF),
                shape((1, part, width), BF),
            ],
            in_specs=[ANY] * (inner * PARTS + 6 + len(extra)),
            out_specs=[ANY] * 3,
            scratch_shapes=[
                pltpu.VMEM((count, width), BF),
                pltpu.VMEM((count, width), BF),
                pltpu.VMEM((count, part), BF),
                pltpu.VMEM((count, 2 * part), BF),
                *grad_scratch,
                pltpu.SemaphoreType.DMA((2 * inner * PARTS,)),
                pltpu.SemaphoreType.DMA((6,)),
                pltpu.SemaphoreType.DMA((8,)),
                *(grad_scratch if own else []),
            ],
            compiler_params=params(),
            cost_estimate=cost(6 * count * part * width, 4 * count * (width + hidden)),
            name="weight_grads",
        )(*got, *mids, *extra)

    def spread(homes, groups, extra):
        slots = inner * sum(plan.sizes[:groups])
        return pl.pallas_call(
            functools.partial(spread_kernel, plan, homes, groups),
            out_shape=[shape((tok, width + LANES), BF)] * len(homes),
            in_specs=[SMEM, VMEM] + [ANY] * (plan.cands + groups * inner + len(extra)),
            out_specs=[VMEM] * len(homes),
            scratch_shapes=[
                pltpu.VMEM((slots, width + LANES), BF),
                pltpu.VMEM((plan.cands, tok, LANES), BF),
                pltpu.VMEM((len(homes) * tok, slots), BF),
                pltpu.SemaphoreType.DMA((groups * inner,)),
                pltpu.SemaphoreType.DMA((plan.cands,)),
            ],
            compiler_params=params(),
            cost_estimate=cost(2 * len(homes) * tok * slots * width, 2 * slots * width),
            name="spread",
        )(
            info,
            jnp.asarray(plan.keys(plan.spans[:groups])),
            *blocks,
            *backs[: groups * inner],
            *extra,
        )

    mine = weight_grads(False, [])
    backs = backs + cross(more[3:])
    (first,) = spread([1], 1, [])
    sums = {}
    mine, backs, first = lax.optimization_barrier((mine, backs, first))
    came = [lax.ppermute(first, "expert", plan.flip(1))]
    theirs = [lax.ppermute(w, "dp", swap) for w in mine]
    rest = [r for r in range(outer) if r != 1]
    sums.update(zip(rest, spread(rest, 2, [mine[0], first])))
    bit = 1
    while bit < outer:
        for r in range(bit, outer, 2 * bit):
            if r == 1:
                continue
            sent = lax.ppermute(sums[r], "expert", plan.flip(bit))
            if r == bit:
                came.append(sent)
            else:
                sums[r - bit] = pl.pallas_call(
                    add_kernel,
                    out_shape=shape((tok, width + LANES), BF),
                    in_specs=[VMEM] * 2,
                    out_specs=VMEM,
                    name="add",
                )(sums[r - bit], sent)
        bit *= 2
    grads = weight_grads(True, theirs)
    home = [sums[0]] + came
    grad_tokens, grad_combine = pl.pallas_call(
        functools.partial(home_kernel, plan, len(home)),
        out_shape=[shape((tok, width), BF), shape((plan.top, tok), BF)],
        in_specs=[VMEM] * (len(home) + 2) + [ANY],
        out_specs=[VMEM] * 2,
        compiler_params=params(),
        cost_estimate=cost(1e6, 2 * tok * width * (outer + 1)),
        name="home",
    )(*home, routes.T, combine.T, grads[0])
    return (grad_tokens, grad_combine.T, *grads)


def solution(mesh):
    rows = P(("parts", "dp", "expert"), None)
    in_specs = (rows,) * 4 + (P("expert", None, "dp"),) * 2 + (P("expert", "dp", None),)
    out_specs = (rows,) * 2 + (P(("parts", "expert"), None, "dp"),) * 2
    out_specs += (P(("parts", "expert"), "dp", None),)
    shape = dict(mesh.shape)

    def whole(tokens, routes, combine, upstream, w_gate, w_up, w_down):
        devices = shape["parts"] * shape["dp"] * shape["expert"]
        plan = Plan(
            shape["expert"],
            tokens.shape[0] // devices,
            routes.shape[1],
            tokens.shape[1],
            w_gate.shape[2],
        )
        body = functools.partial(on_device, plan)
        return jax.shard_map(
            body, mesh=mesh, in_specs=in_specs, out_specs=out_specs, check_vma=False
        )(tokens, routes, combine, upstream, w_gate, w_up, w_down)

    return whole
```

```python
import functools

import jax
import jax.numpy as jnp
import numpy as np
from jax import lax
from jax.experimental import pallas as pl
from jax.experimental.pallas import tpu as pltpu
from jax.sharding import PartitionSpec as P

BF = jnp.bfloat16
F32 = jnp.float32
LANES = 128
HALF = 64
STRIDE = 1024
PARTS = 4
NOWHERE = -(1 << 20)
ANY = pl.BlockSpec(memory_space=pltpu.HBM)
VMEM = pl.BlockSpec(memory_space=pltpu.VMEM)
SMEM = pl.BlockSpec(memory_space=pltpu.SMEM)
TN = (((0,), (0,)), ((), ()))
NT = (((1,), (1,)), ((), ()))


def params(megabytes=60):
    return pltpu.CompilerParams(vmem_limit_bytes=megabytes << 20)


def cost(flops, moved):
    return pl.CostEstimate(flops=int(flops), bytes_accessed=int(moved), transcendentals=0)


class Plan:
    def __init__(self, experts, tok, top, width, hidden):
        self.experts, self.tok, self.top = experts, tok, top
        self.width, self.hidden = width, hidden
        outer = 1
        while outer * outer < experts:
            outer *= 2
        self.outer, self.inner = outer, experts // outer
        mean = tok * top // experts
        self.cap = min(tok, max(2, mean + tok * top // (8 * experts)))
        total = -(-self.outer * self.cap // 16) * 16
        step = self.outer // PARTS
        marks = [k * step * self.cap // 16 * 16 for k in range(PARTS)] + [total]
        self.chunks = [(marks[k], marks[k + 1]) for k in range(PARTS)]
        self.rows = [b - a for a, b in self.chunks]
        self.steps = [(k + 1) * step - 1 for k in range(PARTS)]
        self.groups = [range(PARTS - 1), range(PARTS - 1, PARTS)]
        self.spans = [(marks[g[0]], marks[g[-1] + 1]) for g in self.groups]
        self.sizes = [b - a for a, b in self.spans]
        self.cands = 2 * self.outer - 1
        self.use = [self.used(*c) for c in self.chunks]
        needed = set().union(*self.use)
        self.last = [
            max(i for i in needed if 0 < i < outer),
            max(i for i in needed if i >= outer) - outer + 1,
        ]

    def keys(self, spans):
        return np.array(
            [[d * STRIDE + q for a, b in spans for d in range(self.inner) for q in range(a, b)]],
            np.int32,
        )

    def order(self, z):
        rest = [s for s in range(self.outer) if s not in (z, z ^ 1)]
        return [z, z ^ 1] + sorted(rest, key=lambda s: abs(s - z))

    def swap(self, z, odd):
        to = z - 1 if (z % 2 == 0) == odd else z + 1
        return to if 0 <= to < self.outer else z

    def trace(self):
        held = {0: list(range(self.outer))}
        for chain in (0, 1):
            last = held[0]
            for r in range(1, self.outer):
                odd = (r % 2 == 0) == (chain == 0)
                last = [last[self.swap(z, odd)] for z in range(self.outer)]
                held[chain * (self.outer - 1) + r] = last
        return held

    def cand(self, z, source):
        step = lambda i: i if i < self.outer else i - self.outer + 1
        found = [i for i, held in self.trace().items() if held[z] == source]
        return min(found, key=lambda i: (step(i), i))

    def exchange(self, r, chain):
        odd = (r % 2 == 0) == (chain == 0)
        return [
            (z * self.inner + p, self.swap(z, odd) * self.inner + p)
            for z in range(self.outer)
            for p in range(self.inner)
        ]

    def used(self, a, b):
        slots = [k for k in range(self.outer) if k * self.cap < b and (k + 1) * self.cap > a]
        return sorted(
            {self.cand(z, self.order(z)[k]) for z in range(self.outer) for k in slots}
        )

    def partner(self, p, d):
        return p ^ d if self.inner & (self.inner - 1) == 0 else (d - p) % self.inner

    def table(self):
        rows = []
        for e in range(self.experts):
            z, p = divmod(e, self.inner)
            offs = [NOWHERE] * self.cands
            for slot, source in enumerate(self.order(z)):
                offs[self.cand(z, source)] = slot * self.cap
            experts = [z * self.inner + self.partner(p, d) for d in range(self.inner)]
            homes = [self.cand(z, z ^ r) for r in range(self.outer)]
            rows.append(offs + experts + homes)
        return np.array(rows, np.int32)

    def across(self, d):
        return [
            (z * self.inner + p, z * self.inner + self.partner(p, d))
            for z in range(self.outer)
            for p in range(self.inner)
        ]

    def flip(self, r):
        return [
            (z * self.inner + p, (z ^ r) * self.inner + p)
            for z in range(self.outer)
            for p in range(self.inner)
        ]


def pack_kernel(plan, tok_ref, up_ref, routes_ref, comb_ref, out_ref):
    tok, width = plan.tok, plan.width
    out_ref[:, :width] = tok_ref[...]
    out_ref[:, width : 2 * width] = up_ref[...]
    kind = lax.broadcasted_iota(jnp.int32, (LANES, tok), 0)
    weight = jnp.zeros((LANES, tok), F32)
    named = jnp.zeros((LANES, tok), F32)
    comb = comb_ref[...].astype(F32)
    for k in range(plan.top):
        e = routes_ref[k : k + 1, :]
        weight = jnp.where(kind == e, comb[k : k + 1, :], weight)
        named = jnp.where(kind == e + HALF, 1.0, named)
    row = lax.broadcasted_iota(jnp.int32, (tok, tok), 0)
    col = lax.broadcasted_iota(jnp.int32, (tok, tok), 1)
    upto = jnp.where(row <= col, 1.0, 0.0).astype(BF)
    count = jnp.dot(named.astype(BF), upto, preferred_element_type=F32)
    table = (weight + count * named).astype(BF)
    same = jnp.where(row == col, 1.0, 0.0).astype(BF)
    turned = lax.dot_general(same, table, NT, preferred_element_type=F32)
    out_ref[:, 2 * width :] = turned.astype(BF)


def picks(plan, meta, off, experts, key, scaled):
    tok = meta.shape[0]
    lane = lax.broadcasted_iota(jnp.int32, (tok, LANES), 1)
    one = jnp.zeros((tok, key.shape[1]), F32)
    two = jnp.zeros((tok, key.shape[1]), F32)
    for d, e in enumerate(experts):
        place = jnp.sum(jnp.where(lane == e + HALF, meta, 0.0), axis=1, keepdims=True)
        place = place.astype(jnp.int32)
        spot = jnp.where(place > 0, place - 1 + off + d * STRIDE, -1)
        hit = spot == key
        one = jnp.where(hit, 1.0, one)
        if scaled:
            weight = jnp.sum(jnp.where(lane == e, meta, 0.0), axis=1, keepdims=True)
            two = jnp.where(hit, weight, two)
    return one, two


def compact_kernel(plan, chunk, *refs):
    use, rows = plan.use[chunk], plan.rows[chunk]
    n, width, tok, inner = len(use), plan.width, plan.tok, plan.inner
    info, key_ref = refs[:2]
    blocks, outs = refs[2 : 2 + n], refs[2 + n : 2 + n + inner]
    held, one_s, two_s, sems = refs[2 + n + inner :]
    copies = [
        pltpu.make_async_copy(b, held.at[pl.ds(i * tok, tok)], sems.at[i])
        for i, b in enumerate(blocks)
    ]
    for c in copies:
        c.start()
    experts = [info[plan.cands + d] for d in range(inner)]
    for i, c in enumerate(copies):
        c.wait()
        meta = held[i * tok : (i + 1) * tok, 2 * width :].astype(F32)
        one, two = picks(plan, meta, info[use[i]], experts, key_ref[...], True)
        one_s[i * tok : (i + 1) * tok, :] = one.astype(BF)
        two_s[i * tok : (i + 1) * tok, :] = two.astype(BF)
    for part, source in ((0, one_s), (1, two_s)):
        have = held[:, part * width : (part + 1) * width]
        found = lax.dot_general(source[...], have, TN, preferred_element_type=F32).astype(BF)
        for d in range(inner):
            outs[d][part * rows : (part + 1) * rows, :] = found[d * rows : (d + 1) * rows]


def pieces(plan, group, got, x_s, d_s, sems, base=0):
    inner, size, first = plan.inner, plan.sizes[group], plan.spans[group][0]
    x_copies, d_copies = [], []
    for i, g in enumerate(got):
        c, d = plan.groups[group][i // inner], i % inner
        rows = plan.rows[c]
        to = pl.ds(base + d * size + plan.chunks[c][0] - first, rows)
        x_copies.append(pltpu.make_async_copy(g.at[pl.ds(0, rows)], x_s.at[to], sems.at[2 * i]))
        d_copies.append(
            pltpu.make_async_copy(g.at[pl.ds(rows, rows)], d_s.at[to], sems.at[2 * i + 1])
        )
    return x_copies, d_copies


def expert_kernel(plan, group, *refs):
    inner, rows, width, hidden = plan.inner, plan.sizes[group], plan.width, plan.hidden
    part, count, n = hidden // 2, inner * rows, inner * len(plan.groups[group])
    info = refs[0]
    got, weights = refs[1 : 1 + n], refs[1 + n : 6 + n]
    hid_o, gate_o, up_o = refs[6 + n : 9 + n]
    backs = refs[9 + n : 9 + n + inner]
    x_s, d_s, wg_s, wu_s, wd_s, comb_s, sems = refs[9 + n + inner :]
    own_g, own_u, own_d, both, other_d = [w.at[0] for w in weights]
    views = [
        (own_g, both.at[:, pl.ds(0, part)]),
        (own_u, both.at[:, pl.ds(part, part)]),
        (own_d, other_d),
    ]
    x_copies, d_copies = pieces(plan, group, got, x_s, d_s, sems)
    tile, tiles = hidden, []
    for t in range(hidden // tile):
        for kind, where in ((0, wg_s), (1, wu_s), (2, wd_s)):
            at, here = t * tile, []
            while at < (t + 1) * tile:
                half, start = divmod(at, part)
                size = min((t + 1) * tile, (half + 1) * part) - at
                source, to = pl.ds(start, size), pl.ds(at, size)
                w = views[kind][half]
                here.append((w.at[source], where.at[to]) if kind == 2 else (w.at[:, source], where.at[:, to]))
                at += size
            tiles.append(here)
    w_copies, used = [], 2 * n
    for here in tiles:
        w_copies.append([])
        for source, to in here:
            w_copies[-1].append(pltpu.make_async_copy(source, to, sems.at[used]))
            used += 1
    for c in x_copies + w_copies[0] + w_copies[1] + d_copies:
        c.start()
    for here in w_copies[2:]:
        for c in here:
            c.start()
    for t in range(hidden // tile):
        at = slice(t * tile, (t + 1) * tile)
        gate_w, up_w, down_w = w_copies[3 * t : 3 * t + 3]
        for c in (x_copies if t == 0 else []) + gate_w:
            c.wait()
        gate = jnp.dot(x_s[...], wg_s[:, at], preferred_element_type=F32)
        for c in up_w:
            c.wait()
        up = jnp.dot(x_s[...], wu_s[:, at], preferred_element_type=F32)
        for c in (d_copies if t == 0 else []) + down_w:
            c.wait()
        mixed = lax.dot_general(d_s[...], wd_s[at, :], NT, preferred_element_type=F32)
        logistic = jax.nn.sigmoid(gate)
        silu = gate * logistic
        hid = (silu * up).astype(BF)
        hid_o[:, at] = hid
        comb = jnp.sum(hid.astype(F32) * mixed, axis=1, keepdims=True)
        comb_s[...] = comb if t == 0 else comb_s[...] + comb
        gate_o[:, at] = (mixed * up * logistic * (1.0 + gate * (1.0 - logistic))).astype(BF)
        up_o[:, at] = (mixed * silu).astype(BF)

    wide = width // 2

    @pl.loop(0, width // wide)
    def _(j):
        at = pl.ds(pl.multiple_of(j * wide, wide), wide)
        back = lax.dot_general(gate_o[...], wg_s[at, :], NT, preferred_element_type=F32)
        back += lax.dot_general(up_o[...], wu_s[at, :], NT, preferred_element_type=F32)
        back = back.astype(BF)
        for d in range(inner):
            backs[d][:, at] = back[d * rows : (d + 1) * rows]

    lane = lax.broadcasted_iota(jnp.int32, (count, LANES), 1)
    comb = jnp.where(lane == info[plan.cands], comb_s[...], 0.0).astype(BF)
    for d in range(inner):
        backs[d][:, width:] = comb[d * rows : (d + 1) * rows]


def weight_kernel(plan, own, *refs):
    inner, width, hidden = plan.inner, plan.width, plan.hidden
    part, n = hidden // 2, plan.inner * PARTS
    got, mids = refs[:n], refs[n : n + 6]
    at = n + 6
    theirs = refs[at : at + 3] if own else None
    at += 3 if own else 0
    outs = refs[at : at + 3]
    x_s, d_s, h_s, gu_s, g_s, u_s, w_s, sems, mid_sems, out_sems = refs[at + 3 : at + 13]
    kept = refs[at + 13 :]
    first, second, base, taken = [], [], 0, 0
    half = pl.ds(0 if own else part, part)
    for g in range(2):
        many = inner * len(plan.groups[g])
        mine = got[taken : taken + many]
        at_sems = sems.at[pl.ds(2 * taken, 2 * many)]
        x_copies, d_copies = pieces(plan, g, mine, x_s, d_s, at_sems, base)
        first += x_copies
        second += d_copies
        to = pl.ds(base, inner * plan.sizes[g])
        spots = (h_s.at[to], gu_s.at[to, pl.ds(0, part)], gu_s.at[to, pl.ds(part, part)])
        for i, (m, s) in enumerate(zip(mids[3 * g : 3 * g + 3], spots)):
            copy = pltpu.make_async_copy(m.at[:, half], s, mid_sems.at[3 * g + i])
            (second if i == 0 else first).append(copy)
        taken += many
        base += inner * plan.sizes[g]
    came = []
    if own:
        came = [
            pltpu.make_async_copy(t.at[0], k, out_sems.at[5 + i])
            for i, (t, k) in enumerate(zip(theirs, kept))
        ]
    for c in first + came[:2] + second + came[2:]:
        c.start()
    for c in first + came[:2]:
        c.wait()
    tile, left = width // 2, []
    for j in range(2):
        to = slice(j * tile, (j + 1) * tile)
        both = lax.dot_general(x_s[:, to], gu_s[...], TN, preferred_element_type=F32)
        for i, (o, s) in enumerate(zip(outs, (g_s, u_s))):
            value = both[:, i * part : (i + 1) * part]
            if own:
                value += kept[i][to, :].astype(F32)
            s[to, :] = value.astype(BF)
            rows = pl.ds(j * tile, tile)
            left.append(
                pltpu.make_async_copy(s.at[rows], o.at[0, rows], out_sems.at[2 * j + i])
            )
            left[-1].start()
    for c in second + came[2:]:
        c.wait()
    down = lax.dot_general(h_s[...], d_s[...], TN, preferred_element_type=F32)
    if own:
        down += kept[2][...].astype(F32)
    w_s[...] = down.astype(BF)
    left.append(pltpu.make_async_copy(w_s, outs[2].at[0], out_sems.at[4]))
    left[-1].start()
    for c in left:
        c.wait()


def spread_kernel(plan, homes, groups, *refs):
    inner, tok, width = plan.inner, plan.tok, plan.width
    info, key_ref = refs[:2]
    blocks = refs[2 : 2 + plan.cands]
    at = 2 + plan.cands
    backs = refs[at : at + groups * inner]
    outs = refs[-5 - len(homes) : -5]
    held, metas, pick_s, sems, meta_sems = refs[-5:]
    copies, later, start = [], [], 0
    for i, b in enumerate(blocks):
        copies.append(
            pltpu.make_async_copy(b.at[:, pl.ds(2 * width, LANES)], metas.at[i], meta_sems.at[i])
        )
    for i, b in enumerate(backs):
        rows = plan.sizes[i // inner]
        later.append(pltpu.make_async_copy(b, held.at[pl.ds(start, rows)], sems.at[i]))
        start += rows
    for c in copies + later:
        c.start()
    for c in copies:
        c.wait()
    experts = [info[plan.cands + d] for d in range(inner)]
    for i, r in enumerate(homes):
        which = info[plan.cands + inner + r]
        meta = metas[which].astype(F32)
        one, _ = picks(plan, meta, info[which], experts, key_ref[...], False)
        pick_s[i * tok : (i + 1) * tok, :] = one.astype(BF)
    for c in later:
        c.wait()
    sums = jnp.dot(pick_s[...], held[...], preferred_element_type=F32).astype(BF)
    for i in range(len(homes)):
        outs[i][...] = sums[i * tok : (i + 1) * tok]


def add_kernel(a_ref, b_ref, o_ref):
    o_ref[...] = (a_ref[...].astype(F32) + b_ref[...].astype(F32)).astype(BF)


def home_kernel(plan, count, *refs):
    parts = refs[:count]
    routes_ref, comb_ref, _, tok_o, comb_o = refs[count:]
    width, tok = plan.width, plan.tok
    total = parts[0][...].astype(F32)
    for p in parts[1:]:
        total += p[...].astype(F32)
    tok_o[...] = total[:, :width].astype(BF)
    row = lax.broadcasted_iota(jnp.int32, (LANES, LANES), 0)
    col = lax.broadcasted_iota(jnp.int32, (LANES, LANES), 1)
    same = jnp.where(row == col, 1.0, 0.0).astype(BF)
    found = total[:, width:].astype(BF)
    found = lax.dot_general(same, found, NT, preferred_element_type=F32)
    kind = lax.broadcasted_iota(jnp.int32, (LANES, tok), 0)
    out = []
    for k in range(plan.top):
        mine = jnp.where(kind == routes_ref[k : k + 1, :], found, 0.0)
        out.append(jnp.sum(mine, axis=0, keepdims=True))
    out = jnp.concatenate(out, axis=0)
    comb_o[...] = (out / comb_ref[...].astype(F32)).astype(BF)


def on_device(plan, tokens, routes, combine, upstream, w_gate, w_up, w_down):
    tok, width, hidden = plan.tok, plan.width, plan.hidden
    inner, outer, part = plan.inner, plan.outer, plan.hidden // 2
    full = 2 * width + LANES
    shape = jax.ShapeDtypeStruct
    info = jnp.asarray(plan.table())[lax.axis_index("expert")]
    swap = [(0, 1), (1, 0)]

    block = pl.pallas_call(
        functools.partial(pack_kernel, plan),
        out_shape=shape((tok, full), BF),
        in_specs=[VMEM] * 4,
        out_specs=VMEM,
        compiler_params=params(),
        cost_estimate=cost(1e6, 4 * tok * full),
        name="pack",
    )(tokens, upstream, routes.T, combine.T)

    gate_up = jnp.concatenate([w_gate, w_up], axis=2)
    blocks = [block] * plan.cands

    def hop(r):
        for chain in (0, 1):
            if r <= plan.last[chain]:
                i = chain * (outer - 1) + r
                before = block if r == 1 else blocks[i - 1]
                blocks[i] = lax.ppermute(before, "expert", plan.exchange(r, chain))
        if 1 < r <= min(plan.last):
            i = outer - 1 + r
            blocks[r], blocks[i] = lax.optimization_barrier((blocks[r], blocks[i]))

    hop(1)
    def compact(c):
        rows, use = plan.rows[c], plan.use[c]
        count, n = inner * rows, len(use)
        return pl.pallas_call(
            functools.partial(compact_kernel, plan, c),
            out_shape=[shape((2 * rows, width), BF)] * inner,
            in_specs=[SMEM, VMEM] + [ANY] * n,
            out_specs=[VMEM] * inner,
            scratch_shapes=[
                pltpu.VMEM((n * tok, full), BF),
                pltpu.VMEM((n * tok, count), BF),
                pltpu.VMEM((n * tok, count), BF),
                pltpu.SemaphoreType.DMA((n,)),
            ],
            compiler_params=params(),
            cost_estimate=cost(4 * n * tok * count * width, 2 * n * tok * full),
            name="compact",
        )(info, jnp.asarray(plan.keys([plan.chunks[c]])), *[blocks[i] for i in use])

    def expert(g, arrived):
        rows, n = plan.sizes[g], inner * len(plan.groups[g])
        count = inner * rows
        return pl.pallas_call(
            functools.partial(expert_kernel, plan, g),
            out_shape=[shape((count, hidden), BF)] * 3
            + [shape((rows, width + LANES), BF)] * inner,
            in_specs=[SMEM] + [ANY] * (n + 5),
            out_specs=[VMEM] * (3 + inner),
            scratch_shapes=[
                pltpu.VMEM((count, width), BF),
                pltpu.VMEM((count, width), BF),
                pltpu.VMEM((width, hidden), BF),
                pltpu.VMEM((width, hidden), BF),
                pltpu.VMEM((hidden, width), BF),
                pltpu.VMEM((count, 1), F32),
                pltpu.SemaphoreType.DMA((2 * n + 6 * (hidden // 128),)),
            ],
            compiler_params=params(),
            cost_estimate=cost(10 * count * hidden * width, 6 * hidden * width),
            name="expert",
        )(info, *arrived, *weights)

    def cross(arrays):
        return [arrays[0]] + [
            lax.ppermute(arrays[d], "expert", plan.across(d)) for d in range(1, inner)
        ]

    got, done = [], 1
    for c in range(PARTS):
        for r in range(done + 1, plan.steps[c] + 1):
            hop(r)
        done = max(done, plan.steps[c])
        sent = compact(c)
        i = outer - 1 + done
        if c == 1:
            got[0], sent, blocks[done], blocks[i] = lax.optimization_barrier(
                (got[0], sent, blocks[done], blocks[i])
            )
        elif c > 1:
            got[-1], sent = lax.optimization_barrier((got[-1], sent))
        if c == PARTS - 2:
            gate_up, sent = lax.optimization_barrier((gate_up, sent))
            gate_up = lax.ppermute(gate_up, "dp", swap)
        if c == PARTS - 1:
            gate_up, sent = lax.optimization_barrier((gate_up, sent))
            down = lax.ppermute(lax.optimization_barrier((w_down, sent))[0], "dp", swap)
        got.append(cross(sent))
    weights = [w_gate, w_up, w_down, gate_up, down]
    outs = expert(0, sum(got[:-1], []))
    late = got[-1]
    got[-1] = late
    backs = cross(outs[3:])
    more = expert(1, late)
    got = sum(got, [])
    mids = outs[:3] + more[:3]

    count = inner * sum(plan.rows)

    grad_scratch = [
        pltpu.VMEM((width, part), BF),
        pltpu.VMEM((width, part), BF),
        pltpu.VMEM((part, width), BF),
    ]

    def weight_grads(own, extra):
        return pl.pallas_call(
            functools.partial(weight_kernel, plan, own),
            out_shape=[
                shape((1, width, part), BF),
                shape((1, width, part), BF),
                shape((1, part, width), BF),
            ],
            in_specs=[ANY] * (inner * PARTS + 6 + len(extra)),
            out_specs=[ANY] * 3,
            scratch_shapes=[
                pltpu.VMEM((count, width), BF),
                pltpu.VMEM((count, width), BF),
                pltpu.VMEM((count, part), BF),
                pltpu.VMEM((count, 2 * part), BF),
                *grad_scratch,
                pltpu.SemaphoreType.DMA((2 * inner * PARTS,)),
                pltpu.SemaphoreType.DMA((6,)),
                pltpu.SemaphoreType.DMA((8,)),
                *(grad_scratch if own else []),
            ],
            compiler_params=params(),
            cost_estimate=cost(6 * count * part * width, 4 * count * (width + hidden)),
            name="weight_grads",
        )(*got, *mids, *extra)

    def spread(homes, groups, extra):
        slots = inner * sum(plan.sizes[:groups])
        return pl.pallas_call(
            functools.partial(spread_kernel, plan, homes, groups),
            out_shape=[shape((tok, width + LANES), BF)] * len(homes),
            in_specs=[SMEM, VMEM] + [ANY] * (plan.cands + groups * inner + len(extra)),
            out_specs=[VMEM] * len(homes),
            scratch_shapes=[
                pltpu.VMEM((slots, width + LANES), BF),
                pltpu.VMEM((plan.cands, tok, LANES), BF),
                pltpu.VMEM((len(homes) * tok, slots), BF),
                pltpu.SemaphoreType.DMA((groups * inner,)),
                pltpu.SemaphoreType.DMA((plan.cands,)),
            ],
            compiler_params=params(),
            cost_estimate=cost(2 * len(homes) * tok * slots * width, 2 * slots * width),
            name="spread",
        )(
            info,
            jnp.asarray(plan.keys(plan.spans[:groups])),
            *blocks,
            *backs[: groups * inner],
            *extra,
        )

    mine = weight_grads(False, [])
    backs = backs + cross(more[3:])
    (first,) = spread([1], 1, [])
    sums = {}
    mine, backs, first = lax.optimization_barrier((mine, backs, first))
    came = [lax.ppermute(first, "expert", plan.flip(1))]
    theirs = [lax.ppermute(w, "dp", swap) for w in mine]
    rest = [r for r in range(outer) if r != 1]
    sums.update(zip(rest, spread(rest, 2, [mine[0], first])))
    bit = 1
    while bit < outer:
        for r in range(bit, outer, 2 * bit):
            if r == 1:
                continue
            sent = lax.ppermute(sums[r], "expert", plan.flip(bit))
            if r == bit:
                came.append(sent)
            else:
                sums[r - bit] = pl.pallas_call(
                    add_kernel,
                    out_shape=shape((tok, width + LANES), BF),
                    in_specs=[VMEM] * 2,
                    out_specs=VMEM,
                    name="add",
                )(sums[r - bit], sent)
        bit *= 2
    grads = weight_grads(True, theirs)
    home = [sums[0]] + came
    grad_tokens, grad_combine = pl.pallas_call(
        functools.partial(home_kernel, plan, len(home)),
        out_shape=[shape((tok, width), BF), shape((plan.top, tok), BF)],
        in_specs=[VMEM] * (len(home) + 2) + [ANY],
        out_specs=[VMEM] * 2,
        compiler_params=params(),
        cost_estimate=cost(1e6, 2 * tok * width * (outer + 1)),
        name="home",
    )(*home, routes.T, combine.T, grads[0])
    return (grad_tokens, grad_combine.T, *grads)


def solution(mesh):
    rows = P(("parts", "dp", "expert"), None)
    in_specs = (rows,) * 4 + (P("expert", None, "dp"),) * 2 + (P("expert", "dp", None),)
    out_specs = (rows,) * 2 + (P(("parts", "expert"), None, "dp"),) * 2
    out_specs += (P(("parts", "expert"), "dp", None),)
    shape = dict(mesh.shape)

    def whole(tokens, routes, combine, upstream, w_gate, w_up, w_down):
        devices = shape["parts"] * shape["dp"] * shape["expert"]
        plan = Plan(
            shape["expert"],
            tokens.shape[0] // devices,
            routes.shape[1],
            tokens.shape[1],
            w_gate.shape[2],
        )
        body = functools.partial(on_device, plan)
        return jax.shard_map(
            body, mesh=mesh, in_specs=in_specs, out_specs=out_specs, check_vma=False
        )(tokens, routes, combine, upstream, w_gate, w_up, w_down)

    return whole
```

```python
import functools

import jax
import jax.numpy as jnp
import numpy as np
from jax import lax
from jax.experimental import pallas as pl
from jax.experimental.pallas import tpu as pltpu
from jax.sharding import PartitionSpec as P

BF = jnp.bfloat16
F32 = jnp.float32
LANES = 128
HALF = 64
STRIDE = 1024
PARTS = 4
NOWHERE = -(1 << 20)
ANY = pl.BlockSpec(memory_space=pltpu.HBM)
VMEM = pl.BlockSpec(memory_space=pltpu.VMEM)
SMEM = pl.BlockSpec(memory_space=pltpu.SMEM)
TN = (((0,), (0,)), ((), ()))
NT = (((1,), (1,)), ((), ()))


def params(megabytes=60):
    return pltpu.CompilerParams(vmem_limit_bytes=megabytes << 20)


def cost(flops, moved):
    return pl.CostEstimate(flops=int(flops), bytes_accessed=int(moved), transcendentals=0)


class Plan:
    def __init__(self, experts, tok, top, width, hidden):
        self.experts, self.tok, self.top = experts, tok, top
        self.width, self.hidden = width, hidden
        outer = 1
        while outer * outer < experts:
            outer *= 2
        self.outer, self.inner = outer, experts // outer
        mean = tok * top // experts
        self.cap = min(tok, max(2, mean + tok * top // (8 * experts)))
        total = -(-self.outer * self.cap // 16) * 16
        step = self.outer // PARTS
        marks = [k * step * self.cap // 16 * 16 for k in range(PARTS)] + [total]
        if marks[1] >= 32:
            marks[1] = marks[1] // 32 * 16
            marks[2] = marks[1] + 32
        self.chunks = [(marks[k], marks[k + 1]) for k in range(PARTS)]
        self.rows = [b - a for a, b in self.chunks]
        self.steps = [(k + 1) * step - 1 for k in range(PARTS)]
        self.groups = [range(PARTS - 1), range(PARTS - 1, PARTS)]
        self.spans = [(marks[g[0]], marks[g[-1] + 1]) for g in self.groups]
        self.sizes = [b - a for a, b in self.spans]
        self.cands = 2 * self.outer - 1
        self.use = [self.used(*c) for c in self.chunks]
        needed = set().union(*self.use)
        self.last = [
            max(i for i in needed if 0 < i < outer),
            max(i for i in needed if i >= outer) - outer + 1,
        ]

    def keys(self, spans):
        return np.array(
            [[d * STRIDE + q for a, b in spans for d in range(self.inner) for q in range(a, b)]],
            np.int32,
        )

    def order(self, z):
        rest = [s for s in range(self.outer) if s not in (z, z ^ 1)]
        return [z, z ^ 1] + sorted(rest, key=lambda s: abs(s - z))

    def swap(self, z, odd):
        to = z - 1 if (z % 2 == 0) == odd else z + 1
        return to if 0 <= to < self.outer else z

    def trace(self):
        held = {0: list(range(self.outer))}
        for chain in (0, 1):
            last = held[0]
            for r in range(1, self.outer):
                odd = (r % 2 == 0) == (chain == 0)
                last = [last[self.swap(z, odd)] for z in range(self.outer)]
                held[chain * (self.outer - 1) + r] = last
        return held

    def cand(self, z, source):
        step = lambda i: i if i < self.outer else i - self.outer + 1
        found = [i for i, held in self.trace().items() if held[z] == source]
        return min(found, key=lambda i: (step(i), i))

    def exchange(self, r, chain):
        odd = (r % 2 == 0) == (chain == 0)
        return [
            (z * self.inner + p, self.swap(z, odd) * self.inner + p)
            for z in range(self.outer)
            for p in range(self.inner)
        ]

    def used(self, a, b):
        slots = [k for k in range(self.outer) if k * self.cap < b and (k + 1) * self.cap > a]
        return sorted(
            {self.cand(z, self.order(z)[k]) for z in range(self.outer) for k in slots}
        )

    def partner(self, p, d):
        return p ^ d if self.inner & (self.inner - 1) == 0 else (d - p) % self.inner

    def table(self):
        rows = []
        for e in range(self.experts):
            z, p = divmod(e, self.inner)
            offs = [NOWHERE] * self.cands
            for slot, source in enumerate(self.order(z)):
                offs[self.cand(z, source)] = slot * self.cap
            experts = [z * self.inner + self.partner(p, d) for d in range(self.inner)]
            homes = [self.cand(z, z ^ r) for r in range(self.outer)]
            rows.append(offs + experts + homes)
        return np.array(rows, np.int32)

    def across(self, d):
        return [
            (z * self.inner + p, z * self.inner + self.partner(p, d))
            for z in range(self.outer)
            for p in range(self.inner)
        ]

    def flip(self, r):
        return [
            (z * self.inner + p, (z ^ r) * self.inner + p)
            for z in range(self.outer)
            for p in range(self.inner)
        ]


def pack_kernel(plan, tok_ref, up_ref, routes_ref, comb_ref, out_ref):
    tok, width = plan.tok, plan.width
    out_ref[:, :width] = tok_ref[...]
    out_ref[:, width : 2 * width] = up_ref[...]
    kind = lax.broadcasted_iota(jnp.int32, (LANES, tok), 0)
    weight = jnp.zeros((LANES, tok), F32)
    named = jnp.zeros((LANES, tok), F32)
    comb = comb_ref[...].astype(F32)
    for k in range(plan.top):
        e = routes_ref[k : k + 1, :]
        weight = jnp.where(kind == e, comb[k : k + 1, :], weight)
        named = jnp.where(kind == e + HALF, 1.0, named)
    row = lax.broadcasted_iota(jnp.int32, (tok, tok), 0)
    col = lax.broadcasted_iota(jnp.int32, (tok, tok), 1)
    upto = jnp.where(row <= col, 1.0, 0.0).astype(BF)
    count = jnp.dot(named.astype(BF), upto, preferred_element_type=F32)
    table = (weight + count * named).astype(BF)
    same = jnp.where(row == col, 1.0, 0.0).astype(BF)
    turned = lax.dot_general(same, table, NT, preferred_element_type=F32)
    out_ref[:, 2 * width :] = turned.astype(BF)


def picks(plan, meta, off, experts, key, scaled):
    tok = meta.shape[0]
    lane = lax.broadcasted_iota(jnp.int32, (tok, LANES), 1)
    one = jnp.zeros((tok, key.shape[1]), F32)
    two = jnp.zeros((tok, key.shape[1]), F32)
    for d, e in enumerate(experts):
        place = jnp.sum(jnp.where(lane == e + HALF, meta, 0.0), axis=1, keepdims=True)
        place = place.astype(jnp.int32)
        spot = jnp.where(place > 0, place - 1 + off + d * STRIDE, -1)
        hit = spot == key
        one = jnp.where(hit, 1.0, one)
        if scaled:
            weight = jnp.sum(jnp.where(lane == e, meta, 0.0), axis=1, keepdims=True)
            two = jnp.where(hit, weight, two)
    return one, two


def compact_kernel(plan, chunk, *refs):
    use, rows = plan.use[chunk], plan.rows[chunk]
    n, width, tok, inner = len(use), plan.width, plan.tok, plan.inner
    info, key_ref = refs[:2]
    blocks, outs = refs[2 : 2 + n], refs[2 + n : 2 + n + inner]
    held, one_s, two_s, sems = refs[2 + n + inner :]
    copies = [
        pltpu.make_async_copy(b, held.at[pl.ds(i * tok, tok)], sems.at[i])
        for i, b in enumerate(blocks)
    ]
    for c in copies:
        c.start()
    experts = [info[plan.cands + d] for d in range(inner)]
    for i, c in enumerate(copies):
        c.wait()
        meta = held[i * tok : (i + 1) * tok, 2 * width :].astype(F32)
        one, two = picks(plan, meta, info[use[i]], experts, key_ref[...], True)
        one_s[i * tok : (i + 1) * tok, :] = one.astype(BF)
        two_s[i * tok : (i + 1) * tok, :] = two.astype(BF)
    for part, source in ((0, one_s), (1, two_s)):
        have = held[:, part * width : (part + 1) * width]
        found = lax.dot_general(source[...], have, TN, preferred_element_type=F32).astype(BF)
        for d in range(inner):
            outs[d][part * rows : (part + 1) * rows, :] = found[d * rows : (d + 1) * rows]


def pieces(plan, group, got, x_s, d_s, sems, base=0):
    inner, size, first = plan.inner, plan.sizes[group], plan.spans[group][0]
    x_copies, d_copies = [], []
    for i, g in enumerate(got):
        c, d = plan.groups[group][i // inner], i % inner
        rows = plan.rows[c]
        to = pl.ds(base + d * size + plan.chunks[c][0] - first, rows)
        x_copies.append(pltpu.make_async_copy(g.at[pl.ds(0, rows)], x_s.at[to], sems.at[2 * i]))
        d_copies.append(
            pltpu.make_async_copy(g.at[pl.ds(rows, rows)], d_s.at[to], sems.at[2 * i + 1])
        )
    return x_copies, d_copies


def expert_kernel(plan, group, *refs):
    inner, rows, width, hidden = plan.inner, plan.sizes[group], plan.width, plan.hidden
    part, count, n = hidden // 2, inner * rows, inner * len(plan.groups[group])
    info = refs[0]
    got, weights = refs[1 : 1 + n], refs[1 + n : 6 + n]
    hid_o, gate_o, up_o = refs[6 + n : 9 + n]
    backs = refs[9 + n : 9 + n + inner]
    x_s, d_s, wg_s, wu_s, wd_s, comb_s, sems = refs[9 + n + inner :]
    own_g, own_u, own_d, both, other_d = [w.at[0] for w in weights]
    views = [
        (own_g, both.at[:, pl.ds(0, part)]),
        (own_u, both.at[:, pl.ds(part, part)]),
        (own_d, other_d),
    ]
    x_copies, d_copies = pieces(plan, group, got, x_s, d_s, sems)
    tile, tiles = hidden, []
    for t in range(hidden // tile):
        for kind, where in ((0, wg_s), (1, wu_s), (2, wd_s)):
            at, here = t * tile, []
            while at < (t + 1) * tile:
                half, start = divmod(at, part)
                size = min((t + 1) * tile, (half + 1) * part) - at
                source, to = pl.ds(start, size), pl.ds(at, size)
                w = views[kind][half]
                here.append((w.at[source], where.at[to]) if kind == 2 else (w.at[:, source], where.at[:, to]))
                at += size
            tiles.append(here)
    w_copies, used = [], 2 * n
    for here in tiles:
        w_copies.append([])
        for source, to in here:
            w_copies[-1].append(pltpu.make_async_copy(source, to, sems.at[used]))
            used += 1
    for c in x_copies + w_copies[0] + w_copies[1] + d_copies:
        c.start()
    for here in w_copies[2:]:
        for c in here:
            c.start()
    for t in range(hidden // tile):
        at = slice(t * tile, (t + 1) * tile)
        gate_w, up_w, down_w = w_copies[3 * t : 3 * t + 3]
        for c in (x_copies if t == 0 else []) + gate_w:
            c.wait()
        gate = jnp.dot(x_s[...], wg_s[:, at], preferred_element_type=F32)
        for c in up_w:
            c.wait()
        up = jnp.dot(x_s[...], wu_s[:, at], preferred_element_type=F32)
        for c in (d_copies if t == 0 else []) + down_w:
            c.wait()
        mixed = lax.dot_general(d_s[...], wd_s[at, :], NT, preferred_element_type=F32)
        logistic = jax.nn.sigmoid(gate)
        silu = gate * logistic
        hid = (silu * up).astype(BF)
        hid_o[:, at] = hid
        comb = jnp.sum(hid.astype(F32) * mixed, axis=1, keepdims=True)
        comb_s[...] = comb if t == 0 else comb_s[...] + comb
        gate_o[:, at] = (mixed * up * logistic * (1.0 + gate * (1.0 - logistic))).astype(BF)
        up_o[:, at] = (mixed * silu).astype(BF)

    wide = width // 2

    @pl.loop(0, width // wide)
    def _(j):
        at = pl.ds(pl.multiple_of(j * wide, wide), wide)
        back = lax.dot_general(gate_o[...], wg_s[at, :], NT, preferred_element_type=F32)
        back += lax.dot_general(up_o[...], wu_s[at, :], NT, preferred_element_type=F32)
        back = back.astype(BF)
        for d in range(inner):
            backs[d][:, at] = back[d * rows : (d + 1) * rows]

    lane = lax.broadcasted_iota(jnp.int32, (count, LANES), 1)
    comb = jnp.where(lane == info[plan.cands], comb_s[...], 0.0).astype(BF)
    for d in range(inner):
        backs[d][:, width:] = comb[d * rows : (d + 1) * rows]


def weight_kernel(plan, own, extra, *refs):
    inner, width, hidden = plan.inner, plan.width, plan.hidden
    part, n = hidden // 2, plan.inner * PARTS
    got, mids = refs[:n], refs[n : n + 6]
    at = n + 6
    theirs = refs[at : at + 3] if own else None
    at += extra
    outs = refs[at : at + 3]
    x_s, d_s, h_s, gu_s, g_s, u_s, w_s, sems, mid_sems, out_sems = refs[at + 3 : at + 13]
    kept = refs[at + 13 :]
    first, second, base, taken = [], [], 0, 0
    half = pl.ds(0 if own else part, part)
    for g in range(2):
        many = inner * len(plan.groups[g])
        mine = got[taken : taken + many]
        at_sems = sems.at[pl.ds(2 * taken, 2 * many)]
        x_copies, d_copies = pieces(plan, g, mine, x_s, d_s, at_sems, base)
        first += x_copies
        second += d_copies
        to = pl.ds(base, inner * plan.sizes[g])
        spots = (h_s.at[to], gu_s.at[to, pl.ds(0, part)], gu_s.at[to, pl.ds(part, part)])
        for i, (m, s) in enumerate(zip(mids[3 * g : 3 * g + 3], spots)):
            copy = pltpu.make_async_copy(m.at[:, half], s, mid_sems.at[3 * g + i])
            (second if i == 0 else first).append(copy)
        taken += many
        base += inner * plan.sizes[g]
    came = []
    if own:
        came = [
            pltpu.make_async_copy(t.at[0], k, out_sems.at[5 + i])
            for i, (t, k) in enumerate(zip(theirs, kept))
        ]
    for c in first + came[:2] + second + came[2:]:
        c.start()
    for c in first + came[:2]:
        c.wait()
    tile, left = width // 2, []
    for j in range(2):
        to = slice(j * tile, (j + 1) * tile)
        both = lax.dot_general(x_s[:, to], gu_s[...], TN, preferred_element_type=F32)
        for i, (o, s) in enumerate(zip(outs, (g_s, u_s))):
            value = both[:, i * part : (i + 1) * part]
            if own:
                value += kept[i][to, :].astype(F32)
            s[to, :] = value.astype(BF)
            rows = pl.ds(j * tile, tile)
            left.append(
                pltpu.make_async_copy(s.at[rows], o.at[0, rows], out_sems.at[2 * j + i])
            )
            left[-1].start()
    for c in second + came[2:]:
        c.wait()
    down = lax.dot_general(h_s[...], d_s[...], TN, preferred_element_type=F32)
    if own:
        down += kept[2][...].astype(F32)
    w_s[...] = down.astype(BF)
    left.append(pltpu.make_async_copy(w_s, outs[2].at[0], out_sems.at[4]))
    left[-1].start()
    for c in left:
        c.wait()


def spread_kernel(plan, homes, groups, *refs):
    inner, tok, width = plan.inner, plan.tok, plan.width
    info, key_ref = refs[:2]
    blocks = refs[2 : 2 + plan.cands]
    at = 2 + plan.cands
    backs = refs[at : at + groups * inner]
    outs = refs[-5 - len(homes) : -5]
    held, metas, pick_s, sems, meta_sems = refs[-5:]
    copies, later, start = [], [], 0
    for i, b in enumerate(blocks):
        copies.append(
            pltpu.make_async_copy(b.at[:, pl.ds(2 * width, LANES)], metas.at[i], meta_sems.at[i])
        )
    for i, b in enumerate(backs):
        rows = plan.sizes[i // inner]
        later.append(pltpu.make_async_copy(b, held.at[pl.ds(start, rows)], sems.at[i]))
        start += rows
    for c in copies + later:
        c.start()
    for c in copies:
        c.wait()
    experts = [info[plan.cands + d] for d in range(inner)]
    for i, r in enumerate(homes):
        which = info[plan.cands + inner + r]
        meta = metas[which].astype(F32)
        one, _ = picks(plan, meta, info[which], experts, key_ref[...], False)
        pick_s[i * tok : (i + 1) * tok, :] = one.astype(BF)
    for c in later:
        c.wait()
    sums = jnp.dot(pick_s[...], held[...], preferred_element_type=F32).astype(BF)
    for i in range(len(homes)):
        outs[i][...] = sums[i * tok : (i + 1) * tok]


def add_kernel(a_ref, b_ref, o_ref):
    o_ref[...] = (a_ref[...].astype(F32) + b_ref[...].astype(F32)).astype(BF)


def home_kernel(plan, count, *refs):
    parts = refs[:count]
    routes_ref, comb_ref, _, tok_o, comb_o = refs[count:]
    width, tok = plan.width, plan.tok
    total = parts[0][...].astype(F32)
    for p in parts[1:]:
        total += p[...].astype(F32)
    tok_o[...] = total[:, :width].astype(BF)
    row = lax.broadcasted_iota(jnp.int32, (LANES, LANES), 0)
    col = lax.broadcasted_iota(jnp.int32, (LANES, LANES), 1)
    same = jnp.where(row == col, 1.0, 0.0).astype(BF)
    found = total[:, width:].astype(BF)
    found = lax.dot_general(same, found, NT, preferred_element_type=F32)
    kind = lax.broadcasted_iota(jnp.int32, (LANES, tok), 0)
    out = []
    for k in range(plan.top):
        mine = jnp.where(kind == routes_ref[k : k + 1, :], found, 0.0)
        out.append(jnp.sum(mine, axis=0, keepdims=True))
    out = jnp.concatenate(out, axis=0)
    comb_o[...] = (out / comb_ref[...].astype(F32)).astype(BF)


def on_device(plan, tokens, routes, combine, upstream, w_gate, w_up, w_down):
    tok, width, hidden = plan.tok, plan.width, plan.hidden
    inner, outer, part = plan.inner, plan.outer, plan.hidden // 2
    full = 2 * width + LANES
    shape = jax.ShapeDtypeStruct
    info = jnp.asarray(plan.table())[lax.axis_index("expert")]
    swap = [(0, 1), (1, 0)]

    block = pl.pallas_call(
        functools.partial(pack_kernel, plan),
        out_shape=shape((tok, full), BF),
        in_specs=[VMEM] * 4,
        out_specs=VMEM,
        compiler_params=params(),
        cost_estimate=cost(1e6, 4 * tok * full),
        name="pack",
    )(tokens, upstream, routes.T, combine.T)

    gate_up = jnp.concatenate([w_gate, w_up], axis=2)
    blocks = [block] * plan.cands

    def hop(r):
        for chain in (0, 1):
            if r <= plan.last[chain]:
                i = chain * (outer - 1) + r
                before = block if r == 1 else blocks[i - 1]
                blocks[i] = lax.ppermute(before, "expert", plan.exchange(r, chain))
        if 1 < r <= min(plan.last):
            i = outer - 1 + r
            blocks[r], blocks[i] = lax.optimization_barrier((blocks[r], blocks[i]))

    hop(1)
    def compact(c):
        rows, use = plan.rows[c], plan.use[c]
        count, n = inner * rows, len(use)
        return pl.pallas_call(
            functools.partial(compact_kernel, plan, c),
            out_shape=[shape((2 * rows, width), BF)] * inner,
            in_specs=[SMEM, VMEM] + [ANY] * n,
            out_specs=[VMEM] * inner,
            scratch_shapes=[
                pltpu.VMEM((n * tok, full), BF),
                pltpu.VMEM((n * tok, count), BF),
                pltpu.VMEM((n * tok, count), BF),
                pltpu.SemaphoreType.DMA((n,)),
            ],
            compiler_params=params(),
            cost_estimate=cost(4 * n * tok * count * width, 2 * n * tok * full),
            name="compact",
        )(info, jnp.asarray(plan.keys([plan.chunks[c]])), *[blocks[i] for i in use])

    def expert(g, arrived):
        rows, n = plan.sizes[g], inner * len(plan.groups[g])
        count = inner * rows
        return pl.pallas_call(
            functools.partial(expert_kernel, plan, g),
            out_shape=[shape((count, hidden), BF)] * 3
            + [shape((rows, width + LANES), BF)] * inner,
            in_specs=[SMEM] + [ANY] * (n + 5),
            out_specs=[VMEM] * (3 + inner),
            scratch_shapes=[
                pltpu.VMEM((count, width), BF),
                pltpu.VMEM((count, width), BF),
                pltpu.VMEM((width, hidden), BF),
                pltpu.VMEM((width, hidden), BF),
                pltpu.VMEM((hidden, width), BF),
                pltpu.VMEM((count, 1), F32),
                pltpu.SemaphoreType.DMA((2 * n + 6 * (hidden // 128),)),
            ],
            compiler_params=params(),
            cost_estimate=cost(10 * count * hidden * width, 6 * hidden * width),
            name="expert",
        )(info, *arrived, *weights)

    def cross(arrays):
        return [arrays[0]] + [
            lax.ppermute(arrays[d], "expert", plan.across(d)) for d in range(1, inner)
        ]

    got, done = [], 1
    for c in range(PARTS):
        for r in range(done + 1, plan.steps[c] + 1):
            hop(r)
        done = max(done, plan.steps[c])
        sent = compact(c)
        if c > 0:
            got[-1], sent = lax.optimization_barrier((got[-1], sent))
        if c == PARTS - 2:
            gate_up, sent = lax.optimization_barrier((gate_up, sent))
            gate_up = lax.ppermute(gate_up, "dp", swap)
        if c == PARTS - 1:
            gate_up, sent = lax.optimization_barrier((gate_up, sent))
            down = lax.ppermute(lax.optimization_barrier((w_down, sent))[0], "dp", swap)
        got.append(cross(sent))
        if c == 0:
            i = outer - 1 + done
            got[0], blocks[done], blocks[i] = lax.optimization_barrier(
                (got[0], blocks[done], blocks[i])
            )
    weights = [w_gate, w_up, w_down, gate_up, down]
    outs = expert(0, sum(got[:-1], []))
    outs = list(outs)
    outs[0], late = lax.optimization_barrier((outs[0], got[-1]))
    got[-1] = late
    backs = cross(outs[3:])
    more = expert(1, late)
    got = sum(got, [])
    mids = outs[:3] + list(more[:3])

    count = inner * sum(plan.rows)

    grad_scratch = [
        pltpu.VMEM((width, part), BF),
        pltpu.VMEM((width, part), BF),
        pltpu.VMEM((part, width), BF),
    ]

    def weight_grads(own, extra):
        return pl.pallas_call(
            functools.partial(weight_kernel, plan, own, len(extra)),
            out_shape=[
                shape((1, width, part), BF),
                shape((1, width, part), BF),
                shape((1, part, width), BF),
            ],
            in_specs=[ANY] * (inner * PARTS + 6 + len(extra)),
            out_specs=[ANY] * 3,
            scratch_shapes=[
                pltpu.VMEM((count, width), BF),
                pltpu.VMEM((count, width), BF),
                pltpu.VMEM((count, part), BF),
                pltpu.VMEM((count, 2 * part), BF),
                *grad_scratch,
                pltpu.SemaphoreType.DMA((2 * inner * PARTS,)),
                pltpu.SemaphoreType.DMA((6,)),
                pltpu.SemaphoreType.DMA((8,)),
                *(grad_scratch if own else []),
            ],
            compiler_params=params(),
            cost_estimate=cost(6 * count * part * width, 4 * count * (width + hidden)),
            name="weight_grads",
        )(*got, *mids, *extra)

    def spread(homes, groups, extra):
        slots = inner * sum(plan.sizes[:groups])
        return pl.pallas_call(
            functools.partial(spread_kernel, plan, homes, groups),
            out_shape=[shape((tok, width + LANES), BF)] * len(homes),
            in_specs=[SMEM, VMEM] + [ANY] * (plan.cands + groups * inner + len(extra)),
            out_specs=[VMEM] * len(homes),
            scratch_shapes=[
                pltpu.VMEM((slots, width + LANES), BF),
                pltpu.VMEM((plan.cands, tok, LANES), BF),
                pltpu.VMEM((len(homes) * tok, slots), BF),
                pltpu.SemaphoreType.DMA((groups * inner,)),
                pltpu.SemaphoreType.DMA((plan.cands,)),
            ],
            compiler_params=params(),
            cost_estimate=cost(2 * len(homes) * tok * slots * width, 2 * slots * width),
            name="spread",
        )(
            info,
            jnp.asarray(plan.keys(plan.spans[:groups])),
            *blocks,
            *backs[: groups * inner],
            *extra,
        )

    mine = weight_grads(False, backs[1:inner])
    backs = backs + cross(more[3:])
    mine, backs = lax.optimization_barrier((mine, backs))
    theirs = [lax.ppermute(w, "dp", swap) for w in mine]
    sums = dict(enumerate(spread(list(range(outer)), 2, [mine[0]])))
    came, bit = [], 1
    while bit < outer:
        for r in range(outer - bit, 0, -2 * bit):
            sent = lax.ppermute(sums[r], "expert", plan.flip(bit))
            if r == bit:
                came.append(sent)
                continue
            if bit == 1:
                sums[1], sent = lax.optimization_barrier((sums[1], sent))
            sums[r - bit] = pl.pallas_call(
                add_kernel,
                out_shape=shape((tok, width + LANES), BF),
                in_specs=[VMEM] * 2,
                out_specs=VMEM,
                name="add",
            )(sums[r - bit], sent)
        bit *= 2
    grads = weight_grads(True, theirs)
    home = [sums[0]] + came
    grad_tokens, grad_combine = pl.pallas_call(
        functools.partial(home_kernel, plan, len(home)),
        out_shape=[shape((tok, width), BF), shape((plan.top, tok), BF)],
        in_specs=[VMEM] * (len(home) + 2) + [ANY],
        out_specs=[VMEM] * 2,
        compiler_params=params(),
        cost_estimate=cost(1e6, 2 * tok * width * (outer + 1)),
        name="home",
    )(*home, routes.T, combine.T, grads[0])
    return (grad_tokens, grad_combine.T, *grads)


def solution(mesh):
    rows = P(("parts", "dp", "expert"), None)
    in_specs = (rows,) * 4 + (P("expert", None, "dp"),) * 2 + (P("expert", "dp", None),)
    out_specs = (rows,) * 2 + (P(("parts", "expert"), None, "dp"),) * 2
    out_specs += (P(("parts", "expert"), "dp", None),)
    shape = dict(mesh.shape)

    def whole(tokens, routes, combine, upstream, w_gate, w_up, w_down):
        devices = shape["parts"] * shape["dp"] * shape["expert"]
        plan = Plan(
            shape["expert"],
            tokens.shape[0] // devices,
            routes.shape[1],
            tokens.shape[1],
            w_gate.shape[2],
        )
        body = functools.partial(on_device, plan)
        return jax.shard_map(
            body, mesh=mesh, in_specs=in_specs, out_specs=out_specs, check_vma=False
        )(tokens, routes, combine, upstream, w_gate, w_up, w_down)

    return whole
```

```python
import functools

import jax
import jax.numpy as jnp
import numpy as np
from jax import lax
from jax.experimental import pallas as pl
from jax.experimental.pallas import tpu as pltpu
from jax.sharding import PartitionSpec as P

BF = jnp.bfloat16
F32 = jnp.float32
LANES = 128
HALF = 64
STRIDE = 1024
PARTS = 4
NOWHERE = -(1 << 20)
ANY = pl.BlockSpec(memory_space=pltpu.HBM)
VMEM = pl.BlockSpec(memory_space=pltpu.VMEM)
SMEM = pl.BlockSpec(memory_space=pltpu.SMEM)
TN = (((0,), (0,)), ((), ()))
NT = (((1,), (1,)), ((), ()))


def params(megabytes=64):
    return pltpu.CompilerParams(vmem_limit_bytes=megabytes << 20)


def cost(flops, moved):
    return pl.CostEstimate(flops=int(flops), bytes_accessed=int(moved), transcendentals=0)


class Plan:
    def __init__(self, experts, tok, top, width, hidden):
        self.experts, self.tok, self.top = experts, tok, top
        self.width, self.hidden = width, hidden
        outer = 1
        while outer * outer < experts:
            outer *= 2
        self.outer, self.inner = outer, experts // outer
        mean = tok * top // experts
        self.cap = min(tok, max(2, mean + tok * top // (8 * experts)))
        total = -(-self.outer * self.cap // 16) * 16
        step = self.outer // PARTS
        marks = [k * step * self.cap // 16 * 16 for k in range(PARTS)] + [total]
        if marks[1] >= 32:
            marks[1] = marks[1] // 32 * 16
            marks[2] = marks[1] + 32
        self.chunks = [(marks[k], marks[k + 1]) for k in range(PARTS)]
        self.rows = [b - a for a, b in self.chunks]
        self.steps = [(k + 1) * step - 1 for k in range(PARTS)]
        self.groups = [range(PARTS - 1), range(PARTS - 1, PARTS)]
        self.spans = [(marks[g[0]], marks[g[-1] + 1]) for g in self.groups]
        self.sizes = [b - a for a, b in self.spans]
        self.cands = 2 * self.outer - 1
        self.use = [self.used(*c) for c in self.chunks]
        needed = set().union(*self.use)
        self.last = [
            max(i for i in needed if 0 < i < outer),
            max(i for i in needed if i >= outer) - outer + 1,
        ]

    def keys(self, spans):
        return np.array(
            [[d * STRIDE + q for a, b in spans for d in range(self.inner) for q in range(a, b)]],
            np.int32,
        )

    def order(self, z):
        rest = [s for s in range(self.outer) if s not in (z, z ^ 1)]
        return [z, z ^ 1] + sorted(rest, key=lambda s: abs(s - z))

    def swap(self, z, odd):
        to = z - 1 if (z % 2 == 0) == odd else z + 1
        return to if 0 <= to < self.outer else z

    def trace(self):
        held = {0: list(range(self.outer))}
        for chain in (0, 1):
            last = held[0]
            for r in range(1, self.outer):
                odd = (r % 2 == 0) == (chain == 0)
                last = [last[self.swap(z, odd)] for z in range(self.outer)]
                held[chain * (self.outer - 1) + r] = last
        return held

    def cand(self, z, source):
        step = lambda i: i if i < self.outer else i - self.outer + 1
        found = [i for i, held in self.trace().items() if held[z] == source]
        return min(found, key=lambda i: (step(i), i))

    def exchange(self, r, chain):
        odd = (r % 2 == 0) == (chain == 0)
        return [
            (z * self.inner + p, self.swap(z, odd) * self.inner + p)
            for z in range(self.outer)
            for p in range(self.inner)
        ]

    def used(self, a, b):
        slots = [k for k in range(self.outer) if k * self.cap < b and (k + 1) * self.cap > a]
        return sorted(
            {self.cand(z, self.order(z)[k]) for z in range(self.outer) for k in slots}
        )

    def partner(self, p, d):
        return p ^ d if self.inner & (self.inner - 1) == 0 else (d - p) % self.inner

    def table(self):
        rows = []
        for e in range(self.experts):
            z, p = divmod(e, self.inner)
            offs = [NOWHERE] * self.cands
            for slot, source in enumerate(self.order(z)):
                offs[self.cand(z, source)] = slot * self.cap
            experts = [z * self.inner + self.partner(p, d) for d in range(self.inner)]
            homes = [self.cand(z, z ^ r) for r in range(self.outer)]
            rows.append(offs + experts + homes)
        return np.array(rows, np.int32)

    def across(self, d):
        return [
            (z * self.inner + p, z * self.inner + self.partner(p, d))
            for z in range(self.outer)
            for p in range(self.inner)
        ]

    def flip(self, r):
        return [
            (z * self.inner + p, (z ^ r) * self.inner + p)
            for z in range(self.outer)
            for p in range(self.inner)
        ]


def pack_kernel(plan, tok_ref, up_ref, routes_ref, comb_ref, out_ref):
    tok, width = plan.tok, plan.width
    out_ref[:, :width] = tok_ref[...]
    out_ref[:, width : 2 * width] = up_ref[...]
    kind = lax.broadcasted_iota(jnp.int32, (LANES, tok), 0)
    weight = jnp.zeros((LANES, tok), F32)
    named = jnp.zeros((LANES, tok), F32)
    comb = comb_ref[...].astype(F32)
    for k in range(plan.top):
        e = routes_ref[k : k + 1, :]
        weight = jnp.where(kind == e, comb[k : k + 1, :], weight)
        named = jnp.where(kind == e + HALF, 1.0, named)
    row = lax.broadcasted_iota(jnp.int32, (tok, tok), 0)
    col = lax.broadcasted_iota(jnp.int32, (tok, tok), 1)
    upto = jnp.where(row <= col, 1.0, 0.0).astype(BF)
    count = jnp.dot(named.astype(BF), upto, preferred_element_type=F32)
    table = (weight + count * named).astype(BF)
    same = jnp.where(row == col, 1.0, 0.0).astype(BF)
    turned = lax.dot_general(same, table, NT, preferred_element_type=F32)
    out_ref[:, 2 * width :] = turned.astype(BF)


def picks(plan, meta, off, experts, key, scaled):
    tok = meta.shape[0]
    lane = lax.broadcasted_iota(jnp.int32, (tok, LANES), 1)
    one = jnp.zeros((tok, key.shape[1]), F32)
    two = jnp.zeros((tok, key.shape[1]), F32)
    for d, e in enumerate(experts):
        place = jnp.sum(jnp.where(lane == e + HALF, meta, 0.0), axis=1, keepdims=True)
        place = place.astype(jnp.int32)
        spot = jnp.where(place > 0, place - 1 + off + d * STRIDE, -1)
        hit = spot == key
        one = jnp.where(hit, 1.0, one)
        if scaled:
            weight = jnp.sum(jnp.where(lane == e, meta, 0.0), axis=1, keepdims=True)
            two = jnp.where(hit, weight, two)
    return one, two


def compact_kernel(plan, chunk, *refs):
    use, rows = plan.use[chunk], plan.rows[chunk]
    n, width, tok, inner = len(use), plan.width, plan.tok, plan.inner
    info, key_ref = refs[:2]
    blocks, outs = refs[2 : 2 + n], refs[2 + n : 2 + n + inner]
    held, one_s, two_s, sems = refs[2 + n + inner :]
    copies = [
        pltpu.make_async_copy(b, held.at[pl.ds(i * tok, tok)], sems.at[i])
        for i, b in enumerate(blocks)
    ]
    for c in copies:
        c.start()
    experts = [info[plan.cands + d] for d in range(inner)]
    for i, c in enumerate(copies):
        c.wait()
        meta = held[i * tok : (i + 1) * tok, 2 * width :].astype(F32)
        one, two = picks(plan, meta, info[use[i]], experts, key_ref[...], True)
        one_s[i * tok : (i + 1) * tok, :] = one.astype(BF)
        two_s[i * tok : (i + 1) * tok, :] = two.astype(BF)
    for part, source in ((0, one_s), (1, two_s)):
        have = held[:, part * width : (part + 1) * width]
        found = lax.dot_general(source[...], have, TN, preferred_element_type=F32).astype(BF)
        for d in range(inner):
            outs[d][part * rows : (part + 1) * rows, :] = found[d * rows : (d + 1) * rows]


def pieces(plan, group, got, x_s, d_s, sems, base=0):
    inner, size, first = plan.inner, plan.sizes[group], plan.spans[group][0]
    x_copies, d_copies = [], []
    for i, g in enumerate(got):
        c, d = plan.groups[group][i // inner], i % inner
        rows = plan.rows[c]
        to = pl.ds(base + d * size + plan.chunks[c][0] - first, rows)
        x_copies.append(pltpu.make_async_copy(g.at[pl.ds(0, rows)], x_s.at[to], sems.at[2 * i]))
        d_copies.append(
            pltpu.make_async_copy(g.at[pl.ds(rows, rows)], d_s.at[to], sems.at[2 * i + 1])
        )
    return x_copies, d_copies


def expert_kernel(plan, group, *refs):
    inner, rows, width, hidden = plan.inner, plan.sizes[group], plan.width, plan.hidden
    part, count, n = hidden // 2, inner * rows, inner * len(plan.groups[group])
    info = refs[0]
    got, weights = refs[1 : 1 + n], refs[1 + n : 6 + n]
    hid_o, gate_o, up_o = refs[6 + n : 9 + n]
    backs = refs[9 + n : 9 + n + inner]
    x_s, d_s, wg_s, wu_s, wd_s, comb_s, sems = refs[9 + n + inner :]
    own_g, own_u, own_d, both, other_d = [w.at[0] for w in weights]
    views = [
        (own_g, both.at[:, pl.ds(0, part)]),
        (own_u, both.at[:, pl.ds(part, part)]),
        (own_d, other_d),
    ]
    x_copies, d_copies = pieces(plan, group, got, x_s, d_s, sems)
    tile, tiles = hidden, []
    for t in range(hidden // tile):
        for kind, where in ((0, wg_s), (1, wu_s), (2, wd_s)):
            at, here = t * tile, []
            while at < (t + 1) * tile:
                half, start = divmod(at, part)
                size = min((t + 1) * tile, (half + 1) * part) - at
                source, to = pl.ds(start, size), pl.ds(at, size)
                w = views[kind][half]
                here.append((w.at[source], where.at[to]) if kind == 2 else (w.at[:, source], where.at[:, to]))
                at += size
            tiles.append(here)
    w_copies, used = [], 2 * n
    for here in tiles:
        w_copies.append([])
        for source, to in here:
            w_copies[-1].append(pltpu.make_async_copy(source, to, sems.at[used]))
            used += 1
    for c in x_copies + w_copies[0] + w_copies[1] + d_copies:
        c.start()
    for here in w_copies[2:]:
        for c in here:
            c.start()
    for t in range(hidden // tile):
        at = slice(t * tile, (t + 1) * tile)
        gate_w, up_w, down_w = w_copies[3 * t : 3 * t + 3]
        for c in (x_copies if t == 0 else []) + gate_w:
            c.wait()
        gate = jnp.dot(x_s[...], wg_s[:, at], preferred_element_type=F32)
        for c in up_w:
            c.wait()
        up = jnp.dot(x_s[...], wu_s[:, at], preferred_element_type=F32)
        for c in (d_copies if t == 0 else []) + down_w:
            c.wait()
        mixed = lax.dot_general(d_s[...], wd_s[at, :], NT, preferred_element_type=F32)
        logistic = jax.nn.sigmoid(gate)
        silu = gate * logistic
        hid = (silu * up).astype(BF)
        hid_o[:, at] = hid
        comb = jnp.sum(hid.astype(F32) * mixed, axis=1, keepdims=True)
        comb_s[...] = comb if t == 0 else comb_s[...] + comb
        gate_o[:, at] = (mixed * up * logistic * (1.0 + gate * (1.0 - logistic))).astype(BF)
        up_o[:, at] = (mixed * silu).astype(BF)

    wide = width // 2

    @pl.loop(0, width // wide)
    def _(j):
        at = pl.ds(pl.multiple_of(j * wide, wide), wide)
        back = lax.dot_general(gate_o[...], wg_s[at, :], NT, preferred_element_type=F32)
        back += lax.dot_general(up_o[...], wu_s[at, :], NT, preferred_element_type=F32)
        back = back.astype(BF)
        for d in range(inner):
            backs[d][:, at] = back[d * rows : (d + 1) * rows]

    lane = lax.broadcasted_iota(jnp.int32, (count, LANES), 1)
    comb = jnp.where(lane == info[plan.cands], comb_s[...], 0.0).astype(BF)
    for d in range(inner):
        backs[d][:, width:] = comb[d * rows : (d + 1) * rows]


def weight_kernel(plan, own, extra, *refs):
    inner, width, hidden = plan.inner, plan.width, plan.hidden
    part, n = hidden // 2, plan.inner * PARTS
    got, mids = refs[:n], refs[n : n + 6]
    at = n + 6
    theirs = refs[at : at + 3] if own else None
    at += extra
    outs = refs[at : at + 3]
    x_s, d_s, h_s, gu_s, g_s, u_s, w_s, sems, mid_sems, out_sems = refs[at + 3 : at + 13]
    kept = refs[at + 13 :]
    first, second, base, taken = [], [], 0, 0
    half = pl.ds(0 if own else part, part)
    for g in range(2):
        many = inner * len(plan.groups[g])
        mine = got[taken : taken + many]
        at_sems = sems.at[pl.ds(2 * taken, 2 * many)]
        x_copies, d_copies = pieces(plan, g, mine, x_s, d_s, at_sems, base)
        first += x_copies
        second += d_copies
        to = pl.ds(base, inner * plan.sizes[g])
        spots = (h_s.at[to], gu_s.at[to, pl.ds(0, part)], gu_s.at[to, pl.ds(part, part)])
        for i, (m, s) in enumerate(zip(mids[3 * g : 3 * g + 3], spots)):
            copy = pltpu.make_async_copy(m.at[:, half], s, mid_sems.at[3 * g + i])
            (second if i == 0 else first).append(copy)
        taken += many
        base += inner * plan.sizes[g]
    came = []
    if own:
        came = [
            pltpu.make_async_copy(t.at[0], k, out_sems.at[5 + i])
            for i, (t, k) in enumerate(zip(theirs, kept))
        ]
    for c in first + came[:2] + second + came[2:]:
        c.start()
    for c in first + came[:2]:
        c.wait()
    tile, left = width // 2, []
    for j in range(2):
        to = slice(j * tile, (j + 1) * tile)
        both = lax.dot_general(x_s[:, to], gu_s[...], TN, preferred_element_type=F32)
        for i, (o, s) in enumerate(zip(outs, (g_s, u_s))):
            value = both[:, i * part : (i + 1) * part]
            if own:
                value += kept[i][to, :].astype(F32)
            s[to, :] = value.astype(BF)
            rows = pl.ds(j * tile, tile)
            left.append(
                pltpu.make_async_copy(s.at[rows], o.at[0, rows], out_sems.at[2 * j + i])
            )
            left[-1].start()
    for c in second + came[2:]:
        c.wait()
    down = lax.dot_general(h_s[...], d_s[...], TN, preferred_element_type=F32)
    if own:
        down += kept[2][...].astype(F32)
    w_s[...] = down.astype(BF)
    left.append(pltpu.make_async_copy(w_s, outs[2].at[0], out_sems.at[4]))
    left[-1].start()
    for c in left:
        c.wait()


def spread_kernel(plan, homes, groups, *refs):
    inner, tok, width = plan.inner, plan.tok, plan.width
    info, key_ref = refs[:2]
    blocks = refs[2 : 2 + plan.cands]
    at = 2 + plan.cands
    backs = refs[at : at + groups * inner]
    outs = refs[-5 - len(homes) : -5]
    held, metas, pick_s, sems, meta_sems = refs[-5:]
    copies, later, start = [], [], 0
    for i, b in enumerate(blocks):
        copies.append(
            pltpu.make_async_copy(b.at[:, pl.ds(2 * width, LANES)], metas.at[i], meta_sems.at[i])
        )
    for i, b in enumerate(backs):
        rows = plan.sizes[i // inner]
        later.append(pltpu.make_async_copy(b, held.at[pl.ds(start, rows)], sems.at[i]))
        start += rows
    for c in copies + later:
        c.start()
    for c in copies:
        c.wait()
    experts = [info[plan.cands + d] for d in range(inner)]
    for i, r in enumerate(homes):
        which = info[plan.cands + inner + r]
        meta = metas[which].astype(F32)
        one, _ = picks(plan, meta, info[which], experts, key_ref[...], False)
        pick_s[i * tok : (i + 1) * tok, :] = one.astype(BF)
    for c in later:
        c.wait()
    sums = jnp.dot(pick_s[...], held[...], preferred_element_type=F32).astype(BF)
    for i in range(len(homes)):
        outs[i][...] = sums[i * tok : (i + 1) * tok]


def home_kernel(plan, count, *refs):
    parts = refs[:count]
    routes_ref, comb_ref, _, tok_o, comb_o = refs[count:]
    width, tok = plan.width, plan.tok
    total = parts[0][...].astype(F32)
    for p in parts[1:]:
        total += p[...].astype(F32)
    tok_o[...] = total[:, :width].astype(BF)
    row = lax.broadcasted_iota(jnp.int32, (LANES, LANES), 0)
    col = lax.broadcasted_iota(jnp.int32, (LANES, LANES), 1)
    same = jnp.where(row == col, 1.0, 0.0).astype(BF)
    found = total[:, width:].astype(BF)
    found = lax.dot_general(same, found, NT, preferred_element_type=F32)
    kind = lax.broadcasted_iota(jnp.int32, (LANES, tok), 0)
    out = []
    for k in range(plan.top):
        mine = jnp.where(kind == routes_ref[k : k + 1, :], found, 0.0)
        out.append(jnp.sum(mine, axis=0, keepdims=True))
    out = jnp.concatenate(out, axis=0)
    comb_o[...] = (out / comb_ref[...].astype(F32)).astype(BF)


def on_device(plan, tokens, routes, combine, upstream, w_gate, w_up, w_down):
    tok, width, hidden = plan.tok, plan.width, plan.hidden
    inner, outer, part = plan.inner, plan.outer, plan.hidden // 2
    full = 2 * width + LANES
    shape = jax.ShapeDtypeStruct
    info = jnp.asarray(plan.table())[lax.axis_index("expert")]
    swap = [(0, 1), (1, 0)]

    block = pl.pallas_call(
        functools.partial(pack_kernel, plan),
        out_shape=shape((tok, full), BF),
        in_specs=[VMEM] * 4,
        out_specs=VMEM,
        compiler_params=params(),
        cost_estimate=cost(1e6, 4 * tok * full),
        name="pack",
    )(tokens, upstream, routes.T, combine.T)

    gate_up = jnp.concatenate([w_gate, w_up], axis=2)
    blocks = [block] * plan.cands

    def hop(r):
        for chain in (0, 1):
            if r <= plan.last[chain]:
                i = chain * (outer - 1) + r
                before = block if r == 1 else blocks[i - 1]
                blocks[i] = lax.ppermute(before, "expert", plan.exchange(r, chain))
        if 1 < r <= min(plan.last):
            i = outer - 1 + r
            blocks[r], blocks[i] = lax.optimization_barrier((blocks[r], blocks[i]))

    hop(1)
    def compact(c):
        rows, use = plan.rows[c], plan.use[c]
        count, n = inner * rows, len(use)
        return pl.pallas_call(
            functools.partial(compact_kernel, plan, c),
            out_shape=[shape((2 * rows, width), BF)] * inner,
            in_specs=[SMEM, VMEM] + [ANY] * n,
            out_specs=[VMEM] * inner,
            scratch_shapes=[
                pltpu.VMEM((n * tok, full), BF),
                pltpu.VMEM((n * tok, count), BF),
                pltpu.VMEM((n * tok, count), BF),
                pltpu.SemaphoreType.DMA((n,)),
            ],
            compiler_params=params(),
            cost_estimate=cost(4 * n * tok * count * width, 2 * n * tok * full),
            name="compact",
        )(info, jnp.asarray(plan.keys([plan.chunks[c]])), *[blocks[i] for i in use])

    def expert(g, arrived):
        rows, n = plan.sizes[g], inner * len(plan.groups[g])
        count = inner * rows
        return pl.pallas_call(
            functools.partial(expert_kernel, plan, g),
            out_shape=[shape((count, hidden), BF)] * 3
            + [shape((rows, width + LANES), BF)] * inner,
            in_specs=[SMEM] + [ANY] * (n + 5),
            out_specs=[VMEM] * (3 + inner),
            scratch_shapes=[
                pltpu.VMEM((count, width), BF),
                pltpu.VMEM((count, width), BF),
                pltpu.VMEM((width, hidden), BF),
                pltpu.VMEM((width, hidden), BF),
                pltpu.VMEM((hidden, width), BF),
                pltpu.VMEM((count, 1), F32),
                pltpu.SemaphoreType.DMA((2 * n + 6 * (hidden // 128),)),
            ],
            compiler_params=params(),
            cost_estimate=cost(10 * count * hidden * width, 6 * hidden * width),
            name="expert",
        )(info, *arrived, *weights)

    def cross(arrays):
        return [arrays[0]] + [
            lax.ppermute(arrays[d], "expert", plan.across(d)) for d in range(1, inner)
        ]

    got, done = [], 1
    for c in range(PARTS):
        for r in range(done + 1, plan.steps[c] + 1):
            hop(r)
        done = max(done, plan.steps[c])
        sent = compact(c)
        if c > 0:
            got[-1], sent = lax.optimization_barrier((got[-1], sent))
        if c == PARTS - 2:
            gate_up, sent = lax.optimization_barrier((gate_up, sent))
            gate_up = lax.ppermute(gate_up, "dp", swap)
        if c == PARTS - 1:
            gate_up, sent = lax.optimization_barrier((gate_up, sent))
            down = lax.ppermute(lax.optimization_barrier((w_down, sent))[0], "dp", swap)
        got.append(cross(sent))
        if c == 0:
            i = outer - 1 + done
            got[0], blocks[done], blocks[i] = lax.optimization_barrier(
                (got[0], blocks[done], blocks[i])
            )
    weights = [w_gate, w_up, w_down, gate_up, down]
    outs = expert(0, sum(got[:-1], []))
    outs = list(outs)
    outs[0], late = lax.optimization_barrier((outs[0], got[-1]))
    got[-1] = late
    backs = cross(outs[3:])
    more = expert(1, late)
    got = sum(got, [])
    mids = outs[:3] + list(more[:3])

    count = inner * sum(plan.rows)

    grad_scratch = [
        pltpu.VMEM((width, part), BF),
        pltpu.VMEM((width, part), BF),
        pltpu.VMEM((part, width), BF),
    ]

    def weight_grads(own, extra):
        return pl.pallas_call(
            functools.partial(weight_kernel, plan, own, len(extra)),
            out_shape=[
                shape((1, width, part), BF),
                shape((1, width, part), BF),
                shape((1, part, width), BF),
            ],
            in_specs=[ANY] * (inner * PARTS + 6 + len(extra)),
            out_specs=[ANY] * 3,
            scratch_shapes=[
                pltpu.VMEM((count, width), BF),
                pltpu.VMEM((count, width), BF),
                pltpu.VMEM((count, part), BF),
                pltpu.VMEM((count, 2 * part), BF),
                *grad_scratch,
                pltpu.SemaphoreType.DMA((2 * inner * PARTS,)),
                pltpu.SemaphoreType.DMA((6,)),
                pltpu.SemaphoreType.DMA((8,)),
                *(grad_scratch if own else []),
            ],
            compiler_params=params(),
            cost_estimate=cost(6 * count * part * width, 4 * count * (width + hidden)),
            name="weight_grads",
        )(*got, *mids, *extra)

    def spread(homes, groups, extra):
        slots = inner * sum(plan.sizes[:groups])
        return pl.pallas_call(
            functools.partial(spread_kernel, plan, homes, groups),
            out_shape=[shape((tok, width + LANES), BF)] * len(homes),
            in_specs=[SMEM, VMEM] + [ANY] * (plan.cands + groups * inner + len(extra)),
            out_specs=[VMEM] * len(homes),
            scratch_shapes=[
                pltpu.VMEM((slots, width + LANES), BF),
                pltpu.VMEM((plan.cands, tok, LANES), BF),
                pltpu.VMEM((len(homes) * tok, slots), BF),
                pltpu.SemaphoreType.DMA((groups * inner,)),
                pltpu.SemaphoreType.DMA((plan.cands,)),
            ],
            compiler_params=params(),
            cost_estimate=cost(2 * len(homes) * tok * slots * width, 2 * slots * width),
            name="spread",
        )(
            info,
            jnp.asarray(plan.keys(plan.spans[:groups])),
            *blocks,
            *backs[: groups * inner],
            *extra,
        )

    mine = weight_grads(False, backs[1:inner])
    backs = backs + cross(more[3:])
    mine, backs = lax.optimization_barrier((mine, backs))
    theirs = [lax.ppermute(w, "dp", swap) for w in mine]
    sums = dict(enumerate(spread(list(range(outer)), 2, [mine[0]])))
    came, bit = [], 1
    while bit < outer:
        for r in range(outer - bit, 0, -2 * bit):
            sent = lax.ppermute(sums[r], "expert", plan.flip(bit))
            if r == bit:
                came.append(sent)
                continue
            if bit == 1:
                sums[1], sent = lax.optimization_barrier((sums[1], sent))
            total = sums[r - bit].astype(F32) + sent.astype(F32)
            sums[r - bit] = total.astype(BF)
        bit *= 2
    grads = weight_grads(True, theirs)
    home = [sums[0]] + came
    grad_tokens, grad_combine = pl.pallas_call(
        functools.partial(home_kernel, plan, len(home)),
        out_shape=[shape((tok, width), BF), shape((plan.top, tok), BF)],
        in_specs=[VMEM] * (len(home) + 2) + [ANY],
        out_specs=[VMEM] * 2,
        compiler_params=params(),
        cost_estimate=cost(1e6, 2 * tok * width * (outer + 1)),
        name="home",
    )(*home, routes.T, combine.T, grads[0])
    return (grad_tokens, grad_combine.T, *grads)


def solution(mesh):
    rows = P(("parts", "dp", "expert"), None)
    in_specs = (rows,) * 4 + (P("expert", None, "dp"),) * 2 + (P("expert", "dp", None),)
    out_specs = (rows,) * 2 + (P(("parts", "expert"), None, "dp"),) * 2
    out_specs += (P(("parts", "expert"), "dp", None),)
    shape = dict(mesh.shape)

    def whole(tokens, routes, combine, upstream, w_gate, w_up, w_down):
        devices = shape["parts"] * shape["dp"] * shape["expert"]
        plan = Plan(
            shape["expert"],
            tokens.shape[0] // devices,
            routes.shape[1],
            tokens.shape[1],
            w_gate.shape[2],
        )
        body = functools.partial(on_device, plan)
        return jax.shard_map(
            body, mesh=mesh, in_specs=in_specs, out_specs=out_specs, check_vma=False
        )(tokens, routes, combine, upstream, w_gate, w_up, w_down)

    return whole
```

```python
import functools

import jax
import jax.numpy as jnp
import numpy as np
from jax import lax
from jax.experimental import pallas as pl
from jax.experimental.pallas import tpu as pltpu
from jax.sharding import PartitionSpec as P

BF = jnp.bfloat16
F32 = jnp.float32
LANES = 128
HALF = 64
STRIDE = 1024
PARTS = 4
NOWHERE = -(1 << 20)
ANY = pl.BlockSpec(memory_space=pltpu.HBM)
VMEM = pl.BlockSpec(memory_space=pltpu.VMEM)
SMEM = pl.BlockSpec(memory_space=pltpu.SMEM)
TN = (((0,), (0,)), ((), ()))
NT = (((1,), (1,)), ((), ()))


def params(megabytes=60):
    return pltpu.CompilerParams(vmem_limit_bytes=megabytes << 20)


def cost(flops, moved):
    return pl.CostEstimate(flops=int(flops), bytes_accessed=int(moved), transcendentals=0)


class Plan:
    def __init__(self, experts, tok, top, width, hidden):
        self.experts, self.tok, self.top = experts, tok, top
        self.width, self.hidden = width, hidden
        outer = 1
        while outer * outer < experts:
            outer *= 2
        self.outer, self.inner = outer, experts // outer
        mean = tok * top // experts
        self.cap = min(tok, max(2, mean + tok * top // (8 * experts)))
        total = -(-self.outer * self.cap // 16) * 16
        step = self.outer // PARTS
        marks = [k * step * self.cap // 16 * 16 for k in range(PARTS)] + [total]
        if marks[1] >= 32:
            marks[1] = marks[1] // 32 * 16
            marks[2] = marks[1] + 32
        self.chunks = [(marks[k], marks[k + 1]) for k in range(PARTS)]
        self.rows = [b - a for a, b in self.chunks]
        self.steps = [(k + 1) * step - 1 for k in range(PARTS)]
        self.groups = [range(PARTS - 1), range(PARTS - 1, PARTS)]
        self.spans = [(marks[g[0]], marks[g[-1] + 1]) for g in self.groups]
        self.sizes = [b - a for a, b in self.spans]
        self.cands = 2 * self.outer - 1
        self.use = [self.used(*c) for c in self.chunks]
        middle, end = width // 2, width + LANES
        self.halves = [(0, 0, end), (1, 0, end)] + [
            (r, a, b) for r in range(2, outer) for a, b in ((0, middle), (middle, end))
        ]
        needed = set().union(*self.use)
        self.last = [
            max(i for i in needed if 0 < i < outer),
            max(i for i in needed if i >= outer) - outer + 1,
        ]

    def keys(self, spans):
        return np.array(
            [[d * STRIDE + q for a, b in spans for d in range(self.inner) for q in range(a, b)]],
            np.int32,
        )

    def order(self, z):
        rest = [s for s in range(self.outer) if s not in (z, z ^ 1)]
        return [z, z ^ 1] + sorted(rest, key=lambda s: abs(s - z))

    def swap(self, z, odd):
        to = z - 1 if (z % 2 == 0) == odd else z + 1
        return to if 0 <= to < self.outer else z

    def trace(self):
        held = {0: list(range(self.outer))}
        for chain in (0, 1):
            last = held[0]
            for r in range(1, self.outer):
                odd = (r % 2 == 0) == (chain == 0)
                last = [last[self.swap(z, odd)] for z in range(self.outer)]
                held[chain * (self.outer - 1) + r] = last
        return held

    def cand(self, z, source):
        step = lambda i: i if i < self.outer else i - self.outer + 1
        found = [i for i, held in self.trace().items() if held[z] == source]
        return min(found, key=lambda i: (step(i), i))

    def exchange(self, r, chain):
        odd = (r % 2 == 0) == (chain == 0)
        return [
            (z * self.inner + p, self.swap(z, odd) * self.inner + p)
            for z in range(self.outer)
            for p in range(self.inner)
        ]

    def used(self, a, b):
        slots = [k for k in range(self.outer) if k * self.cap < b and (k + 1) * self.cap > a]
        return sorted(
            {self.cand(z, self.order(z)[k]) for z in range(self.outer) for k in slots}
        )

    def partner(self, p, d):
        return p ^ d if self.inner & (self.inner - 1) == 0 else (d - p) % self.inner

    def table(self):
        rows = []
        for e in range(self.experts):
            z, p = divmod(e, self.inner)
            offs = [NOWHERE] * self.cands
            for slot, source in enumerate(self.order(z)):
                offs[self.cand(z, source)] = slot * self.cap
            experts = [z * self.inner + self.partner(p, d) for d in range(self.inner)]
            homes = [self.cand(z, z ^ r) for r in range(self.outer)]
            rows.append(offs + experts + homes)
        return np.array(rows, np.int32)

    def across(self, d):
        return [
            (z * self.inner + p, z * self.inner + self.partner(p, d))
            for z in range(self.outer)
            for p in range(self.inner)
        ]

    def flip(self, r):
        return [
            (z * self.inner + p, (z ^ r) * self.inner + p)
            for z in range(self.outer)
            for p in range(self.inner)
        ]


def pack_kernel(plan, tok_ref, up_ref, routes_ref, comb_ref, out_ref):
    tok, width = plan.tok, plan.width
    out_ref[:, :width] = tok_ref[...]
    out_ref[:, width : 2 * width] = up_ref[...]
    kind = lax.broadcasted_iota(jnp.int32, (LANES, tok), 0)
    weight = jnp.zeros((LANES, tok), F32)
    named = jnp.zeros((LANES, tok), F32)
    comb = comb_ref[...].astype(F32)
    for k in range(plan.top):
        e = routes_ref[k : k + 1, :]
        weight = jnp.where(kind == e, comb[k : k + 1, :], weight)
        named = jnp.where(kind == e + HALF, 1.0, named)
    row = lax.broadcasted_iota(jnp.int32, (tok, tok), 0)
    col = lax.broadcasted_iota(jnp.int32, (tok, tok), 1)
    upto = jnp.where(row <= col, 1.0, 0.0).astype(BF)
    count = jnp.dot(named.astype(BF), upto, preferred_element_type=F32)
    table = (weight + count * named).astype(BF)
    same = jnp.where(row == col, 1.0, 0.0).astype(BF)
    turned = lax.dot_general(same, table, NT, preferred_element_type=F32)
    out_ref[:, 2 * width :] = turned.astype(BF)


def picks(plan, meta, off, experts, key, scaled):
    tok = meta.shape[0]
    lane = lax.broadcasted_iota(jnp.int32, (tok, LANES), 1)
    one = jnp.zeros((tok, key.shape[1]), F32)
    two = jnp.zeros((tok, key.shape[1]), F32)
    for d, e in enumerate(experts):
        place = jnp.sum(jnp.where(lane == e + HALF, meta, 0.0), axis=1, keepdims=True)
        place = place.astype(jnp.int32)
        spot = jnp.where(place > 0, place - 1 + off + d * STRIDE, -1)
        hit = spot == key
        one = jnp.where(hit, 1.0, one)
        if scaled:
            weight = jnp.sum(jnp.where(lane == e, meta, 0.0), axis=1, keepdims=True)
            two = jnp.where(hit, weight, two)
    return one, two


def compact_kernel(plan, chunk, *refs):
    use, rows = plan.use[chunk], plan.rows[chunk]
    n, width, tok, inner = len(use), plan.width, plan.tok, plan.inner
    info, key_ref = refs[:2]
    blocks, outs = refs[2 : 2 + n], refs[2 + n : 2 + n + inner]
    held, one_s, two_s, sems = refs[2 + n + inner :]
    copies = [
        pltpu.make_async_copy(b, held.at[pl.ds(i * tok, tok)], sems.at[i])
        for i, b in enumerate(blocks)
    ]
    for c in copies:
        c.start()
    experts = [info[plan.cands + d] for d in range(inner)]
    for i, c in enumerate(copies):
        c.wait()
        meta = held[i * tok : (i + 1) * tok, 2 * width :].astype(F32)
        one, two = picks(plan, meta, info[use[i]], experts, key_ref[...], True)
        one_s[i * tok : (i + 1) * tok, :] = one.astype(BF)
        two_s[i * tok : (i + 1) * tok, :] = two.astype(BF)
    for part, source in ((0, one_s), (1, two_s)):
        have = held[:, part * width : (part + 1) * width]
        found = lax.dot_general(source[...], have, TN, preferred_element_type=F32).astype(BF)
        for d in range(inner):
            outs[d][part * rows : (part + 1) * rows, :] = found[d * rows : (d + 1) * rows]


def pieces(plan, group, got, x_s, d_s, sems, base=0):
    inner, size, first = plan.inner, plan.sizes[group], plan.spans[group][0]
    x_copies, d_copies = [], []
    for i, g in enumerate(got):
        c, d = plan.groups[group][i // inner], i % inner
        rows = plan.rows[c]
        to = pl.ds(base + d * size + plan.chunks[c][0] - first, rows)
        x_copies.append(pltpu.make_async_copy(g.at[pl.ds(0, rows)], x_s.at[to], sems.at[2 * i]))
        d_copies.append(
            pltpu.make_async_copy(g.at[pl.ds(rows, rows)], d_s.at[to], sems.at[2 * i + 1])
        )
    return x_copies, d_copies


def expert_kernel(plan, group, *refs):
    inner, rows, width, hidden = plan.inner, plan.sizes[group], plan.width, plan.hidden
    part, count, n = hidden // 2, inner * rows, inner * len(plan.groups[group])
    info = refs[0]
    got, weights = refs[1 : 1 + n], refs[1 + n : 6 + n]
    hid_o, gate_o, up_o = refs[6 + n : 9 + n]
    backs = refs[9 + n : 9 + n + inner]
    x_s, d_s, wg_s, wu_s, wd_s, comb_s, sems = refs[9 + n + inner :]
    own_g, own_u, own_d, both, other_d = [w.at[0] for w in weights]
    views = [
        (own_g, both.at[:, pl.ds(0, part)]),
        (own_u, both.at[:, pl.ds(part, part)]),
        (own_d, other_d),
    ]
    x_copies, d_copies = pieces(plan, group, got, x_s, d_s, sems)
    tile, tiles = hidden, []
    for t in range(hidden // tile):
        for kind, where in ((0, wg_s), (1, wu_s), (2, wd_s)):
            at, here = t * tile, []
            while at < (t + 1) * tile:
                half, start = divmod(at, part)
                size = min((t + 1) * tile, (half + 1) * part) - at
                source, to = pl.ds(start, size), pl.ds(at, size)
                w = views[kind][half]
                here.append((w.at[source], where.at[to]) if kind == 2 else (w.at[:, source], where.at[:, to]))
                at += size
            tiles.append(here)
    w_copies, used = [], 2 * n
    for here in tiles:
        w_copies.append([])
        for source, to in here:
            w_copies[-1].append(pltpu.make_async_copy(source, to, sems.at[used]))
            used += 1
    for c in x_copies + w_copies[0] + w_copies[1] + d_copies:
        c.start()
    for here in w_copies[2:]:
        for c in here:
            c.start()
    for t in range(hidden // tile):
        at = slice(t * tile, (t + 1) * tile)
        gate_w, up_w, down_w = w_copies[3 * t : 3 * t + 3]
        for c in (x_copies if t == 0 else []) + gate_w:
            c.wait()
        gate = jnp.dot(x_s[...], wg_s[:, at], preferred_element_type=F32)
        for c in up_w:
            c.wait()
        up = jnp.dot(x_s[...], wu_s[:, at], preferred_element_type=F32)
        for c in (d_copies if t == 0 else []) + down_w:
            c.wait()
        mixed = lax.dot_general(d_s[...], wd_s[at, :], NT, preferred_element_type=F32)
        logistic = jax.nn.sigmoid(gate)
        silu = gate * logistic
        hid = (silu * up).astype(BF)
        hid_o[:, at] = hid
        comb = jnp.sum(hid.astype(F32) * mixed, axis=1, keepdims=True)
        comb_s[...] = comb if t == 0 else comb_s[...] + comb
        gate_o[:, at] = (mixed * up * logistic * (1.0 + gate * (1.0 - logistic))).astype(BF)
        up_o[:, at] = (mixed * silu).astype(BF)

    wide = width // 2

    @pl.loop(0, width // wide)
    def _(j):
        at = pl.ds(pl.multiple_of(j * wide, wide), wide)
        back = lax.dot_general(gate_o[...], wg_s[at, :], NT, preferred_element_type=F32)
        back += lax.dot_general(up_o[...], wu_s[at, :], NT, preferred_element_type=F32)
        back = back.astype(BF)
        for d in range(inner):
            backs[d][:, at] = back[d * rows : (d + 1) * rows]

    lane = lax.broadcasted_iota(jnp.int32, (count, LANES), 1)
    comb = jnp.where(lane == info[plan.cands], comb_s[...], 0.0).astype(BF)
    for d in range(inner):
        backs[d][:, width:] = comb[d * rows : (d + 1) * rows]


def weight_kernel(plan, own, extra, *refs):
    inner, width, hidden = plan.inner, plan.width, plan.hidden
    part, n = hidden // 2, plan.inner * PARTS
    got, mids = refs[:n], refs[n : n + 6]
    at = n + 6
    theirs = refs[at : at + 3] if own else None
    at += extra
    outs = refs[at : at + 3]
    x_s, d_s, h_s, gu_s, g_s, u_s, w_s, sems, mid_sems, out_sems = refs[at + 3 : at + 13]
    kept = refs[at + 13 :]
    first, second, base, taken = [], [], 0, 0
    half = pl.ds(0 if own else part, part)
    for g in range(2):
        many = inner * len(plan.groups[g])
        mine = got[taken : taken + many]
        at_sems = sems.at[pl.ds(2 * taken, 2 * many)]
        x_copies, d_copies = pieces(plan, g, mine, x_s, d_s, at_sems, base)
        first += x_copies
        second += d_copies
        to = pl.ds(base, inner * plan.sizes[g])
        spots = (h_s.at[to], gu_s.at[to, pl.ds(0, part)], gu_s.at[to, pl.ds(part, part)])
        for i, (m, s) in enumerate(zip(mids[3 * g : 3 * g + 3], spots)):
            copy = pltpu.make_async_copy(m.at[:, half], s, mid_sems.at[3 * g + i])
            (second if i == 0 else first).append(copy)
        taken += many
        base += inner * plan.sizes[g]
    came = []
    if own:
        came = [
            pltpu.make_async_copy(t.at[0], k, out_sems.at[5 + i])
            for i, (t, k) in enumerate(zip(theirs, kept))
        ]
    for c in first + came[:2] + second + came[2:]:
        c.start()
    for c in first + came[:2]:
        c.wait()
    tile, left = width // 2, []
    for j in range(2):
        to = slice(j * tile, (j + 1) * tile)
        both = lax.dot_general(x_s[:, to], gu_s[...], TN, preferred_element_type=F32)
        for i, (o, s) in enumerate(zip(outs, (g_s, u_s))):
            value = both[:, i * part : (i + 1) * part]
            if own:
                value += kept[i][to, :].astype(F32)
            s[to, :] = value.astype(BF)
            rows = pl.ds(j * tile, tile)
            left.append(
                pltpu.make_async_copy(s.at[rows], o.at[0, rows], out_sems.at[2 * j + i])
            )
            left[-1].start()
    for c in second + came[2:]:
        c.wait()
    down = lax.dot_general(h_s[...], d_s[...], TN, preferred_element_type=F32)
    if own:
        down += kept[2][...].astype(F32)
    w_s[...] = down.astype(BF)
    left.append(pltpu.make_async_copy(w_s, outs[2].at[0], out_sems.at[4]))
    left[-1].start()
    for c in left:
        c.wait()


def spread_kernel(plan, homes, groups, *refs):
    inner, tok, width = plan.inner, plan.tok, plan.width
    info, key_ref = refs[:2]
    blocks = refs[2 : 2 + plan.cands]
    at = 2 + plan.cands
    backs = refs[at : at + groups * inner]
    outs = list(refs[at + groups * inner : -5])
    outs = outs[len(outs) - len(plan.halves) :]
    held, metas, pick_s, sems, meta_sems = refs[-5:]
    copies, later, start = [], [], 0
    for i, b in enumerate(blocks):
        copies.append(
            pltpu.make_async_copy(b.at[:, pl.ds(2 * width, LANES)], metas.at[i], meta_sems.at[i])
        )
    for i, b in enumerate(backs):
        rows = plan.sizes[i // inner]
        later.append(pltpu.make_async_copy(b, held.at[pl.ds(start, rows)], sems.at[i]))
        start += rows
    for c in copies + later:
        c.start()
    for c in copies:
        c.wait()
    experts = [info[plan.cands + d] for d in range(inner)]
    for i, r in enumerate(homes):
        which = info[plan.cands + inner + r]
        meta = metas[which].astype(F32)
        one, _ = picks(plan, meta, info[which], experts, key_ref[...], False)
        pick_s[i * tok : (i + 1) * tok, :] = one.astype(BF)
    for c in later:
        c.wait()
    sums = jnp.dot(pick_s[...], held[...], preferred_element_type=F32).astype(BF)
    for o, (r, a, b) in zip(outs, plan.halves):
        o[...] = sums[r * tok : (r + 1) * tok, a:b]


def home_kernel(plan, count, *refs):
    parts = refs[:count]
    routes_ref, comb_ref, _, tok_o, comb_o = refs[count:]
    width, tok = plan.width, plan.tok
    middle = width // 2
    total = parts[0][...].astype(F32) + parts[1][...].astype(F32)
    low, high = total[:, :middle], total[:, middle:]
    for p in parts[2::2]:
        low += p[...].astype(F32)
    for p in parts[3::2]:
        high += p[...].astype(F32)
    tok_o[:, :middle] = low.astype(BF)
    tok_o[:, middle:] = high[:, :middle].astype(BF)
    row = lax.broadcasted_iota(jnp.int32, (LANES, LANES), 0)
    col = lax.broadcasted_iota(jnp.int32, (LANES, LANES), 1)
    same = jnp.where(row == col, 1.0, 0.0).astype(BF)
    found = high[:, width - middle :].astype(BF)
    found = lax.dot_general(same, found, NT, preferred_element_type=F32)
    kind = lax.broadcasted_iota(jnp.int32, (LANES, tok), 0)
    out = []
    for k in range(plan.top):
        mine = jnp.where(kind == routes_ref[k : k + 1, :], found, 0.0)
        out.append(jnp.sum(mine, axis=0, keepdims=True))
    out = jnp.concatenate(out, axis=0)
    comb_o[...] = (out / comb_ref[...].astype(F32)).astype(BF)


def on_device(plan, tokens, routes, combine, upstream, w_gate, w_up, w_down):
    tok, width, hidden = plan.tok, plan.width, plan.hidden
    inner, outer, part = plan.inner, plan.outer, plan.hidden // 2
    full = 2 * width + LANES
    shape = jax.ShapeDtypeStruct
    info = jnp.asarray(plan.table())[lax.axis_index("expert")]
    swap = [(0, 1), (1, 0)]

    block = pl.pallas_call(
        functools.partial(pack_kernel, plan),
        out_shape=shape((tok, full), BF),
        in_specs=[VMEM] * 4,
        out_specs=VMEM,
        compiler_params=params(),
        cost_estimate=cost(1e6, 4 * tok * full),
        name="pack",
    )(tokens, upstream, routes.T, combine.T)

    gate_up = jnp.concatenate([w_gate, w_up], axis=2)
    blocks = [block] * plan.cands

    def hop(r):
        for chain in (0, 1):
            if r <= plan.last[chain]:
                i = chain * (outer - 1) + r
                before = block if r == 1 else blocks[i - 1]
                blocks[i] = lax.ppermute(before, "expert", plan.exchange(r, chain))
        if 1 < r <= min(plan.last):
            i = outer - 1 + r
            blocks[r], blocks[i] = lax.optimization_barrier((blocks[r], blocks[i]))

    hop(1)
    def compact(c):
        rows, use = plan.rows[c], plan.use[c]
        count, n = inner * rows, len(use)
        return pl.pallas_call(
            functools.partial(compact_kernel, plan, c),
            out_shape=[shape((2 * rows, width), BF)] * inner,
            in_specs=[SMEM, VMEM] + [ANY] * n,
            out_specs=[VMEM] * inner,
            scratch_shapes=[
                pltpu.VMEM((n * tok, full), BF),
                pltpu.VMEM((n * tok, count), BF),
                pltpu.VMEM((n * tok, count), BF),
                pltpu.SemaphoreType.DMA((n,)),
            ],
            compiler_params=params(),
            cost_estimate=cost(4 * n * tok * count * width, 2 * n * tok * full),
            name="compact",
        )(info, jnp.asarray(plan.keys([plan.chunks[c]])), *[blocks[i] for i in use])

    def expert(g, arrived):
        rows, n = plan.sizes[g], inner * len(plan.groups[g])
        count = inner * rows
        return pl.pallas_call(
            functools.partial(expert_kernel, plan, g),
            out_shape=[shape((count, hidden), BF)] * 3
            + [shape((rows, width + LANES), BF)] * inner,
            in_specs=[SMEM] + [ANY] * (n + 5),
            out_specs=[VMEM] * (3 + inner),
            scratch_shapes=[
                pltpu.VMEM((count, width), BF),
                pltpu.VMEM((count, width), BF),
                pltpu.VMEM((width, hidden), BF),
                pltpu.VMEM((width, hidden), BF),
                pltpu.VMEM((hidden, width), BF),
                pltpu.VMEM((count, 1), F32),
                pltpu.SemaphoreType.DMA((2 * n + 6 * (hidden // 128),)),
            ],
            compiler_params=params(),
            cost_estimate=cost(10 * count * hidden * width, 6 * hidden * width),
            name="expert",
        )(info, *arrived, *weights)

    def cross(arrays):
        return [arrays[0]] + [
            lax.ppermute(arrays[d], "expert", plan.across(d)) for d in range(1, inner)
        ]

    got, done = [], 1
    for c in range(PARTS):
        for r in range(done + 1, plan.steps[c] + 1):
            hop(r)
        done = max(done, plan.steps[c])
        sent = compact(c)
        if c > 0:
            got[-1], sent = lax.optimization_barrier((got[-1], sent))
        if c == PARTS - 2:
            gate_up, sent = lax.optimization_barrier((gate_up, sent))
            gate_up = lax.ppermute(gate_up, "dp", swap)
        if c == PARTS - 1:
            gate_up, sent = lax.optimization_barrier((gate_up, sent))
            down = lax.ppermute(lax.optimization_barrier((w_down, sent))[0], "dp", swap)
        got.append(cross(sent))
        if c == 0:
            i = outer - 1 + done
            got[0], blocks[done], blocks[i] = lax.optimization_barrier(
                (got[0], blocks[done], blocks[i])
            )
    weights = [w_gate, w_up, w_down, gate_up, down]
    outs = expert(0, sum(got[:-1], []))
    outs = list(outs)
    outs[0], late = lax.optimization_barrier((outs[0], got[-1]))
    got[-1] = late
    backs = cross(outs[3:])
    more = expert(1, late)
    got = sum(got, [])
    mids = outs[:3] + list(more[:3])

    count = inner * sum(plan.rows)

    grad_scratch = [
        pltpu.VMEM((width, part), BF),
        pltpu.VMEM((width, part), BF),
        pltpu.VMEM((part, width), BF),
    ]

    def weight_grads(own, extra):
        return pl.pallas_call(
            functools.partial(weight_kernel, plan, own, len(extra)),
            out_shape=[
                shape((1, width, part), BF),
                shape((1, width, part), BF),
                shape((1, part, width), BF),
            ],
            in_specs=[ANY] * (inner * PARTS + 6 + len(extra)),
            out_specs=[ANY] * 3,
            scratch_shapes=[
                pltpu.VMEM((count, width), BF),
                pltpu.VMEM((count, width), BF),
                pltpu.VMEM((count, part), BF),
                pltpu.VMEM((count, 2 * part), BF),
                *grad_scratch,
                pltpu.SemaphoreType.DMA((2 * inner * PARTS,)),
                pltpu.SemaphoreType.DMA((6,)),
                pltpu.SemaphoreType.DMA((8,)),
                *(grad_scratch if own else []),
            ],
            compiler_params=params(),
            cost_estimate=cost(6 * count * part * width, 4 * count * (width + hidden)),
            name="weight_grads",
        )(*got, *mids, *extra)

    def spread(homes, groups, extra):
        slots = inner * sum(plan.sizes[:groups])
        return pl.pallas_call(
            functools.partial(spread_kernel, plan, homes, groups),
            out_shape=[shape((tok, b - a), BF) for _, a, b in plan.halves],
            in_specs=[SMEM, VMEM] + [ANY] * (plan.cands + groups * inner + len(extra)),
            out_specs=[VMEM] * len(plan.halves),
            scratch_shapes=[
                pltpu.VMEM((slots, width + LANES), BF),
                pltpu.VMEM((plan.cands, tok, LANES), BF),
                pltpu.VMEM((len(homes) * tok, slots), BF),
                pltpu.SemaphoreType.DMA((groups * inner,)),
                pltpu.SemaphoreType.DMA((plan.cands,)),
            ],
            compiler_params=params(),
            cost_estimate=cost(2 * len(homes) * tok * slots * width, 2 * slots * width),
            name="spread",
        )(
            info,
            jnp.asarray(plan.keys(plan.spans[:groups])),
            *blocks,
            *backs[: groups * inner],
            *extra,
        )

    mine = weight_grads(False, backs[1:inner])
    backs = backs + cross(more[3:])
    mine, backs = lax.optimization_barrier((mine, backs))
    theirs = [lax.ppermute(w, "dp", swap) for w in mine]
    cut = spread(list(range(outer)), 2, [mine[0]])
    sums = {(r, a): part for (r, a, b), part in zip(plan.halves, cut)}
    came, bit, starts = [], 1, (0, width // 2)
    while bit < outer:
        for r in range(outer - bit, 0, -2 * bit):
            if r == 1:
                came.append(lax.ppermute(sums[1, 0], "expert", plan.flip(1)))
                continue
            for a in starts:
                sent = lax.ppermute(sums[r, a], "expert", plan.flip(bit))
                if r == bit:
                    came.append(sent)
                    continue
                if bit == 1:
                    sums[1, 0], sent = lax.optimization_barrier((sums[1, 0], sent))
                total = sums[r - bit, a].astype(F32) + sent.astype(F32)
                sums[r - bit, a] = total.astype(BF)
        bit *= 2
    grads = weight_grads(True, theirs)
    home = [sums[0, 0]] + came
    grad_tokens, grad_combine = pl.pallas_call(
        functools.partial(home_kernel, plan, len(home)),
        out_shape=[shape((tok, width), BF), shape((plan.top, tok), BF)],
        in_specs=[VMEM] * (len(home) + 2) + [ANY],
        out_specs=[VMEM] * 2,
        compiler_params=params(),
        cost_estimate=cost(1e6, 2 * tok * width * (outer + 1)),
        name="home",
    )(*home, routes.T, combine.T, grads[0])
    return (grad_tokens, grad_combine.T, *grads)


def solution(mesh):
    rows = P(("parts", "dp", "expert"), None)
    in_specs = (rows,) * 4 + (P("expert", None, "dp"),) * 2 + (P("expert", "dp", None),)
    out_specs = (rows,) * 2 + (P(("parts", "expert"), None, "dp"),) * 2
    out_specs += (P(("parts", "expert"), "dp", None),)
    shape = dict(mesh.shape)

    def whole(tokens, routes, combine, upstream, w_gate, w_up, w_down):
        devices = shape["parts"] * shape["dp"] * shape["expert"]
        plan = Plan(
            shape["expert"],
            tokens.shape[0] // devices,
            routes.shape[1],
            tokens.shape[1],
            w_gate.shape[2],
        )
        body = functools.partial(on_device, plan)
        return jax.shard_map(
            body, mesh=mesh, in_specs=in_specs, out_specs=out_specs, check_vma=False
        )(tokens, routes, combine, upstream, w_gate, w_up, w_down)

    return whole
```

```python
import functools

import jax
import jax.numpy as jnp
import numpy as np
from jax import lax
from jax.experimental import pallas as pl
from jax.experimental.pallas import tpu as pltpu
from jax.sharding import PartitionSpec as P

BF = jnp.bfloat16
F32 = jnp.float32
LANES = 128
HALF = 64
STRIDE = 1024
PARTS = 4
NOWHERE = -(1 << 20)
ANY = pl.BlockSpec(memory_space=pltpu.HBM)
VMEM = pl.BlockSpec(memory_space=pltpu.VMEM)
SMEM = pl.BlockSpec(memory_space=pltpu.SMEM)
TN = (((0,), (0,)), ((), ()))
NT = (((1,), (1,)), ((), ()))


def params(megabytes=60):
    return pltpu.CompilerParams(vmem_limit_bytes=megabytes << 20)


def cost(flops, moved):
    return pl.CostEstimate(flops=int(flops), bytes_accessed=int(moved), transcendentals=0)


class Plan:
    def __init__(self, experts, tok, top, width, hidden):
        self.experts, self.tok, self.top = experts, tok, top
        self.width, self.hidden = width, hidden
        outer = 1
        while outer * outer < experts:
            outer *= 2
        self.outer, self.inner = outer, experts // outer
        mean = tok * top // experts
        self.cap = min(tok, max(2, mean + tok * top // (8 * experts)))
        total = -(-self.outer * self.cap // 16) * 16
        step = self.outer // PARTS
        marks = [k * step * self.cap // 16 * 16 for k in range(PARTS)] + [total]
        if marks[1] >= 32:
            marks[1] = marks[1] // 32 * 16
            marks[2] = marks[1] + 32
        self.chunks = [(marks[k], marks[k + 1]) for k in range(PARTS)]
        self.rows = [b - a for a, b in self.chunks]
        self.steps = [(k + 1) * step - 1 for k in range(PARTS)]
        self.groups = [range(PARTS - 1), range(PARTS - 1, PARTS)]
        self.spans = [(marks[g[0]], marks[g[-1] + 1]) for g in self.groups]
        self.sizes = [b - a for a, b in self.spans]
        self.cands = 2 * self.outer - 1
        self.use = [self.used(*c) for c in self.chunks]
        middle, end = width // 2, width + LANES
        self.halves = [(0, 0, end), (1, 0, end)] + [
            (r, a, b) for r in range(2, outer) for a, b in ((0, middle), (middle, end))
        ]
        needed = set().union(*self.use)
        self.last = [
            max(i for i in needed if 0 < i < outer),
            max(i for i in needed if i >= outer) - outer + 1,
        ]

    def keys(self, spans):
        return np.array(
            [[d * STRIDE + q for a, b in spans for d in range(self.inner) for q in range(a, b)]],
            np.int32,
        )

    def order(self, z):
        rest = [s for s in range(self.outer) if s not in (z, z ^ 1)]
        return [z, z ^ 1] + sorted(rest, key=lambda s: abs(s - z))

    def swap(self, z, odd):
        to = z - 1 if (z % 2 == 0) == odd else z + 1
        return to if 0 <= to < self.outer else z

    def trace(self):
        held = {0: list(range(self.outer))}
        for chain in (0, 1):
            last = held[0]
            for r in range(1, self.outer):
                odd = (r % 2 == 0) == (chain == 0)
                last = [last[self.swap(z, odd)] for z in range(self.outer)]
                held[chain * (self.outer - 1) + r] = last
        return held

    def cand(self, z, source):
        step = lambda i: i if i < self.outer else i - self.outer + 1
        found = [i for i, held in self.trace().items() if held[z] == source]
        return min(found, key=lambda i: (step(i), i))

    def exchange(self, r, chain):
        odd = (r % 2 == 0) == (chain == 0)
        return [
            (z * self.inner + p, self.swap(z, odd) * self.inner + p)
            for z in range(self.outer)
            for p in range(self.inner)
        ]

    def used(self, a, b):
        slots = [k for k in range(self.outer) if k * self.cap < b and (k + 1) * self.cap > a]
        return sorted(
            {self.cand(z, self.order(z)[k]) for z in range(self.outer) for k in slots}
        )

    def partner(self, p, d):
        return p ^ d if self.inner & (self.inner - 1) == 0 else (d - p) % self.inner

    def table(self):
        rows = []
        for e in range(self.experts):
            z, p = divmod(e, self.inner)
            offs = [NOWHERE] * self.cands
            for slot, source in enumerate(self.order(z)):
                offs[self.cand(z, source)] = slot * self.cap
            experts = [z * self.inner + self.partner(p, d) for d in range(self.inner)]
            homes = [self.cand(z, z ^ r) for r in range(self.outer)]
            rows.append(offs + experts + homes)
        return np.array(rows, np.int32)

    def across(self, d):
        return [
            (z * self.inner + p, z * self.inner + self.partner(p, d))
            for z in range(self.outer)
            for p in range(self.inner)
        ]

    def flip(self, r):
        return [
            (z * self.inner + p, (z ^ r) * self.inner + p)
            for z in range(self.outer)
            for p in range(self.inner)
        ]


def pack_kernel(plan, tok_ref, up_ref, routes_ref, comb_ref, out_ref):
    tok, width = plan.tok, plan.width
    out_ref[:, :width] = tok_ref[...]
    out_ref[:, width : 2 * width] = up_ref[...]
    kind = lax.broadcasted_iota(jnp.int32, (LANES, tok), 0)
    weight = jnp.zeros((LANES, tok), F32)
    named = jnp.zeros((LANES, tok), F32)
    comb = comb_ref[...].astype(F32)
    for k in range(plan.top):
        e = routes_ref[k : k + 1, :]
        weight = jnp.where(kind == e, comb[k : k + 1, :], weight)
        named = jnp.where(kind == e + HALF, 1.0, named)
    row = lax.broadcasted_iota(jnp.int32, (tok, tok), 0)
    col = lax.broadcasted_iota(jnp.int32, (tok, tok), 1)
    upto = jnp.where(row <= col, 1.0, 0.0).astype(BF)
    count = jnp.dot(named.astype(BF), upto, preferred_element_type=F32)
    table = (weight + count * named).astype(BF)
    same = jnp.where(row == col, 1.0, 0.0).astype(BF)
    turned = lax.dot_general(same, table, NT, preferred_element_type=F32)
    out_ref[:, 2 * width :] = turned.astype(BF)


def picks(plan, meta, off, experts, key, scaled):
    tok = meta.shape[0]
    lane = lax.broadcasted_iota(jnp.int32, (tok, LANES), 1)
    one = jnp.zeros((tok, key.shape[1]), F32)
    two = jnp.zeros((tok, key.shape[1]), F32)
    for d, e in enumerate(experts):
        place = jnp.sum(jnp.where(lane == e + HALF, meta, 0.0), axis=1, keepdims=True)
        place = place.astype(jnp.int32)
        spot = jnp.where(place > 0, place - 1 + off + d * STRIDE, -1)
        hit = spot == key
        one = jnp.where(hit, 1.0, one)
        if scaled:
            weight = jnp.sum(jnp.where(lane == e, meta, 0.0), axis=1, keepdims=True)
            two = jnp.where(hit, weight, two)
    return one, two


def compact_kernel(plan, chunk, *refs):
    use, rows = plan.use[chunk], plan.rows[chunk]
    n, width, tok, inner = len(use), plan.width, plan.tok, plan.inner
    info, key_ref = refs[:2]
    blocks, outs = refs[2 : 2 + n], refs[2 + n : 2 + n + inner]
    held, one_s, two_s, sems = refs[2 + n + inner :]
    copies = [
        pltpu.make_async_copy(b, held.at[pl.ds(i * tok, tok)], sems.at[i])
        for i, b in enumerate(blocks)
    ]
    for c in copies:
        c.start()
    experts = [info[plan.cands + d] for d in range(inner)]
    for i, c in enumerate(copies):
        c.wait()
        meta = held[i * tok : (i + 1) * tok, 2 * width :].astype(F32)
        one, two = picks(plan, meta, info[use[i]], experts, key_ref[...], True)
        one_s[i * tok : (i + 1) * tok, :] = one.astype(BF)
        two_s[i * tok : (i + 1) * tok, :] = two.astype(BF)
    for part, source in ((0, one_s), (1, two_s)):
        have = held[:, part * width : (part + 1) * width]
        found = lax.dot_general(source[...], have, TN, preferred_element_type=F32).astype(BF)
        for d in range(inner):
            outs[d][part * rows : (part + 1) * rows, :] = found[d * rows : (d + 1) * rows]


def pieces(plan, group, got, x_s, d_s, sems, base=0):
    inner, size, first = plan.inner, plan.sizes[group], plan.spans[group][0]
    x_copies, d_copies = [], []
    for i, g in enumerate(got):
        c, d = plan.groups[group][i // inner], i % inner
        rows = plan.rows[c]
        to = pl.ds(base + d * size + plan.chunks[c][0] - first, rows)
        x_copies.append(pltpu.make_async_copy(g.at[pl.ds(0, rows)], x_s.at[to], sems.at[2 * i]))
        d_copies.append(
            pltpu.make_async_copy(g.at[pl.ds(rows, rows)], d_s.at[to], sems.at[2 * i + 1])
        )
    return x_copies, d_copies


def expert_kernel(plan, group, *refs):
    inner, rows, width, hidden = plan.inner, plan.sizes[group], plan.width, plan.hidden
    part, count, n = hidden // 2, inner * rows, inner * len(plan.groups[group])
    info = refs[0]
    got, weights = refs[1 : 1 + n], refs[1 + n : 6 + n]
    hid_o, gate_o, up_o = refs[6 + n : 9 + n]
    backs = refs[9 + n : 9 + n + inner]
    x_s, d_s, wg_s, wu_s, wd_s, comb_s, sems = refs[9 + n + inner :]
    own_g, own_u, own_d, both, other_d = [w.at[0] for w in weights]
    views = [
        (own_g, both.at[:, pl.ds(0, part)]),
        (own_u, both.at[:, pl.ds(part, part)]),
        (own_d, other_d),
    ]
    x_copies, d_copies = pieces(plan, group, got, x_s, d_s, sems)
    tile, tiles = hidden, []
    for t in range(hidden // tile):
        for kind, where in ((0, wg_s), (1, wu_s), (2, wd_s)):
            at, here = t * tile, []
            while at < (t + 1) * tile:
                half, start = divmod(at, part)
                size = min((t + 1) * tile, (half + 1) * part) - at
                source, to = pl.ds(start, size), pl.ds(at, size)
                w = views[kind][half]
                here.append((w.at[source], where.at[to]) if kind == 2 else (w.at[:, source], where.at[:, to]))
                at += size
            tiles.append(here)
    w_copies, used = [], 2 * n
    for here in tiles:
        w_copies.append([])
        for source, to in here:
            w_copies[-1].append(pltpu.make_async_copy(source, to, sems.at[used]))
            used += 1
    for c in x_copies + w_copies[0] + w_copies[1] + d_copies:
        c.start()
    for here in w_copies[2:]:
        for c in here:
            c.start()
    for t in range(hidden // tile):
        at = slice(t * tile, (t + 1) * tile)
        gate_w, up_w, down_w = w_copies[3 * t : 3 * t + 3]
        for c in (x_copies if t == 0 else []) + gate_w:
            c.wait()
        gate = jnp.dot(x_s[...], wg_s[:, at], preferred_element_type=F32)
        for c in up_w:
            c.wait()
        up = jnp.dot(x_s[...], wu_s[:, at], preferred_element_type=F32)
        for c in (d_copies if t == 0 else []) + down_w:
            c.wait()
        mixed = lax.dot_general(d_s[...], wd_s[at, :], NT, preferred_element_type=F32)
        logistic = jax.nn.sigmoid(gate)
        silu = gate * logistic
        hid = (silu * up).astype(BF)
        hid_o[:, at] = hid
        comb = jnp.sum(hid.astype(F32) * mixed, axis=1, keepdims=True)
        comb_s[...] = comb if t == 0 else comb_s[...] + comb
        gate_o[:, at] = (mixed * up * logistic * (1.0 + gate * (1.0 - logistic))).astype(BF)
        up_o[:, at] = (mixed * silu).astype(BF)

    wide = width // 2

    @pl.loop(0, width // wide)
    def _(j):
        at = pl.ds(pl.multiple_of(j * wide, wide), wide)
        back = lax.dot_general(gate_o[...], wg_s[at, :], NT, preferred_element_type=F32)
        back += lax.dot_general(up_o[...], wu_s[at, :], NT, preferred_element_type=F32)
        back = back.astype(BF)
        for d in range(inner):
            backs[d][:, at] = back[d * rows : (d + 1) * rows]

    lane = lax.broadcasted_iota(jnp.int32, (count, LANES), 1)
    comb = jnp.where(lane == info[plan.cands], comb_s[...], 0.0).astype(BF)
    for d in range(inner):
        backs[d][:, width:] = comb[d * rows : (d + 1) * rows]


def weight_kernel(plan, own, extra, *refs):
    inner, width, hidden = plan.inner, plan.width, plan.hidden
    part, n = hidden // 2, plan.inner * PARTS
    got, mids = refs[:n], refs[n : n + 6]
    at = n + 6
    theirs = refs[at : at + 3] if own else None
    at += extra
    outs = refs[at : at + 3]
    x_s, d_s, h_s, gu_s, g_s, u_s, w_s, sems, mid_sems, out_sems = refs[at + 3 : at + 13]
    kept = refs[at + 13 :]
    first, second, base, taken = [], [], 0, 0
    half = pl.ds(0 if own else part, part)
    for g in range(2):
        many = inner * len(plan.groups[g])
        mine = got[taken : taken + many]
        at_sems = sems.at[pl.ds(2 * taken, 2 * many)]
        x_copies, d_copies = pieces(plan, g, mine, x_s, d_s, at_sems, base)
        first += x_copies
        second += d_copies
        to = pl.ds(base, inner * plan.sizes[g])
        spots = (h_s.at[to], gu_s.at[to, pl.ds(0, part)], gu_s.at[to, pl.ds(part, part)])
        for i, (m, s) in enumerate(zip(mids[3 * g : 3 * g + 3], spots)):
            copy = pltpu.make_async_copy(m.at[:, half], s, mid_sems.at[3 * g + i])
            (second if i == 0 else first).append(copy)
        taken += many
        base += inner * plan.sizes[g]
    came = []
    if own:
        came = [
            pltpu.make_async_copy(t.at[0], k, out_sems.at[5 + i])
            for i, (t, k) in enumerate(zip(theirs, kept))
        ]
    for c in first + came[:2] + second + came[2:]:
        c.start()
    for c in first + came[:2]:
        c.wait()
    tile, left = width // 2, []
    for j in range(2):
        to = slice(j * tile, (j + 1) * tile)
        both = lax.dot_general(x_s[:, to], gu_s[...], TN, preferred_element_type=F32)
        for i, (o, s) in enumerate(zip(outs, (g_s, u_s))):
            value = both[:, i * part : (i + 1) * part]
            if own:
                value += kept[i][to, :].astype(F32)
            s[to, :] = value.astype(BF)
            rows = pl.ds(j * tile, tile)
            left.append(
                pltpu.make_async_copy(s.at[rows], o.at[0, rows], out_sems.at[2 * j + i])
            )
            left[-1].start()
    for c in second + came[2:]:
        c.wait()
    down = lax.dot_general(h_s[...], d_s[...], TN, preferred_element_type=F32)
    if own:
        down += kept[2][...].astype(F32)
    w_s[...] = down.astype(BF)
    left.append(pltpu.make_async_copy(w_s, outs[2].at[0], out_sems.at[4]))
    left[-1].start()
    for c in left:
        c.wait()


def spread_kernel(plan, homes, groups, *refs):
    inner, tok, width = plan.inner, plan.tok, plan.width
    info, key_ref = refs[:2]
    blocks = refs[2 : 2 + plan.cands]
    at = 2 + plan.cands
    backs = refs[at : at + groups * inner]
    outs = list(refs[at + groups * inner : -5])
    outs = outs[len(outs) - len(plan.halves) :]
    held, metas, pick_s, sems, meta_sems = refs[-5:]
    copies, later, start = [], [], 0
    for i, b in enumerate(blocks):
        copies.append(
            pltpu.make_async_copy(b.at[:, pl.ds(2 * width, LANES)], metas.at[i], meta_sems.at[i])
        )
    for i, b in enumerate(backs):
        rows = plan.sizes[i // inner]
        later.append(pltpu.make_async_copy(b, held.at[pl.ds(start, rows)], sems.at[i]))
        start += rows
    for c in copies + later:
        c.start()
    for c in copies:
        c.wait()
    experts = [info[plan.cands + d] for d in range(inner)]
    for i, r in enumerate(homes):
        which = info[plan.cands + inner + r]
        meta = metas[which].astype(F32)
        one, _ = picks(plan, meta, info[which], experts, key_ref[...], False)
        pick_s[i * tok : (i + 1) * tok, :] = one.astype(BF)
    for c in later:
        c.wait()
    sums = jnp.dot(pick_s[...], held[...], preferred_element_type=F32).astype(BF)
    for o, (r, a, b) in zip(outs, plan.halves):
        o[...] = sums[r * tok : (r + 1) * tok, a:b]


def home_kernel(plan, count, *refs):
    parts = refs[:count]
    routes_ref, comb_ref, _, tok_o, comb_o = refs[count:]
    width, tok = plan.width, plan.tok
    middle = width // 2
    total = parts[0][...].astype(F32) + parts[1][...].astype(F32)
    low, high = total[:, :middle], total[:, middle:]
    for p in parts[2::2]:
        low += p[...].astype(F32)
    for p in parts[3::2]:
        high += p[...].astype(F32)
    tok_o[:, :middle] = low.astype(BF)
    tok_o[:, middle:] = high[:, :middle].astype(BF)
    row = lax.broadcasted_iota(jnp.int32, (LANES, LANES), 0)
    col = lax.broadcasted_iota(jnp.int32, (LANES, LANES), 1)
    same = jnp.where(row == col, 1.0, 0.0).astype(BF)
    found = high[:, width - middle :].astype(BF)
    found = lax.dot_general(same, found, NT, preferred_element_type=F32)
    kind = lax.broadcasted_iota(jnp.int32, (LANES, tok), 0)
    out = []
    for k in range(plan.top):
        mine = jnp.where(kind == routes_ref[k : k + 1, :], found, 0.0)
        out.append(jnp.sum(mine, axis=0, keepdims=True))
    out = jnp.concatenate(out, axis=0)
    comb_o[...] = (out / comb_ref[...].astype(F32)).astype(BF)


def on_device(plan, tokens, routes, combine, upstream, w_gate, w_up, w_down):
    tok, width, hidden = plan.tok, plan.width, plan.hidden
    inner, outer, part = plan.inner, plan.outer, plan.hidden // 2
    full = 2 * width + LANES
    shape = jax.ShapeDtypeStruct
    info = jnp.asarray(plan.table())[lax.axis_index("expert")]
    swap = [(0, 1), (1, 0)]

    block = pl.pallas_call(
        functools.partial(pack_kernel, plan),
        out_shape=shape((tok, full), BF),
        in_specs=[VMEM] * 4,
        out_specs=VMEM,
        compiler_params=params(),
        cost_estimate=cost(1e6, 4 * tok * full),
        name="pack",
    )(tokens, upstream, routes.T, combine.T)

    gate_up = jnp.concatenate([w_gate, w_up], axis=2)
    blocks = [block] * plan.cands

    def hop(r):
        for chain in (0, 1):
            if r <= plan.last[chain]:
                i = chain * (outer - 1) + r
                before = block if r == 1 else blocks[i - 1]
                blocks[i] = lax.ppermute(before, "expert", plan.exchange(r, chain))
        if 1 < r <= min(plan.last):
            i = outer - 1 + r
            blocks[r], blocks[i] = lax.optimization_barrier((blocks[r], blocks[i]))

    hop(1)
    def compact(c):
        rows, use = plan.rows[c], plan.use[c]
        count, n = inner * rows, len(use)
        return pl.pallas_call(
            functools.partial(compact_kernel, plan, c),
            out_shape=[shape((2 * rows, width), BF)] * inner,
            in_specs=[SMEM, VMEM] + [ANY] * n,
            out_specs=[VMEM] * inner,
            scratch_shapes=[
                pltpu.VMEM((n * tok, full), BF),
                pltpu.VMEM((n * tok, count), BF),
                pltpu.VMEM((n * tok, count), BF),
                pltpu.SemaphoreType.DMA((n,)),
            ],
            compiler_params=params(),
            cost_estimate=cost(4 * n * tok * count * width, 2 * n * tok * full),
            name="compact",
        )(info, jnp.asarray(plan.keys([plan.chunks[c]])), *[blocks[i] for i in use])

    def expert(g, arrived):
        rows, n = plan.sizes[g], inner * len(plan.groups[g])
        count = inner * rows
        return pl.pallas_call(
            functools.partial(expert_kernel, plan, g),
            out_shape=[shape((count, hidden), BF)] * 3
            + [shape((rows, width + LANES), BF)] * inner,
            in_specs=[SMEM] + [ANY] * (n + 5),
            out_specs=[VMEM] * (3 + inner),
            scratch_shapes=[
                pltpu.VMEM((count, width), BF),
                pltpu.VMEM((count, width), BF),
                pltpu.VMEM((width, hidden), BF),
                pltpu.VMEM((width, hidden), BF),
                pltpu.VMEM((hidden, width), BF),
                pltpu.VMEM((count, 1), F32),
                pltpu.SemaphoreType.DMA((2 * n + 6 * (hidden // 128),)),
            ],
            compiler_params=params(),
            cost_estimate=cost(10 * count * hidden * width, 6 * hidden * width),
            name="expert",
        )(info, *arrived, *weights)

    def cross(arrays):
        return [arrays[0]] + [
            lax.ppermute(arrays[d], "expert", plan.across(d)) for d in range(1, inner)
        ]

    got, done = [], 1
    for c in range(PARTS):
        for r in range(done + 1, plan.steps[c] + 1):
            hop(r)
        done = max(done, plan.steps[c])
        sent = compact(c)
        if c > 0:
            got[-1], sent = lax.optimization_barrier((got[-1], sent))
        if c == PARTS - 2:
            gate_up, sent = lax.optimization_barrier((gate_up, sent))
            gate_up = lax.ppermute(gate_up, "dp", swap)
        if c == PARTS - 1:
            gate_up, sent = lax.optimization_barrier((gate_up, sent))
            down = lax.ppermute(lax.optimization_barrier((w_down, sent))[0], "dp", swap)
        got.append(cross(sent))
        if c == 0:
            i = outer - 1 + done
            got[0], blocks[done], blocks[i] = lax.optimization_barrier(
                (got[0], blocks[done], blocks[i])
            )
    weights = [w_gate, w_up, w_down, gate_up, down]
    outs = expert(0, sum(got[:-1], []))
    outs = list(outs)
    outs[0], late = lax.optimization_barrier((outs[0], got[-1]))
    got[-1] = late
    backs = cross(outs[3:])
    more = expert(1, late)
    got = sum(got, [])
    mids = outs[:3] + list(more[:3])

    count = inner * sum(plan.rows)

    grad_scratch = [
        pltpu.VMEM((width, part), BF),
        pltpu.VMEM((width, part), BF),
        pltpu.VMEM((part, width), BF),
    ]

    def weight_grads(own, extra):
        return pl.pallas_call(
            functools.partial(weight_kernel, plan, own, len(extra)),
            out_shape=[
                shape((1, width, part), BF),
                shape((1, width, part), BF),
                shape((1, part, width), BF),
            ],
            in_specs=[ANY] * (inner * PARTS + 6 + len(extra)),
            out_specs=[ANY] * 3,
            scratch_shapes=[
                pltpu.VMEM((count, width), BF),
                pltpu.VMEM((count, width), BF),
                pltpu.VMEM((count, part), BF),
                pltpu.VMEM((count, 2 * part), BF),
                *grad_scratch,
                pltpu.SemaphoreType.DMA((2 * inner * PARTS,)),
                pltpu.SemaphoreType.DMA((6,)),
                pltpu.SemaphoreType.DMA((8,)),
                *(grad_scratch if own else []),
            ],
            compiler_params=params(64 if own else 60),
            cost_estimate=cost(6 * count * part * width, 4 * count * (width + hidden)),
            name="weight_grads",
        )(*got, *mids, *extra)

    def spread(homes, groups, extra):
        slots = inner * sum(plan.sizes[:groups])
        return pl.pallas_call(
            functools.partial(spread_kernel, plan, homes, groups),
            out_shape=[shape((tok, b - a), BF) for _, a, b in plan.halves],
            in_specs=[SMEM, VMEM] + [ANY] * (plan.cands + groups * inner + len(extra)),
            out_specs=[VMEM] * len(plan.halves),
            scratch_shapes=[
                pltpu.VMEM((slots, width + LANES), BF),
                pltpu.VMEM((plan.cands, tok, LANES), BF),
                pltpu.VMEM((len(homes) * tok, slots), BF),
                pltpu.SemaphoreType.DMA((groups * inner,)),
                pltpu.SemaphoreType.DMA((plan.cands,)),
            ],
            compiler_params=params(),
            cost_estimate=cost(2 * len(homes) * tok * slots * width, 2 * slots * width),
            name="spread",
        )(
            info,
            jnp.asarray(plan.keys(plan.spans[:groups])),
            *blocks,
            *backs[: groups * inner],
            *extra,
        )

    mine = weight_grads(False, backs[1:inner])
    backs = backs + cross(more[3:])
    mine, backs = lax.optimization_barrier((mine, backs))
    theirs = [lax.ppermute(w, "dp", swap) for w in mine]
    cut = spread(list(range(outer)), 2, [mine[0]])
    sums = {(r, a): part for (r, a, b), part in zip(plan.halves, cut)}
    came, bit, starts = [], 1, (0, width // 2)
    while bit < outer:
        for r in range(outer - bit, 0, -2 * bit):
            if r == 1:
                came.append(lax.ppermute(sums[1, 0], "expert", plan.flip(1)))
                continue
            for a in starts:
                sent = lax.ppermute(sums[r, a], "expert", plan.flip(bit))
                if r == bit:
                    came.append(sent)
                    continue
                if bit == 1:
                    sums[1, 0], sent = lax.optimization_barrier((sums[1, 0], sent))
                total = sums[r - bit, a].astype(F32) + sent.astype(F32)
                sums[r - bit, a] = total.astype(BF)
        bit *= 2
    grads = weight_grads(True, theirs)
    home = [sums[0, 0]] + came
    grad_tokens, grad_combine = pl.pallas_call(
        functools.partial(home_kernel, plan, len(home)),
        out_shape=[shape((tok, width), BF), shape((plan.top, tok), BF)],
        in_specs=[VMEM] * (len(home) + 2) + [ANY],
        out_specs=[VMEM] * 2,
        compiler_params=params(),
        cost_estimate=cost(1e6, 2 * tok * width * (outer + 1)),
        name="home",
    )(*home, routes.T, combine.T, grads[0])
    return (grad_tokens, grad_combine.T, *grads)


def solution(mesh):
    rows = P(("parts", "dp", "expert"), None)
    in_specs = (rows,) * 4 + (P("expert", None, "dp"),) * 2 + (P("expert", "dp", None),)
    out_specs = (rows,) * 2 + (P(("parts", "expert"), None, "dp"),) * 2
    out_specs += (P(("parts", "expert"), "dp", None),)
    shape = dict(mesh.shape)

    def whole(tokens, routes, combine, upstream, w_gate, w_up, w_down):
        devices = shape["parts"] * shape["dp"] * shape["expert"]
        plan = Plan(
            shape["expert"],
            tokens.shape[0] // devices,
            routes.shape[1],
            tokens.shape[1],
            w_gate.shape[2],
        )
        body = functools.partial(on_device, plan)
        return jax.shard_map(
            body, mesh=mesh, in_specs=in_specs, out_specs=out_specs, check_vma=False
        )(tokens, routes, combine, upstream, w_gate, w_up, w_down)

    return whole
```

```python
import functools

import jax
import jax.numpy as jnp
import numpy as np
from jax import lax
from jax.experimental import pallas as pl
from jax.experimental.pallas import tpu as pltpu
from jax.sharding import PartitionSpec as P

BF = jnp.bfloat16
F32 = jnp.float32
LANES = 128
HALF = 64
STRIDE = 1024
PARTS = 4
NOWHERE = -(1 << 20)
ANY = pl.BlockSpec(memory_space=pltpu.HBM)
VMEM = pl.BlockSpec(memory_space=pltpu.VMEM)
SMEM = pl.BlockSpec(memory_space=pltpu.SMEM)
TN = (((0,), (0,)), ((), ()))
NT = (((1,), (1,)), ((), ()))


def params(megabytes=60):
    return pltpu.CompilerParams(vmem_limit_bytes=megabytes << 20)


def cost(flops, moved):
    return pl.CostEstimate(flops=int(flops), bytes_accessed=int(moved), transcendentals=0)


class Plan:
    def __init__(self, experts, tok, top, width, hidden):
        self.experts, self.tok, self.top = experts, tok, top
        self.width, self.hidden = width, hidden
        outer = 1
        while outer * outer < experts:
            outer *= 2
        self.outer, self.inner = outer, experts // outer
        mean = tok * top // experts
        self.cap = min(tok, max(2, mean + tok * top // (8 * experts)))
        total = -(-self.outer * self.cap // 16) * 16
        step = self.outer // PARTS
        marks = [k * step * self.cap // 16 * 16 for k in range(PARTS)] + [total]
        if marks[1] >= 32:
            marks[1] = marks[1] // 32 * 16
            marks[2] = marks[1] + 32
        self.chunks = [(marks[k], marks[k + 1]) for k in range(PARTS)]
        self.rows = [b - a for a, b in self.chunks]
        self.steps = [(k + 1) * step - 1 for k in range(PARTS)]
        self.groups = [range(PARTS - 1), range(PARTS - 1, PARTS)]
        self.spans = [(marks[g[0]], marks[g[-1] + 1]) for g in self.groups]
        self.sizes = [b - a for a, b in self.spans]
        self.cands = 2 * self.outer - 1
        self.use = [self.used(*c) for c in self.chunks]
        middle, end = width // 2, width + LANES
        self.halves = [(0, 0, end), (1, 0, end)] + [
            (r, a, b) for r in range(2, outer) for a, b in ((0, middle), (middle, end))
        ]
        needed = set().union(*self.use)
        self.last = [
            max(i for i in needed if 0 < i < outer),
            max(i for i in needed if i >= outer) - outer + 1,
        ]

    def keys(self, spans):
        return np.array(
            [[d * STRIDE + q for a, b in spans for d in range(self.inner) for q in range(a, b)]],
            np.int32,
        )

    def order(self, z):
        rest = [s for s in range(self.outer) if s not in (z, z ^ 1)]
        return [z, z ^ 1] + sorted(rest, key=lambda s: abs(s - z))

    def swap(self, z, odd):
        to = z - 1 if (z % 2 == 0) == odd else z + 1
        return to if 0 <= to < self.outer else z

    def trace(self):
        held = {0: list(range(self.outer))}
        for chain in (0, 1):
            last = held[0]
            for r in range(1, self.outer):
                odd = (r % 2 == 0) == (chain == 0)
                last = [last[self.swap(z, odd)] for z in range(self.outer)]
                held[chain * (self.outer - 1) + r] = last
        return held

    def cand(self, z, source):
        step = lambda i: i if i < self.outer else i - self.outer + 1
        found = [i for i, held in self.trace().items() if held[z] == source]
        return min(found, key=lambda i: (step(i), i))

    def exchange(self, r, chain):
        odd = (r % 2 == 0) == (chain == 0)
        return [
            (z * self.inner + p, self.swap(z, odd) * self.inner + p)
            for z in range(self.outer)
            for p in range(self.inner)
        ]

    def used(self, a, b):
        slots = [k for k in range(self.outer) if k * self.cap < b and (k + 1) * self.cap > a]
        return sorted(
            {self.cand(z, self.order(z)[k]) for z in range(self.outer) for k in slots}
        )

    def partner(self, p, d):
        return p ^ d if self.inner & (self.inner - 1) == 0 else (d - p) % self.inner

    def table(self):
        rows = []
        for e in range(self.experts):
            z, p = divmod(e, self.inner)
            offs = [NOWHERE] * self.cands
            for slot, source in enumerate(self.order(z)):
                offs[self.cand(z, source)] = slot * self.cap
            experts = [z * self.inner + self.partner(p, d) for d in range(self.inner)]
            homes = [self.cand(z, z ^ r) for r in range(self.outer)]
            rows.append(offs + experts + homes)
        return np.array(rows, np.int32)

    def across(self, d):
        return [
            (z * self.inner + p, z * self.inner + self.partner(p, d))
            for z in range(self.outer)
            for p in range(self.inner)
        ]

    def flip(self, r):
        return [
            (z * self.inner + p, (z ^ r) * self.inner + p)
            for z in range(self.outer)
            for p in range(self.inner)
        ]


def pack_kernel(plan, tok_ref, up_ref, routes_ref, comb_ref, out_ref):
    tok, width = plan.tok, plan.width
    out_ref[:, :width] = tok_ref[...]
    out_ref[:, width : 2 * width] = up_ref[...]
    kind = lax.broadcasted_iota(jnp.int32, (LANES, tok), 0)
    weight = jnp.zeros((LANES, tok), F32)
    named = jnp.zeros((LANES, tok), F32)
    comb = comb_ref[...].astype(F32)
    for k in range(plan.top):
        e = routes_ref[k : k + 1, :]
        weight = jnp.where(kind == e, comb[k : k + 1, :], weight)
        named = jnp.where(kind == e + HALF, 1.0, named)
    row = lax.broadcasted_iota(jnp.int32, (tok, tok), 0)
    col = lax.broadcasted_iota(jnp.int32, (tok, tok), 1)
    upto = jnp.where(row <= col, 1.0, 0.0).astype(BF)
    count = jnp.dot(named.astype(BF), upto, preferred_element_type=F32)
    table = (weight + count * named).astype(BF)
    same = jnp.where(row == col, 1.0, 0.0).astype(BF)
    turned = lax.dot_general(same, table, NT, preferred_element_type=F32)
    out_ref[:, 2 * width :] = turned.astype(BF)


def picks(plan, meta, off, experts, key, scaled):
    tok = meta.shape[0]
    lane = lax.broadcasted_iota(jnp.int32, (tok, LANES), 1)
    one = jnp.zeros((tok, key.shape[1]), F32)
    two = jnp.zeros((tok, key.shape[1]), F32)
    for d, e in enumerate(experts):
        place = jnp.sum(jnp.where(lane == e + HALF, meta, 0.0), axis=1, keepdims=True)
        place = place.astype(jnp.int32)
        spot = jnp.where(place > 0, place - 1 + off + d * STRIDE, -1)
        hit = spot == key
        one = jnp.where(hit, 1.0, one)
        if scaled:
            weight = jnp.sum(jnp.where(lane == e, meta, 0.0), axis=1, keepdims=True)
            two = jnp.where(hit, weight, two)
    return one, two


def compact_kernel(plan, chunk, *refs):
    use, rows = plan.use[chunk], plan.rows[chunk]
    n, width, tok, inner = len(use), plan.width, plan.tok, plan.inner
    info, key_ref = refs[:2]
    blocks, outs = refs[2 : 2 + n], refs[2 + n : 2 + n + inner]
    held, one_s, two_s, sems = refs[2 + n + inner :]
    copies = [
        pltpu.make_async_copy(b, held.at[pl.ds(i * tok, tok)], sems.at[i])
        for i, b in enumerate(blocks)
    ]
    for c in copies:
        c.start()
    experts = [info[plan.cands + d] for d in range(inner)]
    for i, c in enumerate(copies):
        c.wait()
        meta = held[i * tok : (i + 1) * tok, 2 * width :].astype(F32)
        one, two = picks(plan, meta, info[use[i]], experts, key_ref[...], True)
        one_s[i * tok : (i + 1) * tok, :] = one.astype(BF)
        two_s[i * tok : (i + 1) * tok, :] = two.astype(BF)
    for part, source in ((0, one_s), (1, two_s)):
        have = held[:, part * width : (part + 1) * width]
        found = lax.dot_general(source[...], have, TN, preferred_element_type=F32).astype(BF)
        for d in range(inner):
            outs[d][part * rows : (part + 1) * rows, :] = found[d * rows : (d + 1) * rows]


def pieces(plan, group, got, x_s, d_s, sems, base=0):
    inner, size, first = plan.inner, plan.sizes[group], plan.spans[group][0]
    x_copies, d_copies = [], []
    for i, g in enumerate(got):
        c, d = plan.groups[group][i // inner], i % inner
        rows = plan.rows[c]
        to = pl.ds(base + d * size + plan.chunks[c][0] - first, rows)
        x_copies.append(pltpu.make_async_copy(g.at[pl.ds(0, rows)], x_s.at[to], sems.at[2 * i]))
        d_copies.append(
            pltpu.make_async_copy(g.at[pl.ds(rows, rows)], d_s.at[to], sems.at[2 * i + 1])
        )
    return x_copies, d_copies


def expert_kernel(plan, group, *refs):
    inner, rows, width, hidden = plan.inner, plan.sizes[group], plan.width, plan.hidden
    part, count, n = hidden // 2, inner * rows, inner * len(plan.groups[group])
    info = refs[0]
    got, weights = refs[1 : 1 + n], refs[1 + n : 6 + n]
    hid_o, gate_o, up_o = refs[6 + n : 9 + n]
    backs = refs[9 + n : 9 + n + inner]
    x_s, d_s, wg_s, wu_s, wd_s, comb_s, sems = refs[9 + n + inner :]
    own_g, own_u, own_d, both, other_d = [w.at[0] for w in weights]
    views = [
        (own_g, both.at[:, pl.ds(0, part)]),
        (own_u, both.at[:, pl.ds(part, part)]),
        (own_d, other_d),
    ]
    x_copies, d_copies = pieces(plan, group, got, x_s, d_s, sems)
    tile, tiles = hidden, []
    for t in range(hidden // tile):
        for kind, where in ((0, wg_s), (1, wu_s), (2, wd_s)):
            at, here = t * tile, []
            while at < (t + 1) * tile:
                half, start = divmod(at, part)
                size = min((t + 1) * tile, (half + 1) * part) - at
                source, to = pl.ds(start, size), pl.ds(at, size)
                w = views[kind][half]
                here.append((w.at[source], where.at[to]) if kind == 2 else (w.at[:, source], where.at[:, to]))
                at += size
            tiles.append(here)
    w_copies, used = [], 2 * n
    for here in tiles:
        w_copies.append([])
        for source, to in here:
            w_copies[-1].append(pltpu.make_async_copy(source, to, sems.at[used]))
            used += 1
    for c in x_copies + w_copies[0] + w_copies[1] + d_copies:
        c.start()
    for here in w_copies[2:]:
        for c in here:
            c.start()
    for t in range(hidden // tile):
        at = slice(t * tile, (t + 1) * tile)
        gate_w, up_w, down_w = w_copies[3 * t : 3 * t + 3]
        for c in (x_copies if t == 0 else []) + gate_w:
            c.wait()
        gate = jnp.dot(x_s[...], wg_s[:, at], preferred_element_type=F32)
        for c in up_w:
            c.wait()
        up = jnp.dot(x_s[...], wu_s[:, at], preferred_element_type=F32)
        for c in (d_copies if t == 0 else []) + down_w:
            c.wait()
        mixed = lax.dot_general(d_s[...], wd_s[at, :], NT, preferred_element_type=F32)
        logistic = jax.nn.sigmoid(gate)
        silu = gate * logistic
        hid = (silu * up).astype(BF)
        hid_o[:, at] = hid
        comb = jnp.sum(hid.astype(F32) * mixed, axis=1, keepdims=True)
        comb_s[...] = comb if t == 0 else comb_s[...] + comb
        gate_o[:, at] = (mixed * up * logistic * (1.0 + gate * (1.0 - logistic))).astype(BF)
        up_o[:, at] = (mixed * silu).astype(BF)

    wide = width // 2

    @pl.loop(0, width // wide)
    def _(j):
        at = pl.ds(pl.multiple_of(j * wide, wide), wide)
        back = lax.dot_general(gate_o[...], wg_s[at, :], NT, preferred_element_type=F32)
        back += lax.dot_general(up_o[...], wu_s[at, :], NT, preferred_element_type=F32)
        back = back.astype(BF)
        for d in range(inner):
            backs[d][:, at] = back[d * rows : (d + 1) * rows]

    lane = lax.broadcasted_iota(jnp.int32, (count, LANES), 1)
    comb = jnp.where(lane == info[plan.cands], comb_s[...], 0.0).astype(BF)
    for d in range(inner):
        backs[d][:, width:] = comb[d * rows : (d + 1) * rows]


def weight_kernel(plan, own, extra, *refs):
    inner, width, hidden = plan.inner, plan.width, plan.hidden
    part, n = hidden // 2, plan.inner * PARTS
    got, mids = refs[:n], refs[n : n + 6]
    at = n + 6
    theirs = refs[at : at + 3] if own else None
    at += extra
    outs = refs[at : at + 3]
    x_s, d_s, h_s, gu_s, g_s, u_s, w_s, sems, mid_sems, out_sems = refs[at + 3 : at + 13]
    kept = refs[at + 13 :]
    first, second, base, taken = [], [], 0, 0
    half = pl.ds(0 if own else part, part)
    for g in range(2):
        many = inner * len(plan.groups[g])
        mine = got[taken : taken + many]
        at_sems = sems.at[pl.ds(2 * taken, 2 * many)]
        x_copies, d_copies = pieces(plan, g, mine, x_s, d_s, at_sems, base)
        first += x_copies
        second += d_copies
        to = pl.ds(base, inner * plan.sizes[g])
        spots = (h_s.at[to], gu_s.at[to, pl.ds(0, part)], gu_s.at[to, pl.ds(part, part)])
        for i, (m, s) in enumerate(zip(mids[3 * g : 3 * g + 3], spots)):
            copy = pltpu.make_async_copy(m.at[:, half], s, mid_sems.at[3 * g + i])
            (second if i == 0 else first).append(copy)
        taken += many
        base += inner * plan.sizes[g]
    came = []
    if own:
        came = [
            pltpu.make_async_copy(t.at[0], k, out_sems.at[5 + i])
            for i, (t, k) in enumerate(zip(theirs, kept))
        ]
    for c in first + came[:2] + second + came[2:]:
        c.start()
    for c in first + came[:2]:
        c.wait()
    tile, left = width // 2, []
    for j in range(2):
        to = slice(j * tile, (j + 1) * tile)
        both = lax.dot_general(x_s[:, to], gu_s[...], TN, preferred_element_type=F32)
        for i, (o, s) in enumerate(zip(outs, (g_s, u_s))):
            value = both[:, i * part : (i + 1) * part]
            if own:
                value += kept[i][to, :].astype(F32)
            s[to, :] = value.astype(BF)
            rows = pl.ds(j * tile, tile)
            left.append(
                pltpu.make_async_copy(s.at[rows], o.at[0, rows], out_sems.at[2 * j + i])
            )
            left[-1].start()
    for c in second + came[2:]:
        c.wait()
    down = lax.dot_general(h_s[...], d_s[...], TN, preferred_element_type=F32)
    if own:
        down += kept[2][...].astype(F32)
    w_s[...] = down.astype(BF)
    left.append(pltpu.make_async_copy(w_s, outs[2].at[0], out_sems.at[4]))
    left[-1].start()
    for c in left:
        c.wait()


def spread_kernel(plan, homes, groups, *refs):
    inner, tok, width = plan.inner, plan.tok, plan.width
    info, key_ref = refs[:2]
    blocks = refs[2 : 2 + plan.cands]
    at = 2 + plan.cands
    backs = refs[at : at + groups * inner]
    outs = list(refs[at + groups * inner : -5])
    outs = outs[len(outs) - len(plan.halves) :]
    held, metas, pick_s, sems, meta_sems = refs[-5:]
    copies, later, start = [], [], 0
    for i, b in enumerate(blocks):
        copies.append(
            pltpu.make_async_copy(b.at[:, pl.ds(2 * width, LANES)], metas.at[i], meta_sems.at[i])
        )
    for i, b in enumerate(backs):
        rows = plan.sizes[i // inner]
        later.append(pltpu.make_async_copy(b, held.at[pl.ds(start, rows)], sems.at[i]))
        start += rows
    for c in copies + later:
        c.start()
    for c in copies:
        c.wait()
    experts = [info[plan.cands + d] for d in range(inner)]
    for i, r in enumerate(homes):
        which = info[plan.cands + inner + r]
        meta = metas[which].astype(F32)
        one, _ = picks(plan, meta, info[which], experts, key_ref[...], False)
        pick_s[i * tok : (i + 1) * tok, :] = one.astype(BF)
    for c in later:
        c.wait()
    sums = jnp.dot(pick_s[...], held[...], preferred_element_type=F32).astype(BF)
    for o, (r, a, b) in zip(outs, plan.halves):
        o[...] = sums[r * tok : (r + 1) * tok, a:b]


def home_kernel(plan, count, *refs):
    parts = refs[:count]
    routes_ref, comb_ref, _, tok_o, comb_o = refs[count:]
    width, tok = plan.width, plan.tok
    middle = width // 2
    total = parts[0][...].astype(F32) + parts[1][...].astype(F32)
    low, high = total[:, :middle], total[:, middle:]
    for p in parts[2::2]:
        low += p[...].astype(F32)
    for p in parts[3::2]:
        high += p[...].astype(F32)
    tok_o[:, :middle] = low.astype(BF)
    tok_o[:, middle:] = high[:, :middle].astype(BF)
    row = lax.broadcasted_iota(jnp.int32, (LANES, LANES), 0)
    col = lax.broadcasted_iota(jnp.int32, (LANES, LANES), 1)
    same = jnp.where(row == col, 1.0, 0.0).astype(BF)
    found = high[:, width - middle :].astype(BF)
    found = lax.dot_general(same, found, NT, preferred_element_type=F32)
    kind = lax.broadcasted_iota(jnp.int32, (LANES, tok), 0)
    out = []
    for k in range(plan.top):
        mine = jnp.where(kind == routes_ref[k : k + 1, :], found, 0.0)
        out.append(jnp.sum(mine, axis=0, keepdims=True))
    out = jnp.concatenate(out, axis=0)
    comb_o[...] = (out / comb_ref[...].astype(F32)).astype(BF)


def on_device(plan, tokens, routes, combine, upstream, w_gate, w_up, w_down):
    tok, width, hidden = plan.tok, plan.width, plan.hidden
    inner, outer, part = plan.inner, plan.outer, plan.hidden // 2
    full = 2 * width + LANES
    shape = jax.ShapeDtypeStruct
    info = jnp.asarray(plan.table())[lax.axis_index("expert")]
    swap = [(0, 1), (1, 0)]

    block = pl.pallas_call(
        functools.partial(pack_kernel, plan),
        out_shape=shape((tok, full), BF),
        in_specs=[VMEM] * 4,
        out_specs=VMEM,
        compiler_params=params(),
        cost_estimate=cost(1e6, 4 * tok * full),
        name="pack",
    )(tokens, upstream, routes.T, combine.T)

    gate_up = jnp.concatenate([w_gate, w_up], axis=2)
    blocks = [block] * plan.cands

    def hop(r):
        for chain in (0, 1):
            if r <= plan.last[chain]:
                i = chain * (outer - 1) + r
                before = block if r == 1 else blocks[i - 1]
                blocks[i] = lax.ppermute(before, "expert", plan.exchange(r, chain))
        if 1 < r <= min(plan.last):
            i = outer - 1 + r
            blocks[r], blocks[i] = lax.optimization_barrier((blocks[r], blocks[i]))

    hop(1)
    def compact(c):
        rows, use = plan.rows[c], plan.use[c]
        count, n = inner * rows, len(use)
        return pl.pallas_call(
            functools.partial(compact_kernel, plan, c),
            out_shape=[shape((2 * rows, width), BF)] * inner,
            in_specs=[SMEM, VMEM] + [ANY] * n,
            out_specs=[VMEM] * inner,
            scratch_shapes=[
                pltpu.VMEM((n * tok, full), BF),
                pltpu.VMEM((n * tok, count), BF),
                pltpu.VMEM((n * tok, count), BF),
                pltpu.SemaphoreType.DMA((n,)),
            ],
            compiler_params=params(),
            cost_estimate=cost(4 * n * tok * count * width, 2 * n * tok * full),
            name="compact",
        )(info, jnp.asarray(plan.keys([plan.chunks[c]])), *[blocks[i] for i in use])

    def expert(g, arrived):
        rows, n = plan.sizes[g], inner * len(plan.groups[g])
        count = inner * rows
        return pl.pallas_call(
            functools.partial(expert_kernel, plan, g),
            out_shape=[shape((count, hidden), BF)] * 3
            + [shape((rows, width + LANES), BF)] * inner,
            in_specs=[SMEM] + [ANY] * (n + 5),
            out_specs=[VMEM] * (3 + inner),
            scratch_shapes=[
                pltpu.VMEM((count, width), BF),
                pltpu.VMEM((count, width), BF),
                pltpu.VMEM((width, hidden), BF),
                pltpu.VMEM((width, hidden), BF),
                pltpu.VMEM((hidden, width), BF),
                pltpu.VMEM((count, 1), F32),
                pltpu.SemaphoreType.DMA((2 * n + 6 * (hidden // 128),)),
            ],
            compiler_params=params(),
            cost_estimate=cost(10 * count * hidden * width, 6 * hidden * width),
            name="expert",
        )(info, *arrived, *weights)

    def cross(arrays):
        return [arrays[0]] + [
            lax.ppermute(arrays[d], "expert", plan.across(d)) for d in range(1, inner)
        ]

    got, done = [], 1
    for c in range(PARTS):
        for r in range(done + 1, plan.steps[c] + 1):
            hop(r)
        done = max(done, plan.steps[c])
        sent = compact(c)
        if c > 0:
            got[-1], sent = lax.optimization_barrier((got[-1], sent))
        if c == PARTS - 2:
            gate_up, sent = lax.optimization_barrier((gate_up, sent))
            gate_up = lax.ppermute(gate_up, "dp", swap)
        if c == PARTS - 1:
            gate_up, sent = lax.optimization_barrier((gate_up, sent))
            down = lax.ppermute(lax.optimization_barrier((w_down, sent))[0], "dp", swap)
        got.append(cross(sent))
        if c == 0:
            i = outer - 1 + done
            got[0], blocks[done], blocks[i] = lax.optimization_barrier(
                (got[0], blocks[done], blocks[i])
            )
    weights = [w_gate, w_up, w_down, gate_up, down]
    outs = expert(0, sum(got[:-1], []))
    outs = list(outs)
    outs[0], late = lax.optimization_barrier((outs[0], got[-1]))
    got[-1] = late
    backs = cross(outs[3:])
    more = expert(1, late)
    got = sum(got, [])
    mids = outs[:3] + list(more[:3])

    count = inner * sum(plan.rows)

    grad_scratch = [
        pltpu.VMEM((width, part), BF),
        pltpu.VMEM((width, part), BF),
        pltpu.VMEM((part, width), BF),
    ]

    def weight_grads(own, extra):
        return pl.pallas_call(
            functools.partial(weight_kernel, plan, own, len(extra)),
            out_shape=[
                shape((1, width, part), BF),
                shape((1, width, part), BF),
                shape((1, part, width), BF),
            ],
            in_specs=[ANY] * (inner * PARTS + 6 + len(extra)),
            out_specs=[ANY] * 3,
            scratch_shapes=[
                pltpu.VMEM((count, width), BF),
                pltpu.VMEM((count, width), BF),
                pltpu.VMEM((count, part), BF),
                pltpu.VMEM((count, 2 * part), BF),
                *grad_scratch,
                pltpu.SemaphoreType.DMA((2 * inner * PARTS,)),
                pltpu.SemaphoreType.DMA((6,)),
                pltpu.SemaphoreType.DMA((8,)),
                *(grad_scratch if own else []),
            ],
            compiler_params=params(64),
            cost_estimate=cost(6 * count * part * width, 4 * count * (width + hidden)),
            name="weight_grads",
        )(*got, *mids, *extra)

    def spread(homes, groups, extra):
        slots = inner * sum(plan.sizes[:groups])
        return pl.pallas_call(
            functools.partial(spread_kernel, plan, homes, groups),
            out_shape=[shape((tok, b - a), BF) for _, a, b in plan.halves],
            in_specs=[SMEM, VMEM] + [ANY] * (plan.cands + groups * inner + len(extra)),
            out_specs=[VMEM] * len(plan.halves),
            scratch_shapes=[
                pltpu.VMEM((slots, width + LANES), BF),
                pltpu.VMEM((plan.cands, tok, LANES), BF),
                pltpu.VMEM((len(homes) * tok, slots), BF),
                pltpu.SemaphoreType.DMA((groups * inner,)),
                pltpu.SemaphoreType.DMA((plan.cands,)),
            ],
            compiler_params=params(),
            cost_estimate=cost(2 * len(homes) * tok * slots * width, 2 * slots * width),
            name="spread",
        )(
            info,
            jnp.asarray(plan.keys(plan.spans[:groups])),
            *blocks,
            *backs[: groups * inner],
            *extra,
        )

    mine = weight_grads(False, backs[1:inner])
    backs = backs + cross(more[3:])
    mine, backs = lax.optimization_barrier((mine, backs))
    theirs = [lax.ppermute(w, "dp", swap) for w in mine]
    cut = spread(list(range(outer)), 2, [mine[0]])
    sums = {(r, a): part for (r, a, b), part in zip(plan.halves, cut)}
    came, bit, starts = [], 1, (0, width // 2)
    while bit < outer:
        for r in range(outer - bit, 0, -2 * bit):
            if r == 1:
                came.append(lax.ppermute(sums[1, 0], "expert", plan.flip(1)))
                continue
            for a in starts:
                sent = lax.ppermute(sums[r, a], "expert", plan.flip(bit))
                if r == bit:
                    came.append(sent)
                    continue
                if bit == 1:
                    sums[1, 0], sent = lax.optimization_barrier((sums[1, 0], sent))
                total = sums[r - bit, a].astype(F32) + sent.astype(F32)
                sums[r - bit, a] = total.astype(BF)
        bit *= 2
    grads = weight_grads(True, theirs)
    home = [sums[0, 0]] + came
    grad_tokens, grad_combine = pl.pallas_call(
        functools.partial(home_kernel, plan, len(home)),
        out_shape=[shape((tok, width), BF), shape((plan.top, tok), BF)],
        in_specs=[VMEM] * (len(home) + 2) + [ANY],
        out_specs=[VMEM] * 2,
        compiler_params=params(),
        cost_estimate=cost(1e6, 2 * tok * width * (outer + 1)),
        name="home",
    )(*home, routes.T, combine.T, grads[0])
    return (grad_tokens, grad_combine.T, *grads)


def solution(mesh):
    rows = P(("parts", "dp", "expert"), None)
    in_specs = (rows,) * 4 + (P("expert", None, "dp"),) * 2 + (P("expert", "dp", None),)
    out_specs = (rows,) * 2 + (P(("parts", "expert"), None, "dp"),) * 2
    out_specs += (P(("parts", "expert"), "dp", None),)
    shape = dict(mesh.shape)

    def whole(tokens, routes, combine, upstream, w_gate, w_up, w_down):
        devices = shape["parts"] * shape["dp"] * shape["expert"]
        plan = Plan(
            shape["expert"],
            tokens.shape[0] // devices,
            routes.shape[1],
            tokens.shape[1],
            w_gate.shape[2],
        )
        body = functools.partial(on_device, plan)
        return jax.shard_map(
            body, mesh=mesh, in_specs=in_specs, out_specs=out_specs, check_vma=False
        )(tokens, routes, combine, upstream, w_gate, w_up, w_down)

    return whole
```
